32 devices in a mesh: dp: 16 (over z, y, x), outer: 2 (over core).
Axes of the slice: x: 2, y: 2, z: 4, core: 2. Of those that a mesh axis runs over, the one named last changes fastest.
Arguments:
- tokens: bfloat16 [4, 32, 512, 512], P(None, ('dp', 'outer')), may hold values from -6 to 6
- memory: float32 [4, 32, 64, 512], P(None, ('dp', 'outer')), may hold values from -6 to 6
- doc_ids: int32 [4, 32, 512], P(None, ('dp', 'outer')), may hold values from 0 to 3, never falling along the last dimension, each value on 1 to 256 neighbouring positions
- resets: int32 [4, 32], P(None, ('dp', 'outer')), may hold values 0 or 1
- out_grad: bfloat16 [4, 32, 512, 512], P(None, ('dp', 'outer')), may hold values from -6 to 6
- memory_grad: float32 [4, 32, 64, 512], P(None, ('dp', 'outer')), may hold values from -6 to 6
- attn_qkv: bfloat16 [3, 512, 512], P(None, 'dp'), may hold values from -0.25 to 0.25
- attn_out: bfloat16 [512, 512], P('dp'), may hold values from -0.75 to 0.75
- ffn_in: bfloat16 [512, 2048], P('dp'), may hold values from -0.25 to 0.25
- ffn_bias: bfloat16 [2048], P('dp'), may hold values from -3 to 3
- ffn_out: bfloat16 [2048, 512], P('dp'), may hold values from -0.125 to 0.125
- writer_qkv: bfloat16 [3, 512, 512], P(None, 'dp'), may hold values from -0.25 to 0.25
- writer_out: bfloat16 [512, 512], P('dp'), may hold values from -0.75 to 0.75
- gate_weight: bfloat16 [1024, 512], P('dp'), may hold values from -0.1875 to 0.1875
- gate_bias: bfloat16 [512], P('dp'), may hold values from -4 to 4
- gains: bfloat16 [3, 512], P(None, 'dp'), may hold values from 0.099609375 to 1.8984375
Outputs:
- out: bfloat16 [4, 32, 512, 512], P(None, ('dp', 'outer'))
- new_memory: float32 [4, 32, 64, 512], P(None, ('dp', 'outer'))
- grad_tokens: float32 [4, 32, 512, 512], P(None, ('dp', 'outer'))
- grad_memory: float32 [4, 32, 64, 512], P(None, ('dp', 'outer'))
- grad_attn_qkv: float32 [3, 512, 512], P(None, 'dp')
- grad_attn_out: float32 [512, 512], P('dp')
- grad_ffn_in: float32 [512, 2048], P('dp')
- grad_ffn_bias: float32 [2048], P('dp')
- grad_ffn_out: float32 [2048, 512], P('dp')
- grad_writer_qkv: float32 [3, 512, 512], P(None, 'dp')
- grad_writer_out: float32 [512, 512], P('dp')
- grad_gate_weight: float32 [1024, 512], P('dp')
- grad_gate_bias: float32 [512], P('dp')
- grad_gains: float32 [3, 512], P(None, 'dp')
The draws below stay inside these ranges and needn't reach their ends.
Inputs may be any that keep to these rules, and one draw needn't show every extreme that they name: `doc_ids`: within each segment the document numbers start at 0, never fall and run up to 3, every document holds 1 to 256 tokens, and some document holds exactly 256.
All inputs are finite; a program needn't handle non-finite values. No bound on the sum of `resets` on one device may be relied on, other than what follows from the above.
Results may differ from the reference program's by a relative error of at most 0.017.
Values may be sent and summed in bfloat16 or wider, within the bound.
A program may use at most 256 MiB of HBM per device.

```python
import math
import jax
import jax.numpy as jnp
import numpy as np
from jax import lax

D = 512
HEADS = 8
FF = 2048
SLOTS = 64
SEG = 512
DOCS = 4
MB = 4
SEGMENTS = 32


def with_ends(values, key, low, largest):
    longest = values.shape.index(max(values.shape))
    spots = []
    for shift in (0, 1):
        where = [jax.random.randint(jax.random.fold_in(key, axis), (), 0, length) for axis, length in enumerate(values.shape)]
        where[longest] = (where[longest] + shift) % values.shape[longest]
        spots.append(tuple(where))
    return values.at[spots[0]].set(low).at[spots[1]].set(largest)


def shard_levels(rng, dims, shards, low, top_value):
    loudness, own = 1.0, jax.random.fold_in(rng, 6)
    for dim, parts in shards:
        draws = jnp.exp(jax.random.uniform(jax.random.fold_in(own, dim), (parts,), jnp.float32, low / len(shards), top_value / len(shards)))
        loudness = loudness * jnp.repeat(draws, dims[dim] // parts).reshape([-1 if axis == dim else 1 for axis in range(len(dims))])
    return loudness


def length_profile(count, total, reach, slope):
    weights = [(1 << 20) // math.isqrt(standing ** slope) + 1 for standing in range(2, count + 1)]
    rest, counts = total - reach - (count - 1), [1] * (count - 1)
    while rest > 0:
        free = [i for i in range(count - 1) if counts[i] < reach]
        mass, budget = sum([weights[i] for i in free]), rest
        for i in free:
            addition = min(reach - counts[i], max(1, budget * weights[i] // mass), rest)
            counts[i] = counts[i] + addition
            rest = rest - addition
    return np.array([reach] + counts)


def ragged(rng, number_of, total, reach, lean):
    if number_of == 2:
        one = jax.random.randint(rng, (), max(1, total - reach), min(reach, total - 1) + 1)
        return jnp.stack([one, total - one])
    tallies = jnp.asarray(length_profile(number_of, total, reach, lean), jnp.int32)
    twos = (number_of - 1) // 2
    source_of, taker = tallies[1:1 + 2 * twos:2], tallies[2:2 + 2 * twos:2]
    slack = jnp.minimum(source_of - 1, reach - taker)
    moved = jax.random.randint(jax.random.fold_in(rng, 1), (twos,), 0, 1 << 20) % (slack + 1)
    tallies = tallies.at[1:1 + 2 * twos:2].set(source_of - moved).at[2:2 + 2 * twos:2].set(taker + moved)
    return tallies[jax.random.permutation(jax.random.fold_in(rng, 2), number_of)]


def scatter_about(own_key, shape, deviation, bound, split=(), dtype=jnp.bfloat16):
    values = deviation * jax.random.normal(own_key, shape, jnp.float32)
    if split:
        values = values * shard_levels(own_key, shape, split, -0.22, 0.18)
    return jnp.clip(values, -bound, bound).astype(dtype)


def setup_inputs(seed: int = 0) -> dict:
    arg_keys = jax.random.split(jax.random.key(seed), 17)
    return {
        "tokens": scatter_about(arg_keys[0], (MB, SEGMENTS, SEG, D), 1.0, 6.0, ((1, 32),)),
        "memory": scatter_about(arg_keys[1], (MB, SEGMENTS, SLOTS, D), 1.0, 6.0, ((1, 32),), jnp.float32),
        "doc_ids": jax.vmap(lambda own: jnp.searchsorted(jnp.cumsum(ragged(own, DOCS, SEG, SEG // 2, 1)), jnp.arange(SEG), side="right"))(jax.random.split(arg_keys[2], MB * SEGMENTS)).reshape((MB, SEGMENTS, SEG)).astype(jnp.int32),
        "resets": with_ends((jax.random.randint(arg_keys[3], (MB, SEGMENTS), 0, 4) < 1).astype(jnp.int32), jax.random.fold_in(arg_keys[3], 1), 0, 1),
        "out_grad": scatter_about(arg_keys[4], (MB, SEGMENTS, SEG, D), 1.0, 6.0, ((1, 32),)),
        "memory_grad": scatter_about(arg_keys[5], (MB, SEGMENTS, SLOTS, D), 1.0, 6.0, ((1, 32),), jnp.float32),
        "attn_qkv": scatter_about(arg_keys[6], (3, D, D), D ** -0.5, 0.25, ((1, 16),)),
        "attn_out": scatter_about(arg_keys[7], (D, D), (D // 8) ** -0.5, 0.75, ((0, 16),)),
        "ffn_in": scatter_about(arg_keys[8], (D, FF), D ** -0.5, 0.25, ((0, 16),)),
        "ffn_bias": scatter_about(arg_keys[9], (FF,), 0.5, 3.0, ((0, 16),)),
        "ffn_out": scatter_about(arg_keys[10], (FF, D), FF ** -0.5, 0.125, ((0, 16),)),
        "writer_qkv": scatter_about(arg_keys[11], (3, D, D), D ** -0.5, 0.25, ((1, 16),)),
        "writer_out": scatter_about(arg_keys[12], (D, D), (D // 8) ** -0.5, 0.75, ((0, 16),)),
        "gate_weight": scatter_about(arg_keys[13], (2 * D, D), (2 * D) ** -0.5, 0.1875, ((0, 16),)),
        "gate_bias": scatter_about(arg_keys[14], (D,), 1.0, 4.0, ((0, 16),)),
        "gains": jnp.clip(1.0 + 0.18 * jax.random.normal(arg_keys[15], (3, D), jnp.float32), 0.099609375, 1.8984375).astype(jnp.bfloat16),
    }


@jax.custom_vjp
def low(v):
    return lax.optimization_barrier(v.astype(jnp.bfloat16)).astype(jnp.float32)

@jax.custom_vjp
def low_back(v):
    return v

def low_keep(v):
    return (low(v), None)

def low_pass(kept, grad):
    return (grad,)

def back_keep(v):
    return (v, None)

def back_low(kept, grad):
    return (low(grad),)
low.defvjp(low_keep, low_pass)
low_back.defvjp(back_keep, back_low)
highest = lax.Precision.HIGHEST

def layer_norm(rows_in, gain):
    centred = rows_in - lax.optimization_barrier(jnp.mean(rows_in, axis=-1, keepdims=True))
    spread = lax.optimization_barrier(jnp.mean(centred * centred, axis=-1, keepdims=True))
    return centred * lax.rsqrt(spread + 1e-05) * gain

def project(left_side, right_side):
    return jnp.dot(left_side, right_side, precision=highest)

def attend(query_rows, key_rows, value_rows, allowed):
    row_count = query_rows.shape[0]
    head_size = query_rows.shape[1] // HEADS
    query_heads = query_rows.reshape(row_count, HEADS, head_size)
    key_heads = key_rows.reshape(key_rows.shape[0], HEADS, head_size)
    value_heads = value_rows.reshape(value_rows.shape[0], HEADS, head_size)
    scores = low_back(jnp.einsum('qhd,khd->hqk', query_heads, key_heads, precision=highest) * head_size ** (-0.5))
    scores = jnp.where(allowed[None], scores, -1000000000.0)
    attn_weights = low(jax.nn.softmax(scores, axis=-1))
    mixed_rows = jnp.einsum('hqk,khd->qhd', attn_weights, value_heads, precision=highest)
    return mixed_rows.reshape(row_count, -1)

def segment(token_rows, memory_rows, documents, reset_flag, params):
    attn_qkv, attn_out, ffn_in, ffn_bias, ffn_out, writer_qkv, writer_out, gate_weight, gate_bias, gains = params
    kept_memory = memory_rows * (1 - reset_flag).astype(jnp.float32)
    normed_one = low(layer_norm(jnp.concatenate([kept_memory, token_rows], 0), gains[0]))
    token_normed = normed_one[SLOTS:]
    query_rows = low_back(low(project(token_normed, attn_qkv[0])))
    key_rows = low_back(low(project(normed_one, attn_qkv[1])))
    value_rows = low_back(low(project(normed_one, attn_qkv[2])))
    position = jnp.arange(SEG)
    same_doc = documents[:, None] == documents[None, :]
    causal = same_doc & (position[None, :] <= position[:, None])
    sees_memory = (documents == documents[0]) & (reset_flag == 0)
    allowed = jnp.concatenate([jnp.broadcast_to(sees_memory[:, None], (SEG, SLOTS)), causal], 1)
    mixed_rows = low_back(low(attend(query_rows, key_rows, value_rows, allowed)))
    hidden_one = token_rows + low_back(project(mixed_rows, attn_out))
    normed_two = low(layer_norm(hidden_one, gains[1]))
    ffn_before = low_back(project(normed_two, ffn_in) + ffn_bias)
    active = low(jax.nn.gelu(ffn_before, approximate=False))
    result = hidden_one + low_back(project(active, ffn_out))
    normed_three = low(layer_norm(jnp.concatenate([kept_memory, result], 0), gains[2]))
    slot_query = low_back(low(project(normed_three[:SLOTS], writer_qkv[0])))
    token_keys = low_back(low(project(normed_three[SLOTS:], writer_qkv[1])))
    token_values = low_back(low(project(normed_three[SLOTS:], writer_qkv[2])))
    reading = jnp.broadcast_to((documents == documents[SEG - 1])[None, :], (SLOTS, SEG))
    written = low_back(low(attend(slot_query, token_keys, token_values, reading)))
    write_value = low_back(project(written, writer_out))
    joined = low(jnp.concatenate([kept_memory, write_value], 1))
    gate_logit = low_back(project(joined, gate_weight) + gate_bias)
    gate_value = jax.nn.sigmoid(gate_logit)
    new_memory = gate_value * kept_memory + (1.0 - gate_value) * write_value
    return (result, new_memory)

def reference(tokens, memory, doc_ids, resets, out_grad, memory_grad, attn_qkv, attn_out, ffn_in, ffn_bias, ffn_out, writer_qkv, writer_out, gate_weight, gate_bias, gains):
    params = tuple((weight.astype(jnp.float32) for weight in (attn_qkv, attn_out, ffn_in, ffn_bias, ffn_out, writer_qkv, writer_out, gate_weight, gate_bias, gains)))
    total = MB * SEGMENTS
    groups = total // 8
    pieces = (tokens.reshape(groups, 8, SEG, D), memory.reshape(groups, 8, SLOTS, D), doc_ids.reshape(groups, 8, SEG), resets.reshape(groups, 8), out_grad.reshape(groups, 8, SEG, D), memory_grad.reshape(groups, 8, SLOTS, D))

    def group_step(totals, group):
        token_group, memory_group, doc_group, reset_group, cot_group, memcot_group = group

        def forward(token_float, memory_float, weights):
            return jax.vmap(segment, in_axes=(0, 0, 0, 0, None))(token_float, memory_float, doc_group, reset_group, weights)
        outputs, pullback = jax.vjp(forward, token_group.astype(jnp.float32), memory_group, params)
        grad_token, grad_mem, grad_weights = pullback((cot_group.astype(jnp.float32), memcot_group))
        totals = jax.tree.map(jnp.add, totals, grad_weights)
        return (totals, (outputs[0].astype(jnp.bfloat16), outputs[1], grad_token, grad_mem))
    zeros = jax.tree.map(jnp.zeros_like, params)
    totals, stacked = lax.scan(group_step, zeros, pieces)
    out = stacked[0].reshape(MB, SEGMENTS, SEG, D)
    new_memory = stacked[1].reshape(MB, SEGMENTS, SLOTS, D)
    grad_tokens = stacked[2].reshape(MB, SEGMENTS, SEG, D)
    grad_memory = stacked[3].reshape(MB, SEGMENTS, SLOTS, D)
    return (out, new_memory, grad_tokens, grad_memory, totals[0], totals[1], totals[2], totals[3], totals[4], totals[5], totals[6], totals[7], totals[8], totals[9])
```

```python
import functools

import jax
import jax.numpy as jnp
from jax import lax
from jax.experimental import pallas as pl
from jax.experimental.pallas import tpu as pltpu
from jax.sharding import PartitionSpec as P

HEADS = 8
BLOCK = 128
SPANS = ((0, 256), (0, 384), (128, 512), (256, 640))
STARTS = (0, 256, 640, 1024)
LIVE = 1408
F32 = jnp.float32
BF16 = jnp.bfloat16
VMEM_LIMIT = 60 * 1024 * 1024


def dot(a, b):
    return jnp.dot(a, b, preferred_element_type=F32)


def dot_nt(a, b):
    return lax.dot_general(a, b, (((1,), (1,)), ((), ())), preferred_element_type=F32)


def dot_tn(a, b):
    return lax.dot_general(a, b, (((0,), (0,)), ((), ())), preferred_element_type=F32)


def norm_parts(rows):
    centred = rows - jnp.mean(rows, axis=-1, keepdims=True)
    rstd = lax.rsqrt(jnp.mean(centred * centred, axis=-1, keepdims=True) + 1e-05)
    return centred * rstd, rstd


def norm_back(grad, hat, rstd, gain):
    scaled = grad * gain
    return rstd * (
        scaled
        - jnp.mean(scaled, axis=-1, keepdims=True)
        - hat * jnp.mean(scaled * hat, axis=-1, keepdims=True)
    )


def diagonal_pair(ref, top):
    ref[0:64, 0:128] = top[0:64]
    ref[64:128, 128:256] = top[64:128]


def forward_kernel(
    tok_ref, mem_ref, doc_ref, keep_ref, attn_ref, w1_ref, w2_ref, b1_ref, gain_ref,
    out_ref, res_ref, h1_ref, n1_ref, qt_ref, k_ref, v_ref, e_ref, linv_ref, ot_ref, act_ref, slope_ref,
    bias_ref, pair_ref, vt_ref,
):
    seg = tok_ref.shape[1]
    slots = mem_ref.shape[1]
    x = tok_ref[0].astype(F32)
    keep = keep_ref[0][:, 0:1]
    gain_one = gain_ref[0:1, :]
    hat, _ = norm_parts(x)
    n1t = (hat * gain_one).astype(BF16)
    hat, _ = norm_parts(mem_ref[0] * keep)
    n1_ref[0, 0:slots, :] = (hat * gain_one).astype(BF16)
    n1_ref[0, slots:128, :] = jnp.zeros((128 - slots, x.shape[1]), BF16)
    n1_ref[0, 128:, :] = n1t
    docs = doc_ref[0].astype(F32)
    key_docs = jnp.broadcast_to(docs, (128, seg)).T
    slot_docs = jnp.broadcast_to(keep - 1.0, (slots, 128))
    key_docs = jnp.concatenate([slot_docs, jnp.full((128 - slots, 128), -1.0, F32), key_docs], 0)
    for block, (first, last) in enumerate(SPANS):
        place = lax.broadcasted_iota(jnp.int32, (last - first, BLOCK), 0) + (first - 128 - block * BLOCK)
        place = place <= lax.broadcasted_iota(jnp.int32, (last - first, BLOCK), 1)
        same = key_docs[first:last] == docs[:, block * BLOCK:(block + 1) * BLOCK]
        bias_ref[STARTS[block]:STARTS[block] + last - first, :] = jnp.where(same & place, 0.0, -1e30)
    qt_ref[0] = (dot_nt(attn_ref[0].T, n1t) * 0.125).astype(BF16)
    n1 = n1_ref[0]
    k_ref[0] = dot(n1, attn_ref[1]).astype(BF16)
    v = dot(n1, attn_ref[2])
    v_ref[0] = v.astype(BF16)
    vt_ref[...] = v.astype(BF16).T
    pair_ref[...] = jnp.zeros_like(pair_ref)

    def one_pair(pair, carry):
        lanes = pl.ds(pl.multiple_of(pair * 128, 128), 128)
        for block, (first, last) in enumerate(SPANS):
            start = STARTS[block]
            held = pair_ref.at[block]
            columns = pl.ds(block * BLOCK, BLOCK)
            diagonal_pair(held, qt_ref[0, lanes, columns])
            scores = dot(k_ref[0, first:last, lanes], held[...])
            bias = bias_ref[start:start + last - first, :]
            scores = scores + jnp.concatenate([bias, bias], 1)
            largest = jnp.max(scores, axis=0, keepdims=True)
            e = jnp.exp(scores - largest)
            linv = 1.0 / jnp.sum(e, axis=0, keepdims=True)
            e = e.astype(BF16)
            e_ref[0, pair, start:start + last - first, :] = e
            linv_ref[0, pair, block, :, :] = linv
            mixed = dot(vt_ref[lanes, first:last], e) * linv
            ot_ref[0, lanes, columns] = jnp.concatenate(
                [mixed[0:64, 0:128], mixed[64:128, 128:256]], 0
            ).astype(BF16)
        return carry

    lax.fori_loop(0, 4, one_pair, 0)
    h1 = x + dot(ot_ref[0].T, attn_ref[3])
    h1_ref[0] = h1
    hat, _ = norm_parts(h1)
    n2 = (hat * gain_ref[1:2, :]).astype(BF16)
    result = h1
    for part in range(4):
        before = dot(n2, w1_ref[part]) + b1_ref[part]
        cdf = 0.5 + 0.5 * lax.erf(before * 0.7071067811865476)
        active = (before * cdf).astype(BF16)
        act_ref[0, part] = active
        slope = cdf + before * jnp.exp(before * before * -0.5) * 0.3989422804014327
        slope_ref[0, part] = slope.astype(BF16)
        result = result + dot(active, w2_ref[part])
    out_ref[0] = result.astype(BF16)
    res_ref[0] = result[seg // 2:]


def full_spec(shape):
    return pl.BlockSpec(shape, lambda i: (0,) * len(shape), pipeline_mode=pl.Buffered(1))


def step_spec(shape):
    return pl.BlockSpec((1,) + shape, lambda i: (i,) + (0,) * len(shape))


def call_forward(tokens, memory, docs, keep, attn, w1, w2, b1, gains):
    n, seg, d = tokens.shape
    slots = memory.shape[1]
    outs = [
        ((seg, d), BF16), ((seg // 2, d), F32), ((seg, d), F32), ((seg + 128, d), BF16), ((d, seg), BF16),
        ((seg + 128, d), BF16), ((seg + 128, d), BF16), ((4, LIVE, 256), BF16), ((4, 4, 1, 256), F32),
        ((d, seg), BF16), ((4, seg, 512), BF16), ((4, seg, 512), BF16),
    ]
    return pl.pallas_call(
        forward_kernel,
        grid=(n,),
        out_shape=[jax.ShapeDtypeStruct((n,) + shape, kind) for shape, kind in outs],
        in_specs=[
            step_spec((seg, d)), step_spec((slots, d)), step_spec((1, seg)), step_spec((1, 128)),
            full_spec(attn.shape), full_spec(w1.shape), full_spec(w2.shape), full_spec(b1.shape), full_spec(gains.shape),
        ],
        out_specs=[step_spec(shape) for shape, _ in outs],
        scratch_shapes=[
            pltpu.VMEM((LIVE, 128), F32), pltpu.VMEM((4, 128, 256), BF16), pltpu.VMEM((d, seg + 128), BF16),
        ],
        compiler_params=pltpu.CompilerParams(vmem_limit_bytes=VMEM_LIMIT),
        name="forward_rows",
    )(tokens, memory, docs, keep, attn, w1, w2, b1, gains)


def writer_kernel(
    res_ref, mem_ref, memgrad_ref, doc_ref, keep_ref, wr_ref, gate_ref, gbias_ref, gain_ref,
    newmem_ref, dres_ref, dkept_ref, gwr_ref, ggate_ref, gsmall_ref,
    n3_ref, ns_ref, kept_ref, sq_ref, tk_ref, tv_ref, p_ref, wt_ref, dsq_ref, dtk_ref, dtv_ref, dlog_ref, dw_ref,
):
    n, half, d = res_ref.shape
    slots = mem_ref.shape[1]
    gain = gain_ref[2:3, :]

    def norm(i, carry):
        rows = pl.ds(pl.multiple_of(i * half, half), half)
        small = pl.ds(pl.multiple_of(i * slots, slots), slots)
        hat, _ = norm_parts(res_ref[i])
        n3_ref[rows, :] = (hat * gain).astype(BF16)
        kept = mem_ref[i] * keep_ref[i][:, 0:1]
        kept_ref[small, :] = kept
        hat, _ = norm_parts(kept)
        ns_ref[small, :] = (hat * gain).astype(BF16)
        tk_ref[rows, :] = dot(n3_ref[rows, :], wr_ref[1]).astype(BF16)
        tv_ref[rows, :] = dot(n3_ref[rows, :], wr_ref[2]).astype(BF16)
        return carry

    lax.fori_loop(0, n, norm, 0)
    sq_ref[...] = (dot(ns_ref[...], wr_ref[0]) * 0.125).astype(BF16)
    low_half = lax.broadcasted_iota(jnp.int32, (1, 128), 1) < 64

    def halves(rows):
        zero = jnp.zeros_like(rows)
        return jnp.concatenate([jnp.where(low_half, rows, zero), jnp.where(low_half, zero, rows)], 0)

    def read(i, carry):
        rows = pl.ds(pl.multiple_of(i * half, half), half)
        small = pl.ds(pl.multiple_of(i * slots, slots), slots)
        docs = doc_ref[i].astype(F32)
        bias = jnp.where(docs == jnp.max(docs), 0.0, -1e30)[:, docs.shape[1] - half:]
        for pair in range(4):
            lanes = slice(pair * 128, pair * 128 + 128)
            scores = dot_nt(halves(sq_ref[small, lanes]), tk_ref[rows, lanes]) + bias
            e = jnp.exp(scores - jnp.max(scores, axis=1, keepdims=True))
            p = e * (1.0 / jnp.sum(e, axis=1, keepdims=True))
            p_ref[i, pair] = p
            mixed = dot(p.astype(BF16), tv_ref[rows, lanes])
            wt_ref[small, lanes] = jnp.where(low_half, mixed[:slots], mixed[slots:]).astype(BF16)
        return carry

    lax.fori_loop(0, n, read, 0)
    write = dot(wt_ref[...], wr_ref[3])
    kept = kept_ref[...]
    write_low = write.astype(BF16)
    kept_low = kept.astype(BF16)
    logit = dot(kept_low, gate_ref[0]) + dot(write_low, gate_ref[1]) + gbias_ref[...]
    gate = jax.nn.sigmoid(logit)
    new = gate * kept + (1.0 - gate) * write
    memgrad = memgrad_ref[...].reshape(n * slots, d)
    newmem_ref[...] = new.reshape(n, slots, d)
    dlogit = memgrad * (kept - write) * gate * (1.0 - gate)
    dlog_ref[...] = dlogit.astype(BF16)
    dlow = dlog_ref[...]
    gsmall_ref[0:1, :] = jnp.sum(dlow.astype(F32), axis=0, keepdims=True)
    ggate_ref[0] = dot_tn(kept_low, dlow).astype(ggate_ref.dtype)
    ggate_ref[1] = dot_tn(write_low, dlow).astype(ggate_ref.dtype)
    dkept = memgrad * gate + dot_nt(dlow, gate_ref[0])
    dwrite = memgrad * (1.0 - gate) + dot_nt(dlow, gate_ref[1])
    dkept_ref[...] = dkept.reshape(n, slots, d)
    dw_low = dwrite.astype(BF16)
    gwr_ref[3] = dot_tn(wt_ref[...], dw_low).astype(gwr_ref.dtype)
    dw_ref[...] = dot_nt(dw_low, wr_ref[3]).astype(BF16)

    def read_back(i, carry):
        rows = pl.ds(pl.multiple_of(i * half, half), half)
        small = pl.ds(pl.multiple_of(i * slots, slots), slots)
        for pair in range(4):
            lanes = slice(pair * 128, pair * 128 + 128)
            p = p_ref[i, pair]
            grads = halves(dw_ref[small, lanes])
            dp = dot_nt(grads, tv_ref[rows, lanes])
            ds = (p * (dp - jnp.sum(dp * p, axis=1, keepdims=True))).astype(BF16)
            dq = dot(ds, tk_ref[rows, lanes]) * 0.125
            dsq_ref[small, lanes] = jnp.where(low_half, dq[:slots], dq[slots:]).astype(BF16)
            dtk_ref[rows, lanes] = dot_tn(ds, halves(sq_ref[small, lanes])).astype(BF16)
            dtv_ref[rows, lanes] = dot_tn(p.astype(BF16), grads).astype(BF16)
        return carry

    lax.fori_loop(0, n, read_back, 0)
    gwr_ref[0] = dot_tn(ns_ref[...], dsq_ref[...]).astype(gwr_ref.dtype)
    gwr_ref[1] = dot_tn(n3_ref[...], dtk_ref[...]).astype(gwr_ref.dtype)
    gwr_ref[2] = dot_tn(n3_ref[...], dtv_ref[...]).astype(gwr_ref.dtype)
    grad = dot_nt(dsq_ref[...], wr_ref[0])
    hat, rstd = norm_parts(kept_ref[...])
    dkept_ref[...] += norm_back(grad, hat, rstd, gain).reshape(n, slots, d)
    ggain = jnp.sum(grad * hat, axis=0, keepdims=True)

    def back(i, ggain):
        rows = pl.ds(pl.multiple_of(i * half, half), half)
        grad = dot_nt(dtk_ref[rows, :], wr_ref[1]) + dot_nt(dtv_ref[rows, :], wr_ref[2])
        hat, rstd = norm_parts(res_ref[i])
        dres_ref[i] = norm_back(grad, hat, rstd, gain)
        return ggain + jnp.sum(grad * hat, axis=0, keepdims=True)

    gsmall_ref[1:2, :] = lax.fori_loop(0, n, back, ggain)


def call_writer(res, memory, memory_grad, docs, keep, wr, gate, gbias, gains):
    n, half, d = res.shape
    slots = memory.shape[1]
    rows, small = n * half, n * slots
    vmem = pl.BlockSpec(memory_space=pltpu.VMEM)
    return pl.pallas_call(
        writer_kernel,
        out_shape=[
            jax.ShapeDtypeStruct((n, slots, d), F32), jax.ShapeDtypeStruct((n, half, d), F32),
            jax.ShapeDtypeStruct((n, slots, d), F32), jax.ShapeDtypeStruct((4, d, d), BF16),
            jax.ShapeDtypeStruct((2, d, d), BF16), jax.ShapeDtypeStruct((2, d), F32),
        ],
        in_specs=[vmem] * 9,
        out_specs=[vmem] * 6,
        scratch_shapes=[
            pltpu.VMEM((rows, d), BF16), pltpu.VMEM((small, d), BF16), pltpu.VMEM((small, d), F32),
            pltpu.VMEM((small, d), BF16), pltpu.VMEM((rows, d), BF16), pltpu.VMEM((rows, d), BF16),
            pltpu.VMEM((n, 4, 2 * slots, half), F32), pltpu.VMEM((small, d), BF16), pltpu.VMEM((small, d), BF16),
            pltpu.VMEM((rows, d), BF16), pltpu.VMEM((rows, d), BF16), pltpu.VMEM((small, d), BF16),
            pltpu.VMEM((small, d), BF16),
        ],
        compiler_params=pltpu.CompilerParams(vmem_limit_bytes=VMEM_LIMIT),
        name="writer",
    )(res, memory, memory_grad, docs, keep, wr, gate, gbias, gains)


def ffn_back_kernel(
    og_ref, dres_ref, h1_ref, act_ref, slope_ref, w1_ref, w2_ref, gain_ref,
    dh_ref, gw1_ref, gw2_ref, gb_ref, ggain_ref,
    acc1_ref, acc2_ref, accb_ref, accg_ref,
):
    step = pl.program_id(0)
    seg = og_ref.shape[1]

    @pl.when(step == 0)
    def _():
        acc1_ref[...] = jnp.zeros_like(acc1_ref)
        acc2_ref[...] = jnp.zeros_like(acc2_ref)
        accb_ref[...] = jnp.zeros_like(accb_ref)
        accg_ref[...] = jnp.zeros_like(accg_ref)

    top = og_ref[0, 0:seg // 2, :].astype(F32)
    bottom = og_ref[0, seg // 2:, :].astype(F32) + dres_ref[0]
    dresult = jnp.concatenate([top, bottom], 0)
    low = dresult.astype(BF16)
    h1 = h1_ref[0]
    hat, rstd = norm_parts(h1)
    gain = gain_ref[1:2, :]
    n2t = (hat * gain).astype(BF16).T
    lowt = low.T
    grad = jnp.zeros_like(dresult)
    for part in range(4):
        acc2_ref[part] += dot(lowt, act_ref[0, part])
        dbefore = (dot_nt(low, w2_ref[part]) * slope_ref[0, part].astype(F32)).astype(BF16)
        accb_ref[part] += jnp.sum(dbefore.astype(F32), axis=0, keepdims=True)
        acc1_ref[part] += dot(n2t, dbefore)
        grad = grad + dot_nt(dbefore, w1_ref[part])
    accg_ref[...] += jnp.sum(grad * hat, axis=0, keepdims=True)
    dh_ref[0] = dresult + norm_back(grad, hat, rstd, gain)

    @pl.when(step == pl.num_programs(0) - 1)
    def _():
        gw1_ref[...] = acc1_ref[...].astype(gw1_ref.dtype)
        for part in range(4):
            gw2_ref[part] = acc2_ref[part].T.astype(gw2_ref.dtype)
        gb_ref[...] = accb_ref[...]
        ggain_ref[...] = accg_ref[...]


def call_ffn_back(out_grad, dres, h1, act, slope, w1, w2, gains):
    n, seg, d = out_grad.shape
    return pl.pallas_call(
        ffn_back_kernel,
        grid=(n,),
        out_shape=[
            jax.ShapeDtypeStruct((n, seg, d), F32), jax.ShapeDtypeStruct(w1.shape, BF16),
            jax.ShapeDtypeStruct(w2.shape, BF16), jax.ShapeDtypeStruct((4, 1, 512), F32),
            jax.ShapeDtypeStruct((1, d), F32),
        ],
        in_specs=[
            step_spec((seg, d)), step_spec((seg // 2, d)), step_spec((seg, d)), step_spec((4, seg, 512)),
            step_spec((4, seg, 512)), full_spec(w1.shape), full_spec(w2.shape), full_spec(gains.shape),
        ],
        out_specs=[
            step_spec((seg, d)), full_spec(w1.shape), full_spec(w2.shape), full_spec((4, 1, 512)), full_spec((1, d)),
        ],
        scratch_shapes=[
            pltpu.VMEM(w1.shape, F32), pltpu.VMEM((4, d, 512), F32), pltpu.VMEM((4, 1, 512), F32), pltpu.VMEM((1, d), F32),
        ],
        compiler_params=pltpu.CompilerParams(vmem_limit_bytes=VMEM_LIMIT),
        name="ffn_back",
    )(out_grad, dres, h1, act, slope, w1, w2, gains)


def attn_back_kernel(
    dh_ref, tok_ref, mem_ref, keep_ref, n1_ref, qt_ref, k_ref, v_ref, e_ref, linv_ref, ot_ref, dkept_ref,
    attn_ref, gain_ref,
    gtok_ref, gmem_ref, gattn_ref, ggain_ref,
    dot_ref, kt_ref, dqt_ref, dk_ref, dv_ref, qp_ref, dp_ref, acc_ref, accg_ref,
):
    step = pl.program_id(0)
    seg = tok_ref.shape[1]
    slots = mem_ref.shape[1]

    @pl.when(step == 0)
    def _():
        acc_ref[...] = jnp.zeros_like(acc_ref)
        accg_ref[...] = jnp.zeros_like(accg_ref)

    dh = dh_ref[0]
    low = dh.astype(BF16)
    acc_ref[3] += dot(ot_ref[0], low)
    dot_ref[...] = dot_nt(attn_ref[3], low)
    kt_ref[...] = k_ref[0].T
    qp_ref[...] = jnp.zeros_like(qp_ref)
    dp_ref[...] = jnp.zeros_like(dp_ref)

    def one_pair(pair, carry):
        lanes = pl.ds(pl.multiple_of(pair * 128, 128), 128)
        dk_ref[:, lanes] = jnp.zeros((seg + 128, 128), F32)
        dv_ref[:, lanes] = jnp.zeros((seg + 128, 128), F32)
        for block, (first, last) in enumerate(SPANS):
            start = STARTS[block]
            columns = pl.ds(block * BLOCK, BLOCK)
            linv = linv_ref[0, pair, block, :, :]
            mixed_grad = dot_ref[lanes, columns]
            top = (mixed_grad[0:64] * linv[:, 0:128]).astype(BF16)
            bottom = (mixed_grad[64:128] * linv[:, 128:256]).astype(BF16)
            mixed = ot_ref[0, lanes, columns].astype(F32)
            delta = jnp.concatenate(
                [
                    jnp.sum(top.astype(F32) * mixed[0:64], axis=0, keepdims=True),
                    jnp.sum(bottom.astype(F32) * mixed[64:128], axis=0, keepdims=True),
                ],
                1,
            )
            held = dp_ref.at[block]
            held[0:64, 0:128] = top
            held[64:128, 128:256] = bottom
            query = qp_ref.at[block]
            diagonal_pair(query, qt_ref[0, lanes, columns])
            e = e_ref[0, pair, start:start + last - first, :]
            dp = dot(v_ref[0, first:last, lanes], held[...])
            ds = (e.astype(F32) * (dp - delta)).astype(BF16)
            dv_ref[first:last, lanes] += dot_nt(e, held[...])
            dk_ref[first:last, lanes] += dot_nt(ds, query[...])
            dq = dot(kt_ref[lanes, first:last], ds) * 0.125
            dqt_ref[lanes, columns] = jnp.concatenate([dq[0:64, 0:128], dq[64:128, 128:256]], 0).astype(BF16)
        return carry

    lax.fori_loop(0, 4, one_pair, 0)
    n1t = n1_ref[0].T
    dk = dk_ref[...].astype(BF16)
    dv = dv_ref[...].astype(BF16)
    acc_ref[0] += dot_nt(n1t[:, 128:], dqt_ref[...])
    acc_ref[1] += dot(n1t, dk)
    acc_ref[2] += dot(n1t, dv)
    gain = gain_ref[0:1, :]
    grad = dot_nt(dk, attn_ref[1]) + dot_nt(dv, attn_ref[2])
    slot_grad = grad[0:slots]
    kept = mem_ref[0] * keep_ref[0][:, 0:1]
    hat, rstd = norm_parts(kept)
    ggain = jnp.sum(slot_grad * hat, axis=0, keepdims=True)
    gmem_ref[0] = (dkept_ref[0] + norm_back(slot_grad, hat, rstd, gain)) * keep_ref[0][:, 0:1]
    grad = grad[128:] + dot_nt(dqt_ref[...].T, attn_ref[0])
    hat, rstd = norm_parts(tok_ref[0].astype(F32))
    accg_ref[...] += ggain + jnp.sum(grad * hat, axis=0, keepdims=True)
    gtok_ref[0] = dh + norm_back(grad, hat, rstd, gain)

    @pl.when(step == pl.num_programs(0) - 1)
    def _():
        gattn_ref[...] = acc_ref[...].astype(gattn_ref.dtype)
        ggain_ref[...] = accg_ref[...]


def call_attn_back(dh, tokens, memory, keep, n1, qt, k, v, e, linv, ot, dkept, attn, gains):
    n, seg, d = tokens.shape
    slots = memory.shape[1]
    return pl.pallas_call(
        attn_back_kernel,
        grid=(n,),
        out_shape=[
            jax.ShapeDtypeStruct((n, seg, d), F32), jax.ShapeDtypeStruct((n, slots, d), F32),
            jax.ShapeDtypeStruct((4, d, d), BF16), jax.ShapeDtypeStruct((1, d), F32),
        ],
        in_specs=[
            step_spec((seg, d)), step_spec((seg, d)), step_spec((slots, d)), step_spec((1, 128)),
            step_spec((seg + 128, d)), step_spec((d, seg)), step_spec((seg + 128, d)), step_spec((seg + 128, d)),
            step_spec((4, LIVE, 256)), step_spec((4, 4, 1, 256)), step_spec((d, seg)), step_spec((slots, d)),
            full_spec(attn.shape), full_spec(gains.shape),
        ],
        out_specs=[step_spec((seg, d)), step_spec((slots, d)), full_spec((4, d, d)), full_spec((1, d))],
        scratch_shapes=[
            pltpu.VMEM((d, seg), F32), pltpu.VMEM((d, seg + 128), BF16), pltpu.VMEM((d, seg), BF16),
            pltpu.VMEM((seg + 128, d), F32), pltpu.VMEM((seg + 128, d), F32), pltpu.VMEM((4, 128, 256), BF16),
            pltpu.VMEM((4, 128, 256), BF16), pltpu.VMEM((4, d, d), F32), pltpu.VMEM((1, d), F32),
        ],
        compiler_params=pltpu.CompilerParams(vmem_limit_bytes=VMEM_LIMIT),
        name="attn_back",
    )(dh, tokens, memory, keep, n1, qt, k, v, e, linv, ot, dkept, attn, gains)


def local_layer(tokens, memory, docs, resets, out_grad, memory_grad, attn, w1, w2, wr, gate, b1, gbias, gains):
    n = tokens.shape[0]
    keep = jnp.broadcast_to((1 - resets).astype(F32)[:, None, None], (n, 1, 128))
    docs = docs[:, None, :]
    out, res, h1, n1, qt, k, v, e, linv, ot, act, slope = call_forward(
        tokens, memory, docs, keep, attn, w1, w2, b1, gains
    )
    new_memory, dres, dkept, gwr, ggate, gsmall = call_writer(
        res, memory, memory_grad, docs, keep, wr, gate, gbias, gains
    )
    dh, gw1, gw2, gb, ggain_two = call_ffn_back(out_grad, dres, h1, act, slope, w1, w2, gains)
    grad_tokens, grad_memory, gattn, ggain_one = call_attn_back(
        dh, tokens, memory, keep, n1, qt, k, v, e, linv, ot, dkept, attn, gains
    )
    ggains = jnp.concatenate([ggain_one, ggain_two, gsmall[1:2]], 0)
    return out, new_memory, grad_tokens, grad_memory, gattn, gw1, gw2, gwr, ggate, gb.reshape(-1), gsmall[0], ggains


def pack_weights(attn_qkv, attn_out, ffn_in, ffn_out, writer_qkv, writer_out, gate_weight):
    rows, d = attn_out.shape
    blocks = ffn_in.shape[1] // d
    return jnp.concatenate(
        [
            attn_qkv, attn_out[None], ffn_in.reshape(rows, blocks, d).transpose(1, 0, 2), ffn_out.reshape(blocks, rows, d),
            writer_qkv, writer_out[None], gate_weight.reshape(2, rows, d),
        ],
        0,
    )


def unpack_weights(gathered):
    n, _, rows, d = gathered.shape

    def by_rows(first, last):
        return gathered[:, first:last].transpose(1, 0, 2, 3).reshape(last - first, n * rows, d)

    return (
        by_rows(0, 4), by_rows(4, 8), gathered[:, 8:12].reshape(4, d, d), by_rows(12, 16), gathered[:, 16:18].reshape(2, d, d),
    )


def pack_grads(n, gattn, gw1, gw2, gwr, ggate):
    d = gattn.shape[1]
    rows = d // n

    def by_rows(grad):
        return grad.reshape(-1, n, rows, d).transpose(1, 0, 2, 3)

    return jnp.concatenate(
        [by_rows(gattn), by_rows(gw1), gw2.reshape(n, 4, rows, d), by_rows(gwr), ggate.reshape(n, 2, rows, d)], 1
    )


def unpack_owned(owned):
    _, rows, d = owned.shape
    return (
        owned[0:3], owned[3], owned[4:8].transpose(1, 0, 2).reshape(rows, 4 * d), owned[8:12].reshape(4 * rows, d),
        owned[12:15], owned[15], owned[16:18].reshape(2 * rows, d),
    )


def body(
    tokens, memory, doc_ids, resets, out_grad, memory_grad,
    attn_qkv, attn_out, ffn_in, ffn_bias, ffn_out, writer_qkv, writer_out, gate_weight, gate_bias, gains,
):
    n = lax.axis_size("dp")
    micro, segs, seg, d = tokens.shape
    slots = memory.shape[2]
    rows = attn_out.shape[0]
    packed = pack_weights(attn_qkv, attn_out, ffn_in, ffn_out, writer_qkv, writer_out, gate_weight)
    small = jnp.concatenate([ffn_bias.reshape(4, rows), gate_bias[None], gains], 0).astype(F32)
    small = lax.all_gather(small, "dp", axis=0)
    bias_one = small[:, 0:4].reshape(4, 1, d)
    small = small.transpose(1, 0, 2).reshape(8, d)
    attn, w1, w2, wr, gate = unpack_weights(lax.all_gather(packed, "dp", axis=0))
    out, new_memory, grad_tokens, grad_memory, gattn, gw1, gw2, gwr, ggate, gb, ggb, ggains = local_layer(
        tokens.reshape(micro * segs, seg, d), memory.reshape(micro * segs, slots, d), doc_ids.reshape(micro * segs, seg),
        resets.reshape(micro * segs), out_grad.reshape(micro * segs, seg, d), memory_grad.reshape(micro * segs, slots, d),
        attn, w1, w2, wr, gate, bias_one, small[4:5], small[5:8],
    )
    owned = lax.psum_scatter(pack_grads(n, gattn, gw1, gw2, gwr, ggate).astype(F32), "dp", scatter_dimension=0, tiled=False)
    owned = lax.psum(owned.astype(BF16), "outer").astype(F32)
    small_grads = jnp.concatenate(
        [gb.reshape(n, 4 * rows), ggb.reshape(n, rows), ggains.reshape(3, n, rows).transpose(1, 0, 2).reshape(n, 3 * rows)], 1
    )
    small_owned = lax.psum(lax.psum_scatter(small_grads, "dp", scatter_dimension=0, tiled=False), "outer")
    gqkv, gout, gin, gffn, gwqkv, gwout, ggw = unpack_owned(owned)
    return (
        out.reshape(micro, segs, seg, d), new_memory.reshape(micro, segs, slots, d),
        grad_tokens.reshape(micro, segs, seg, d), grad_memory.reshape(micro, segs, slots, d),
        gqkv, gout, gin, small_owned[0:4 * rows], gffn, gwqkv, gwout, ggw, small_owned[4 * rows:5 * rows],
        small_owned[5 * rows:].reshape(3, rows),
    )


def solution(mesh):
    split = ("dp", "outer")
    whole = P(None, split, None, None)
    weights = (
        P(None, "dp", None), P("dp", None), P("dp", None), P("dp"), P("dp", None), P(None, "dp", None),
        P("dp", None), P("dp", None), P("dp"), P(None, "dp"),
    )
    return jax.shard_map(
        body,
        mesh=mesh,
        in_specs=(whole, whole, P(None, split, None), P(None, split), whole, whole) + weights,
        out_specs=(whole, whole, whole, whole) + weights,
        check_vma=False,
    )
```

```python
import functools

import jax
import jax.numpy as jnp
from jax import lax
from jax.experimental import pallas as pl
from jax.experimental.pallas import tpu as pltpu
from jax.sharding import PartitionSpec as P

HEADS = 8
BLOCK = 128
SPANS = ((0, 256), (0, 384), (128, 512), (256, 640))
STARTS = (0, 256, 640, 1024)
LIVE = 1408
F32 = jnp.float32
BF16 = jnp.bfloat16
VMEM_LIMIT = 60 * 1024 * 1024


def dot(a, b):
    return jnp.dot(a, b, preferred_element_type=F32)


def dot_nt(a, b):
    return lax.dot_general(a, b, (((1,), (1,)), ((), ())), preferred_element_type=F32)


def dot_tn(a, b):
    return lax.dot_general(a, b, (((0,), (0,)), ((), ())), preferred_element_type=F32)


def norm_parts(rows):
    centred = rows - jnp.mean(rows, axis=-1, keepdims=True)
    rstd = lax.rsqrt(jnp.mean(centred * centred, axis=-1, keepdims=True) + 1e-05)
    return centred * rstd, rstd


def norm_back(grad, hat, rstd, gain):
    scaled = grad * gain
    return rstd * (
        scaled
        - jnp.mean(scaled, axis=-1, keepdims=True)
        - hat * jnp.mean(scaled * hat, axis=-1, keepdims=True)
    )


def diagonal_pair(ref, top):
    ref[0:64, 0:128] = top[0:64]
    ref[64:128, 128:256] = top[64:128]


def forward_kernel(
    tok_ref, mem_ref, doc_ref, keep_ref, attn_ref, w1_ref, w2_ref, b1_ref, gain_ref,
    out_ref, res_ref, h1_ref, n1_ref, qt_ref, k_ref, v_ref, e_ref, linv_ref, ot_ref, act_ref, slope_ref,
    bias_ref, pair_ref, vt_ref,
):
    seg = tok_ref.shape[1]
    slots = mem_ref.shape[1]
    x = tok_ref[0].astype(F32)
    keep = keep_ref[0][:, 0:1]
    gain_one = gain_ref[0:1, :]
    hat, _ = norm_parts(x)
    n1t = (hat * gain_one).astype(BF16)
    hat, _ = norm_parts(mem_ref[0] * keep)
    n1_ref[0, 0:slots, :] = (hat * gain_one).astype(BF16)
    n1_ref[0, slots:128, :] = jnp.zeros((128 - slots, x.shape[1]), BF16)
    n1_ref[0, 128:, :] = n1t
    docs = doc_ref[0].astype(F32)
    key_docs = jnp.broadcast_to(docs, (128, seg)).T
    slot_docs = jnp.broadcast_to(keep - 1.0, (slots, 128))
    key_docs = jnp.concatenate([slot_docs, jnp.full((128 - slots, 128), -1.0, F32), key_docs], 0)
    for block, (first, last) in enumerate(SPANS):
        place = lax.broadcasted_iota(jnp.int32, (last - first, BLOCK), 0) + (first - 128 - block * BLOCK)
        place = place <= lax.broadcasted_iota(jnp.int32, (last - first, BLOCK), 1)
        same = key_docs[first:last] == docs[:, block * BLOCK:(block + 1) * BLOCK]
        bias_ref[STARTS[block]:STARTS[block] + last - first, :] = jnp.where(same & place, 0.0, -1e30)
    qt_ref[0] = (dot_nt(attn_ref[0].T, n1t) * 0.125).astype(BF16)
    n1 = n1_ref[0]
    k_ref[0] = dot(n1, attn_ref[1]).astype(BF16)
    v = dot(n1, attn_ref[2])
    v_ref[0] = v.astype(BF16)
    vt_ref[...] = v.astype(BF16).T
    pair_ref[...] = jnp.zeros_like(pair_ref)

    def one_pair(pair, carry):
        lanes = pl.ds(pl.multiple_of(pair * 128, 128), 128)
        for block, (first, last) in enumerate(SPANS):
            start = STARTS[block]
            held = pair_ref.at[block]
            columns = pl.ds(block * BLOCK, BLOCK)
            diagonal_pair(held, qt_ref[0, lanes, columns])
            scores = dot(k_ref[0, first:last, lanes], held[...])
            bias = bias_ref[start:start + last - first, :]
            scores = scores + jnp.concatenate([bias, bias], 1)
            largest = jnp.max(scores, axis=0, keepdims=True)
            e = jnp.exp(scores - largest)
            linv = 1.0 / jnp.sum(e, axis=0, keepdims=True)
            e = e.astype(BF16)
            e_ref[0, pair, start:start + last - first, :] = e
            linv_ref[0, pair, block, :, :] = linv
            mixed = dot(vt_ref[lanes, first:last], e) * linv
            ot_ref[0, lanes, columns] = jnp.concatenate(
                [mixed[0:64, 0:128], mixed[64:128, 128:256]], 0
            ).astype(BF16)
        return carry

    lax.fori_loop(0, 4, one_pair, 0)
    h1 = x + dot(ot_ref[0].T, attn_ref[3])
    h1_ref[0] = h1
    hat, _ = norm_parts(h1)
    n2 = (hat * gain_ref[1:2, :]).astype(BF16)
    result = h1
    for part in range(4):
        before = dot(n2, w1_ref[part]) + b1_ref[part]
        cdf = 0.5 + 0.5 * lax.erf(before * 0.7071067811865476)
        active = (before * cdf).astype(BF16)
        act_ref[0, part] = active
        slope = cdf + before * jnp.exp(before * before * -0.5) * 0.3989422804014327
        slope_ref[0, part] = slope.astype(BF16)
        result = result + dot(active, w2_ref[part])
    out_ref[0] = result.astype(BF16)
    res_ref[0] = result[seg // 2:]


def full_spec(shape):
    return pl.BlockSpec(shape, lambda i: (0,) * len(shape), pipeline_mode=pl.Buffered(1))


def step_spec(shape):
    return pl.BlockSpec((1,) + shape, lambda i: (i,) + (0,) * len(shape))


def call_forward(tokens, memory, docs, keep, attn, w1, w2, b1, gains):
    n, seg, d = tokens.shape
    slots = memory.shape[1]
    outs = [
        ((seg, d), BF16), ((seg // 2, d), F32), ((seg, d), F32), ((seg + 128, d), BF16), ((d, seg), BF16),
        ((seg + 128, d), BF16), ((seg + 128, d), BF16), ((4, LIVE, 256), BF16), ((4, 4, 1, 256), F32),
        ((d, seg), BF16), ((4, seg, 512), BF16), ((4, seg, 512), BF16),
    ]
    return pl.pallas_call(
        forward_kernel,
        grid=(n,),
        out_shape=[jax.ShapeDtypeStruct((n,) + shape, kind) for shape, kind in outs],
        in_specs=[
            step_spec((seg, d)), step_spec((slots, d)), step_spec((1, seg)), step_spec((1, 128)),
            full_spec(attn.shape), full_spec(w1.shape), full_spec(w2.shape), full_spec(b1.shape), full_spec(gains.shape),
        ],
        out_specs=[step_spec(shape) for shape, _ in outs],
        scratch_shapes=[
            pltpu.VMEM((LIVE, 128), F32), pltpu.VMEM((4, 128, 256), BF16), pltpu.VMEM((d, seg + 128), BF16),
        ],
        compiler_params=pltpu.CompilerParams(vmem_limit_bytes=VMEM_LIMIT),
        name="forward_rows",
    )(tokens, memory, docs, keep, attn, w1, w2, b1, gains)


def writer_kernel(
    res_ref, mem_ref, memgrad_ref, doc_ref, keep_ref, wr_ref, gate_ref, gbias_ref, gain_ref,
    newmem_ref, dres_ref, dkept_ref, gwr_ref, ggate_ref, gsmall_ref,
    n3_ref, ns_ref, kept_ref, sq_ref, tk_ref, tv_ref, p_ref, wt_ref, dsq_ref, dtk_ref, dtv_ref, dlog_ref, dw_ref,
):
    n, half, d = res_ref.shape
    slots = mem_ref.shape[1]
    gain = gain_ref[2:3, :]

    def norm(i, carry):
        rows = pl.ds(pl.multiple_of(i * half, half), half)
        small = pl.ds(pl.multiple_of(i * slots, slots), slots)
        hat, _ = norm_parts(res_ref[i])
        n3_ref[rows, :] = (hat * gain).astype(BF16)
        kept = mem_ref[i] * keep_ref[i][:, 0:1]
        kept_ref[small, :] = kept
        hat, _ = norm_parts(kept)
        ns_ref[small, :] = (hat * gain).astype(BF16)
        tk_ref[rows, :] = dot(n3_ref[rows, :], wr_ref[1]).astype(BF16)
        tv_ref[rows, :] = dot(n3_ref[rows, :], wr_ref[2]).astype(BF16)
        return carry

    lax.fori_loop(0, n, norm, 0)
    sq_ref[...] = (dot(ns_ref[...], wr_ref[0]) * 0.125).astype(BF16)
    low_half = lax.broadcasted_iota(jnp.int32, (1, 128), 1) < 64

    def halves(rows):
        zero = jnp.zeros_like(rows)
        return jnp.concatenate([jnp.where(low_half, rows, zero), jnp.where(low_half, zero, rows)], 0)

    def read(i, carry):
        rows = pl.ds(pl.multiple_of(i * half, half), half)
        small = pl.ds(pl.multiple_of(i * slots, slots), slots)
        docs = doc_ref[i].astype(F32)
        bias = jnp.where(docs == jnp.max(docs), 0.0, -1e30)[:, docs.shape[1] - half:]
        for pair in range(4):
            lanes = slice(pair * 128, pair * 128 + 128)
            scores = dot_nt(halves(sq_ref[small, lanes]), tk_ref[rows, lanes]) + bias
            e = jnp.exp(scores - jnp.max(scores, axis=1, keepdims=True))
            p = e * (1.0 / jnp.sum(e, axis=1, keepdims=True))
            p_ref[i, pair] = p
            mixed = dot(p.astype(BF16), tv_ref[rows, lanes])
            wt_ref[small, lanes] = jnp.where(low_half, mixed[:slots], mixed[slots:]).astype(BF16)
        return carry

    lax.fori_loop(0, n, read, 0)
    write = dot(wt_ref[...], wr_ref[3])
    kept = kept_ref[...]
    write_low = write.astype(BF16)
    kept_low = kept.astype(BF16)
    logit = dot(kept_low, gate_ref[0]) + dot(write_low, gate_ref[1]) + gbias_ref[...]
    gate = jax.nn.sigmoid(logit)
    new = gate * kept + (1.0 - gate) * write
    memgrad = memgrad_ref[...].reshape(n * slots, d)
    newmem_ref[...] = new.reshape(n, slots, d)
    dlogit = memgrad * (kept - write) * gate * (1.0 - gate)
    dlog_ref[...] = dlogit.astype(BF16)
    dlow = dlog_ref[...]
    gsmall_ref[0:1, :] = jnp.sum(dlow.astype(F32), axis=0, keepdims=True)
    ggate_ref[0] = dot_tn(kept_low, dlow).astype(ggate_ref.dtype)
    ggate_ref[1] = dot_tn(write_low, dlow).astype(ggate_ref.dtype)
    dkept = memgrad * gate + dot_nt(dlow, gate_ref[0])
    dwrite = memgrad * (1.0 - gate) + dot_nt(dlow, gate_ref[1])
    dkept_ref[...] = dkept.reshape(n, slots, d)
    dw_low = dwrite.astype(BF16)
    gwr_ref[3] = dot_tn(wt_ref[...], dw_low).astype(gwr_ref.dtype)
    dw_ref[...] = dot_nt(dw_low, wr_ref[3]).astype(BF16)

    def read_back(i, carry):
        rows = pl.ds(pl.multiple_of(i * half, half), half)
        small = pl.ds(pl.multiple_of(i * slots, slots), slots)
        for pair in range(4):
            lanes = slice(pair * 128, pair * 128 + 128)
            p = p_ref[i, pair]
            grads = halves(dw_ref[small, lanes])
            dp = dot_nt(grads, tv_ref[rows, lanes])
            ds = (p * (dp - jnp.sum(dp * p, axis=1, keepdims=True))).astype(BF16)
            dq = dot(ds, tk_ref[rows, lanes]) * 0.125
            dsq_ref[small, lanes] = jnp.where(low_half, dq[:slots], dq[slots:]).astype(BF16)
            dtk_ref[rows, lanes] = dot_tn(ds, halves(sq_ref[small, lanes])).astype(BF16)
            dtv_ref[rows, lanes] = dot_tn(p.astype(BF16), grads).astype(BF16)
        return carry

    lax.fori_loop(0, n, read_back, 0)
    gwr_ref[0] = dot_tn(ns_ref[...], dsq_ref[...]).astype(gwr_ref.dtype)
    gwr_ref[1] = dot_tn(n3_ref[...], dtk_ref[...]).astype(gwr_ref.dtype)
    gwr_ref[2] = dot_tn(n3_ref[...], dtv_ref[...]).astype(gwr_ref.dtype)
    grad = dot_nt(dsq_ref[...], wr_ref[0])
    hat, rstd = norm_parts(kept_ref[...])
    dkept_ref[...] += norm_back(grad, hat, rstd, gain).reshape(n, slots, d)
    ggain = jnp.sum(grad * hat, axis=0, keepdims=True)

    def back(i, ggain):
        rows = pl.ds(pl.multiple_of(i * half, half), half)
        grad = dot_nt(dtk_ref[rows, :], wr_ref[1]) + dot_nt(dtv_ref[rows, :], wr_ref[2])
        hat, rstd = norm_parts(res_ref[i])
        dres_ref[i] = norm_back(grad, hat, rstd, gain)
        return ggain + jnp.sum(grad * hat, axis=0, keepdims=True)

    gsmall_ref[1:2, :] = lax.fori_loop(0, n, back, ggain)


def call_writer(res, memory, memory_grad, docs, keep, wr, gate, gbias, gains):
    n, half, d = res.shape
    slots = memory.shape[1]
    rows, small = n * half, n * slots
    vmem = pl.BlockSpec(memory_space=pltpu.VMEM)
    return pl.pallas_call(
        writer_kernel,
        out_shape=[
            jax.ShapeDtypeStruct((n, slots, d), F32), jax.ShapeDtypeStruct((n, half, d), F32),
            jax.ShapeDtypeStruct((n, slots, d), F32), jax.ShapeDtypeStruct((4, d, d), BF16),
            jax.ShapeDtypeStruct((2, d, d), BF16), jax.ShapeDtypeStruct((2, d), F32),
        ],
        in_specs=[vmem] * 9,
        out_specs=[vmem] * 6,
        scratch_shapes=[
            pltpu.VMEM((rows, d), BF16), pltpu.VMEM((small, d), BF16), pltpu.VMEM((small, d), F32),
            pltpu.VMEM((small, d), BF16), pltpu.VMEM((rows, d), BF16), pltpu.VMEM((rows, d), BF16),
            pltpu.VMEM((n, 4, 2 * slots, half), F32), pltpu.VMEM((small, d), BF16), pltpu.VMEM((small, d), BF16),
            pltpu.VMEM((rows, d), BF16), pltpu.VMEM((rows, d), BF16), pltpu.VMEM((small, d), BF16),
            pltpu.VMEM((small, d), BF16),
        ],
        compiler_params=pltpu.CompilerParams(vmem_limit_bytes=VMEM_LIMIT),
        name="writer",
    )(res, memory, memory_grad, docs, keep, wr, gate, gbias, gains)


def ffn_back_kernel(
    og_ref, dres_ref, h1_ref, act_ref, slope_ref, w1_ref, w2_ref, gain_ref,
    dh_ref, gw1_ref, gw2_ref, gb_ref, ggain_ref,
    acc1_ref, acc2_ref, accb_ref, accg_ref,
):
    step = pl.program_id(0)
    seg = og_ref.shape[1]

    @pl.when(step == 0)
    def _():
        acc1_ref[...] = jnp.zeros_like(acc1_ref)
        acc2_ref[...] = jnp.zeros_like(acc2_ref)
        accb_ref[...] = jnp.zeros_like(accb_ref)
        accg_ref[...] = jnp.zeros_like(accg_ref)

    top = og_ref[0, 0:seg // 2, :].astype(F32)
    bottom = og_ref[0, seg // 2:, :].astype(F32) + dres_ref[0]
    dresult = jnp.concatenate([top, bottom], 0)
    low = dresult.astype(BF16)
    h1 = h1_ref[0]
    hat, rstd = norm_parts(h1)
    gain = gain_ref[1:2, :]
    n2t = (hat * gain).astype(BF16).T
    lowt = low.T
    grad = jnp.zeros_like(dresult)
    for part in range(4):
        acc2_ref[part] += dot(lowt, act_ref[0, part])
        dbefore = (dot_nt(low, w2_ref[part]) * slope_ref[0, part].astype(F32)).astype(BF16)
        accb_ref[part] += jnp.sum(dbefore.astype(F32), axis=0, keepdims=True)
        acc1_ref[part] += dot(n2t, dbefore)
        grad = grad + dot_nt(dbefore, w1_ref[part])
    accg_ref[...] += jnp.sum(grad * hat, axis=0, keepdims=True)
    dh_ref[0] = dresult + norm_back(grad, hat, rstd, gain)

    @pl.when(step == pl.num_programs(0) - 1)
    def _():
        gw1_ref[...] = acc1_ref[...].astype(gw1_ref.dtype)
        for part in range(4):
            gw2_ref[part] = acc2_ref[part].T.astype(gw2_ref.dtype)
        gb_ref[...] = accb_ref[...]
        ggain_ref[...] = accg_ref[...]


def call_ffn_back(out_grad, dres, h1, act, slope, w1, w2, gains):
    n, seg, d = out_grad.shape
    return pl.pallas_call(
        ffn_back_kernel,
        grid=(n,),
        out_shape=[
            jax.ShapeDtypeStruct((n, seg, d), F32), jax.ShapeDtypeStruct(w1.shape, BF16),
            jax.ShapeDtypeStruct(w2.shape, BF16), jax.ShapeDtypeStruct((4, 1, 512), F32),
            jax.ShapeDtypeStruct((1, d), F32),
        ],
        in_specs=[
            step_spec((seg, d)), step_spec((seg // 2, d)), step_spec((seg, d)), step_spec((4, seg, 512)),
            step_spec((4, seg, 512)), full_spec(w1.shape), full_spec(w2.shape), full_spec(gains.shape),
        ],
        out_specs=[
            step_spec((seg, d)), full_spec(w1.shape), full_spec(w2.shape), full_spec((4, 1, 512)), full_spec((1, d)),
        ],
        scratch_shapes=[
            pltpu.VMEM(w1.shape, F32), pltpu.VMEM((4, d, 512), F32), pltpu.VMEM((4, 1, 512), F32), pltpu.VMEM((1, d), F32),
        ],
        compiler_params=pltpu.CompilerParams(vmem_limit_bytes=VMEM_LIMIT),
        name="ffn_back",
    )(out_grad, dres, h1, act, slope, w1, w2, gains)


def attn_back_kernel(
    dh_ref, tok_ref, mem_ref, keep_ref, n1_ref, qt_ref, k_ref, v_ref, e_ref, linv_ref, ot_ref, dkept_ref,
    attn_ref, gain_ref,
    gtok_ref, gmem_ref, gattn_ref, ggain_ref,
    dot_ref, kt_ref, dqt_ref, dk_ref, dv_ref, qp_ref, dp_ref, acc_ref, accg_ref,
):
    step = pl.program_id(0)
    seg = tok_ref.shape[1]
    slots = mem_ref.shape[1]

    @pl.when(step == 0)
    def _():
        acc_ref[...] = jnp.zeros_like(acc_ref)
        accg_ref[...] = jnp.zeros_like(accg_ref)

    dh = dh_ref[0]
    low = dh.astype(BF16)
    acc_ref[3] += dot(ot_ref[0], low)
    dot_ref[...] = dot_nt(attn_ref[3], low)
    kt_ref[...] = k_ref[0].T
    qp_ref[...] = jnp.zeros_like(qp_ref)
    dp_ref[...] = jnp.zeros_like(dp_ref)

    def one_pair(pair, carry):
        lanes = pl.ds(pl.multiple_of(pair * 128, 128), 128)
        dk_ref[:, lanes] = jnp.zeros((seg + 128, 128), F32)
        dv_ref[:, lanes] = jnp.zeros((seg + 128, 128), F32)
        for block, (first, last) in enumerate(SPANS):
            start = STARTS[block]
            columns = pl.ds(block * BLOCK, BLOCK)
            linv = linv_ref[0, pair, block, :, :]
            mixed_grad = dot_ref[lanes, columns]
            top = (mixed_grad[0:64] * linv[:, 0:128]).astype(BF16)
            bottom = (mixed_grad[64:128] * linv[:, 128:256]).astype(BF16)
            mixed = ot_ref[0, lanes, columns].astype(F32)
            delta = jnp.concatenate(
                [
                    jnp.sum(top.astype(F32) * mixed[0:64], axis=0, keepdims=True),
                    jnp.sum(bottom.astype(F32) * mixed[64:128], axis=0, keepdims=True),
                ],
                1,
            )
            held = dp_ref.at[block]
            held[0:64, 0:128] = top
            held[64:128, 128:256] = bottom
            query = qp_ref.at[block]
            diagonal_pair(query, qt_ref[0, lanes, columns])
            e = e_ref[0, pair, start:start + last - first, :]
            dp = dot(v_ref[0, first:last, lanes], held[...])
            ds = (e.astype(F32) * (dp - delta)).astype(BF16)
            dv_ref[first:last, lanes] += dot_nt(e, held[...])
            dk_ref[first:last, lanes] += dot_nt(ds, query[...])
            dq = dot(kt_ref[lanes, first:last], ds) * 0.125
            dqt_ref[lanes, columns] = jnp.concatenate([dq[0:64, 0:128], dq[64:128, 128:256]], 0).astype(BF16)
        return carry

    lax.fori_loop(0, 4, one_pair, 0)
    n1t = n1_ref[0].T
    dk = dk_ref[...].astype(BF16)
    dv = dv_ref[...].astype(BF16)
    acc_ref[0] += dot_nt(n1t[:, 128:], dqt_ref[...])
    acc_ref[1] += dot(n1t, dk)
    acc_ref[2] += dot(n1t, dv)
    gain = gain_ref[0:1, :]
    grad = dot_nt(dk, attn_ref[1]) + dot_nt(dv, attn_ref[2])
    slot_grad = grad[0:slots]
    kept = mem_ref[0] * keep_ref[0][:, 0:1]
    hat, rstd = norm_parts(kept)
    ggain = jnp.sum(slot_grad * hat, axis=0, keepdims=True)
    gmem_ref[0] = (dkept_ref[0] + norm_back(slot_grad, hat, rstd, gain)) * keep_ref[0][:, 0:1]
    grad = grad[128:] + dot_nt(dqt_ref[...].T, attn_ref[0])
    hat, rstd = norm_parts(tok_ref[0].astype(F32))
    accg_ref[...] += ggain + jnp.sum(grad * hat, axis=0, keepdims=True)
    gtok_ref[0] = dh + norm_back(grad, hat, rstd, gain)

    @pl.when(step == pl.num_programs(0) - 1)
    def _():
        gattn_ref[...] = acc_ref[...].astype(gattn_ref.dtype)
        ggain_ref[...] = accg_ref[...]


def call_attn_back(dh, tokens, memory, keep, n1, qt, k, v, e, linv, ot, dkept, attn, gains):
    n, seg, d = tokens.shape
    slots = memory.shape[1]
    return pl.pallas_call(
        attn_back_kernel,
        grid=(n,),
        out_shape=[
            jax.ShapeDtypeStruct((n, seg, d), F32), jax.ShapeDtypeStruct((n, slots, d), F32),
            jax.ShapeDtypeStruct((4, d, d), BF16), jax.ShapeDtypeStruct((1, d), F32),
        ],
        in_specs=[
            step_spec((seg, d)), step_spec((seg, d)), step_spec((slots, d)), step_spec((1, 128)),
            step_spec((seg + 128, d)), step_spec((d, seg)), step_spec((seg + 128, d)), step_spec((seg + 128, d)),
            step_spec((4, LIVE, 256)), step_spec((4, 4, 1, 256)), step_spec((d, seg)), step_spec((slots, d)),
            full_spec(attn.shape), full_spec(gains.shape),
        ],
        out_specs=[step_spec((seg, d)), step_spec((slots, d)), full_spec((4, d, d)), full_spec((1, d))],
        scratch_shapes=[
            pltpu.VMEM((d, seg), F32), pltpu.VMEM((d, seg + 128), BF16), pltpu.VMEM((d, seg), BF16),
            pltpu.VMEM((seg + 128, d), F32), pltpu.VMEM((seg + 128, d), F32), pltpu.VMEM((4, 128, 256), BF16),
            pltpu.VMEM((4, 128, 256), BF16), pltpu.VMEM((4, d, d), F32), pltpu.VMEM((1, d), F32),
        ],
        compiler_params=pltpu.CompilerParams(vmem_limit_bytes=VMEM_LIMIT),
        name="attn_back",
    )(dh, tokens, memory, keep, n1, qt, k, v, e, linv, ot, dkept, attn, gains)


def local_layer(tokens, memory, docs, resets, out_grad, memory_grad, attn, w1, w2, wr, gate, b1, gbias, gains):
    n = tokens.shape[0]
    keep = jnp.broadcast_to((1 - resets).astype(F32)[:, None, None], (n, 1, 128))
    docs = docs[:, None, :]
    out, res, h1, n1, qt, k, v, e, linv, ot, act, slope = call_forward(
        tokens, memory, docs, keep, attn, w1, w2, b1, gains
    )
    new_memory, dres, dkept, gwr, ggate, gsmall = call_writer(
        res, memory, memory_grad, docs, keep, wr, gate, gbias, gains
    )
    dh, gw1, gw2, gb, ggain_two = call_ffn_back(out_grad, dres, h1, act, slope, w1, w2, gains)
    grad_tokens, grad_memory, gattn, ggain_one = call_attn_back(
        dh, tokens, memory, keep, n1, qt, k, v, e, linv, ot, dkept, attn, gains
    )
    ggains = jnp.concatenate([ggain_one, ggain_two, gsmall[1:2]], 0)
    return out, new_memory, grad_tokens, grad_memory, gattn, gw1, gw2, gwr, ggate, gb.reshape(-1), gsmall[0], ggains


MESH = pl.DeviceIdType.MESH


class Place:
    def __init__(self):
        self.dp = lax.axis_index("dp")
        self.core = lax.axis_index("outer")
        self.z, self.y, self.x = self.dp // 4, (self.dp // 2) % 2, self.dp % 2

    def sibling(self):
        return (self.dp, 1 - self.core)

    def along_x(self):
        return (self.dp + 1 - 2 * self.x, self.core)

    def along_y(self):
        return (self.dp + 2 - 4 * self.y, self.core)

    def other_z(self, shift):
        return lax.rem(self.z + shift, 4)

    def along_z(self, shift):
        return (self.dp + 4 * (self.other_z(shift) - self.z), self.core)

    def greet(self):
        barrier = pltpu.get_barrier_semaphore()
        everyone = [self.sibling(), self.along_x(), self.along_y()] + [self.along_z(shift) for shift in (1, 2, 3)]
        for device in everyone:
            pl.semaphore_signal(barrier, inc=1, device_id=device, device_id_type=MESH)
        pl.semaphore_wait(barrier, len(everyone))


def remote(src, dst, send, recv, device):
    return pltpu.make_async_remote_copy(
        src_ref=src, dst_ref=dst, send_sem=send, recv_sem=recv, device_id=device, device_id_type=MESH
    )


class Gather:
    STAGES = 7

    def __init__(self, place, view, own, lane, send, recv, local):
        self.place, self.view, self.own, self.lane = place, view, own, lane
        self.send, self.recv, self.local = send, recv, local
        self.unit = 2 * place.core + lane
        self.sent = []
        self.every = slice(None)

    def go(self, stage, src, dst, device):
        copy = remote(src, dst, self.send.at[stage], self.recv.at[stage], device)
        copy.start()
        self.sent.append(copy)

    def arrived(self, stage, dst):
        remote(dst, dst, self.send.at[stage], self.recv.at[stage], self.place.sibling()).wait_recv()

    def stage_z(self):
        at = self.place
        mine = self.view(self.unit, at.z, at.y, at.x)
        self.keep = pltpu.make_async_copy(self.own, mine, self.local)
        self.keep.start()
        for shift in (1, 2, 3):
            self.go(shift - 1, self.own, mine, at.along_z(shift))

    def wait_z(self):
        at = self.place
        self.keep.wait()
        for shift in (1, 2, 3):
            self.arrived(shift - 1, self.view(self.unit, at.other_z(4 - shift), at.y, at.x))

    def stage_first(self):
        at = self.place
        part = self.view(self.unit, self.every, at.y, at.x)
        self.go(3, part, part, at.along_y() if self.lane else at.along_x())

    def wait_first(self):
        at = self.place
        if self.lane:
            self.arrived(3, self.view(self.unit, self.every, 1 - at.y, at.x))
        else:
            self.arrived(3, self.view(self.unit, self.every, at.y, 1 - at.x))

    def half(self, unit, far):
        at = self.place
        if self.lane:
            return self.view(unit, self.every, self.every, 1 - at.x if far else at.x)
        return self.view(unit, self.every, 1 - at.y if far else at.y, self.every)

    def stage_second(self):
        at = self.place
        part = self.half(self.unit, False)
        self.go(4, part, part, at.along_x() if self.lane else at.along_y())
        self.go(5, part, part, at.sibling())

    def wait_second(self):
        self.arrived(4, self.half(self.unit, True))

    def stage_share(self):
        part = self.half(self.unit, True)
        self.go(6, part, part, self.place.sibling())

    def wait_share(self):
        other = 2 * (1 - self.place.core) + self.lane
        self.arrived(5, self.half(other, False))
        self.arrived(6, self.half(other, True))

    def finish(self):
        for copy in self.sent:
            copy.wait_send()


class GatherSmall:
    def __init__(self, place, view, own, send, recv, local):
        self.place, self.view, self.own = place, view, own
        self.send, self.recv, self.local = send, recv, local
        self.sent = []

    go = Gather.go
    arrived = Gather.arrived
    finish = Gather.finish

    def stage_z(self):
        at = self.place
        mine = self.view(at.z, at.y, at.x)
        self.keep = pltpu.make_async_copy(self.own, mine, self.local)
        self.keep.start()
        for shift in (1, 2, 3):
            self.go(shift - 1, self.own, mine, at.along_z(shift))

    def wait_z(self):
        at = self.place
        self.keep.wait()
        for shift in (1, 2, 3):
            self.arrived(shift - 1, self.view(at.other_z(4 - shift), at.y, at.x))

    def stage_first(self):
        at = self.place
        part = self.view(slice(None), at.y, at.x)
        self.go(3, part, part, at.along_x())

    def wait_first(self):
        at = self.place
        self.arrived(3, self.view(slice(None), at.y, 1 - at.x))

    def stage_second(self):
        at = self.place
        part = self.view(slice(None), at.y, slice(None))
        self.go(4, part, part, at.along_y())

    def wait_second(self):
        at = self.place
        self.arrived(4, self.view(slice(None), 1 - at.y, slice(None)))


def unit_first(ref):
    return lambda u, z, y, x: ref.at[u, z, y, x]


def unit_last(ref):
    return lambda u, z, y, x: ref.at[z, y, x, u]


def gather_kernel(
    src_ref, gsrc_ref, ssrc_ref, attn_ref, w1_ref, w2_ref, wr_ref, gate_ref, small_ref, send, recv, local, ssend, srecv, slocal
):
    place = Place()
    place.greet()
    views = [unit_first(attn_ref), unit_first(w1_ref), unit_last(w2_ref), unit_first(wr_ref), unit_last(gate_ref)]
    rounds = []
    for r, view in enumerate(views):
        lanes = []
        for lane in range(2):
            unit = 2 * place.core + lane
            own = src_ref.at[4 * r + unit] if r < 4 else gsrc_ref.at[unit]
            lanes.append(Gather(place, view, own, lane, send.at[r, lane], recv.at[r, lane], local.at[r, lane]))
        rounds.append(lanes)
    small = GatherSmall(place, lambda z, y, x: small_ref.at[z, y, x], ssrc_ref, ssend, srecv, slocal)

    def each(r, name):
        for lane in rounds[r]:
            getattr(lane, name)()

    last = len(rounds) - 1
    small.stage_z()
    each(0, "stage_z")
    small.wait_z()
    small.stage_first()
    each(0, "wait_z")
    for r in range(last + 1):
        each(r, "stage_first")
        if r == 0:
            small.wait_first()
            small.stage_second()
        if r > 0:
            each(r - 1, "wait_second")
            each(r - 1, "stage_share")
        if r < last:
            each(r + 1, "stage_z")
        each(r, "wait_first")
        each(r, "stage_second")
        if r < last:
            each(r + 1, "wait_z")
    small.wait_second()
    each(last, "wait_second")
    each(last, "stage_share")
    for r in range(last + 1):
        each(r, "wait_share")
        each(r, "finish")
    small.finish()


def call_gather(units, gate_units, small):
    _, rows, d = units.shape
    any_space = pl.BlockSpec(memory_space=pl.ANY)
    first = (4, 4, 2, 2, rows, d)
    shapes = [
        (first, BF16), (first, BF16), ((4, 2, 2, 4, rows, d), BF16), (first, BF16), ((4, 2, 2, 4, rows // 2, d), BF16),
        ((4, 2, 2, 8, 128), F32),
    ]
    return pl.pallas_call(
        gather_kernel,
        out_shape=[jax.ShapeDtypeStruct(shape, kind) for shape, kind in shapes],
        in_specs=[any_space] * 3,
        out_specs=[any_space] * 6,
        scratch_shapes=[
            pltpu.SemaphoreType.DMA((5, 2, 7)), pltpu.SemaphoreType.DMA((5, 2, 7)), pltpu.SemaphoreType.DMA((5, 2)),
            pltpu.SemaphoreType.DMA((5,)), pltpu.SemaphoreType.DMA((5,)), pltpu.SemaphoreType.DMA,
        ],
        compiler_params=pltpu.CompilerParams(collective_id=0, has_side_effects=True),
        name="gather_weights",
    )(units, gate_units, small)


class Reduce:
    def __init__(self, place, grad, lane, acc, wide, mid, narrow, final, send, recv):
        self.place, self.grad, self.lane = place, grad, lane
        self.acc, self.wide, self.mid, self.narrow, self.final = acc, wide, mid, narrow, final
        self.send, self.recv = send, recv
        self.unit = 2 * place.core + lane
        self.other = 2 * (1 - place.core) + lane
        self.sent = []
        self.every = slice(None)

    go = Gather.go
    arrived = Gather.arrived
    finish = Gather.finish

    def stage_share(self):
        e = self.every
        self.go(0, self.grad(self.other, e, e, e), self.wide, self.place.sibling())

    def wait_share(self):
        self.arrived(0, self.wide)
        for z in range(4):
            self.acc[z] = self.grad(self.unit, z, self.every, self.every)[...] + self.wide[z]

    def half(self, far):
        at = self.place
        if self.lane:
            return self.acc.at[:, :, 1 - at.x if far else at.x]
        return self.acc.at[:, 1 - at.y if far else at.y]

    def stage_first(self):
        at = self.place
        self.go(1, self.half(True), self.mid, at.along_x() if self.lane else at.along_y())

    def wait_first(self):
        self.arrived(1, self.mid)
        half = self.half(False)
        half[...] = half[...] + self.mid[...]

    def stage_second(self):
        at = self.place
        if self.lane:
            part, device = self.acc.at[:, 1 - at.y, at.x], at.along_y()
        else:
            part, device = self.acc.at[:, at.y, 1 - at.x], at.along_x()
        self.go(2, part, self.narrow.at[0:4], device)

    def wait_second(self):
        at = self.place
        self.arrived(2, self.narrow.at[0:4])
        part = self.acc.at[:, at.y, at.x]
        part[...] = part[...] + self.narrow[0:4]

    def stage_z(self):
        at = self.place
        for shift in (1, 2, 3):
            self.go(2 + shift, self.acc.at[at.other_z(shift), at.y, at.x], self.narrow.at[3 + shift], at.along_z(shift))

    def wait_z(self):
        at = self.place
        total = self.acc[at.z, at.y, at.x].astype(F32)
        for shift in (1, 2, 3):
            self.arrived(2 + shift, self.narrow.at[3 + shift])
            total = total + self.narrow[3 + shift].astype(F32)
        self.final[self.unit] = total

    def stage_final(self):
        self.go(6, self.final.at[self.unit], self.final.at[self.unit], self.place.sibling())

    def wait_final(self):
        self.arrived(6, self.final.at[self.other])


class ReduceSmall:
    def __init__(self, place, grad, wide, mid, narrow, final, send, recv):
        self.place, self.acc = place, grad
        self.wide, self.mid, self.narrow, self.final = wide, mid, narrow, final
        self.send, self.recv = send, recv
        self.sent = []

    go = Gather.go
    arrived = Gather.arrived
    finish = Gather.finish

    def stage_share(self):
        self.go(0, self.acc, self.wide, self.place.sibling())

    def wait_share(self):
        self.arrived(0, self.wide)
        self.sent.pop().wait_send()
        self.acc[...] = self.acc[...] + self.wide[...]

    def stage_first(self):
        at = self.place
        self.go(1, self.acc.at[:, 1 - at.y], self.mid, at.along_y())

    def wait_first(self):
        at = self.place
        self.arrived(1, self.mid)
        half = self.acc.at[:, at.y]
        half[...] = half[...] + self.mid[...]

    def stage_second(self):
        at = self.place
        self.go(2, self.acc.at[:, at.y, 1 - at.x], self.narrow.at[0:4], at.along_x())

    def wait_second(self):
        at = self.place
        self.arrived(2, self.narrow.at[0:4])
        part = self.acc.at[:, at.y, at.x]
        part[...] = part[...] + self.narrow[0:4]

    def stage_z(self):
        at = self.place
        for shift in (1, 2, 3):
            self.go(2 + shift, self.acc.at[at.other_z(shift), at.y, at.x], self.narrow.at[3 + shift], at.along_z(shift))

    def wait_z(self):
        at = self.place
        total = self.acc[at.z, at.y, at.x]
        for shift in (1, 2, 3):
            self.arrived(2 + shift, self.narrow.at[3 + shift])
            total = total + self.narrow[3 + shift]
        self.final[...] = total


def reduce_kernel(
    gattn_ref, gw1_ref, gw2_ref, gwr_ref, ggate_ref, gsmall_ref, out_ref, gout_ref, sout_ref,
    acc, wide, mid, narrow, gacc, gwide, gmid, gnarrow, sgrad, swide, smid, snarrow, send, recv, ssend, srecv,
):
    place = Place()
    place.greet()
    order = [4, 3, 2, 1, 0]
    grads = [unit_first(gattn_ref), unit_first(gw1_ref), unit_last(gw2_ref), unit_first(gwr_ref), unit_last(ggate_ref)]
    rounds = {}
    for r in order:
        rounds[r] = []
        for lane in range(2):
            scratch = (gacc, gwide, gmid, gnarrow) if r == 4 else [ref.at[r] for ref in (acc, wide, mid, narrow)]
            final = gout_ref if r == 4 else out_ref.at[r]
            rounds[r].append(
                Reduce(place, grads[r], lane, *[ref.at[lane] for ref in scratch], final, send.at[r, lane], recv.at[r, lane])
            )
    sgrad[...] = gsmall_ref[...]
    small = ReduceSmall(place, sgrad, swide, smid, snarrow, sout_ref, ssend, srecv)

    def each(r, name):
        for lane in rounds[r]:
            getattr(lane, name)()

    stages = ("share", "first", "second", "z", "final")
    small.stage_share()
    for tick in range(len(order) + len(stages)):
        for s in reversed(range(len(stages) + 1)):
            i = tick - s
            if 0 <= i < len(order):
                if s > 0:
                    each(order[i], "wait_" + stages[s - 1])
                if s < len(stages):
                    each(order[i], "stage_" + stages[s])
        if tick < 4:
            getattr(small, "wait_" + stages[tick])()
        if tick < 3:
            getattr(small, "stage_" + stages[tick + 1])()
    for r in order:
        each(r, "finish")
    small.finish()


def call_reduce(gattn, gw1, gw2, gwr, ggate, gsmall):
    rows, d = gattn.shape[-2:]
    vmem = pl.BlockSpec(memory_space=pltpu.VMEM)

    def scratch(lead, rows):
        return [
            pltpu.VMEM(lead + (4, 2, 2, rows, d), BF16), pltpu.VMEM(lead + (4, 2, 2, rows, d), BF16),
            pltpu.VMEM(lead + (4, 2, rows, d), BF16), pltpu.VMEM(lead + (7, rows, d), BF16),
        ]

    return pl.pallas_call(
        reduce_kernel,
        out_shape=[
            jax.ShapeDtypeStruct((4, 4, rows, d), F32), jax.ShapeDtypeStruct((4, rows // 2, d), F32),
            jax.ShapeDtypeStruct((8, 128), F32),
        ],
        in_specs=[vmem] * 6,
        out_specs=[vmem] * 3,
        scratch_shapes=scratch((4, 2), rows) + scratch((2,), rows // 2) + [
            pltpu.VMEM((4, 2, 2, 8, 128), F32), pltpu.VMEM((4, 2, 2, 8, 128), F32), pltpu.VMEM((4, 2, 8, 128), F32),
            pltpu.VMEM((7, 8, 128), F32),
            pltpu.SemaphoreType.DMA((5, 2, 7)), pltpu.SemaphoreType.DMA((5, 2, 7)),
            pltpu.SemaphoreType.DMA((6,)), pltpu.SemaphoreType.DMA((6,)),
        ],
        compiler_params=pltpu.CompilerParams(collective_id=1, has_side_effects=True, vmem_limit_bytes=VMEM_LIMIT),
        name="reduce_grads",
    )(gattn, gw1, gw2, gwr, ggate, gsmall)


def pack_weights(attn_qkv, attn_out, ffn_in, ffn_out, writer_qkv, writer_out):
    rows, d = attn_out.shape
    blocks = ffn_in.shape[1] // d
    return jnp.concatenate(
        [
            attn_qkv, attn_out[None], ffn_in.reshape(rows, blocks, d).transpose(1, 0, 2), ffn_out.reshape(blocks, rows, d),
            writer_qkv, writer_out[None],
        ],
        0,
    )


def own_weights(owned, gate):
    rows, d = owned.shape[2:]
    return (
        owned[0, 0:3], owned[0, 3], owned[1].transpose(1, 0, 2).reshape(rows, 4 * d), owned[2].reshape(4 * rows, d),
        owned[3, 0:3], owned[3, 3], gate.reshape(2 * rows, d),
    )


def ring_weights(units, gate_weight, ffn_bias, gate_bias, gains):
    rows, d = units.shape[1:]
    place = lax.axis_index("dp") % 4
    lane = jnp.arange(128) // rows == place
    narrow = jnp.concatenate([gate_bias[None], gains], 0)
    narrow = jnp.where(lane, jnp.tile(narrow, (1, 128 // rows)), 0)
    small = jnp.concatenate([ffn_bias[None], narrow, jnp.zeros((3, 128), BF16)], 0).astype(F32)
    attn, w1, w2, wr, gate, small = call_gather(units, gate_weight.reshape(4, rows // 2, d), small)
    small = small.reshape(4, 4, 8, 128)
    b1 = small[:, :, 0, :].reshape(4, 1, d)
    narrow = small.sum(1).transpose(1, 0, 2).reshape(8, d)
    return (
        attn.reshape(4, d, d), w1.reshape(4, d, d), w2.reshape(4, d, d), wr.reshape(4, d, d), gate.reshape(2, d, d),
        b1, narrow[1:2], narrow[2:5],
    )


def ring_grads(rows, gattn, gw1, gw2, gwr, ggate, gb, ggb, ggains):
    d = gattn.shape[-1]
    narrow = jnp.concatenate([ggb[None], ggains], 0).reshape(4, 4, 128).transpose(1, 0, 2)
    narrow = jnp.repeat(narrow, 4, axis=0)
    small = jnp.concatenate([gb.reshape(16, 1, 128), narrow, jnp.zeros((16, 3, 128), F32)], 1)
    first = (4, 4, 2, 2, rows, d)
    owned, gate, small = call_reduce(
        gattn.reshape(first), gw1.reshape(first), gw2.reshape(4, 2, 2, 4, rows, d), gwr.reshape(first),
        ggate.reshape(4, 2, 2, 4, rows // 2, d), small.reshape(4, 2, 2, 8, 128),
    )
    place = lax.axis_index("dp") % 4
    narrow = lax.dynamic_slice(small, (0, place * rows), (8, rows))
    return own_weights(owned, gate), small[0], narrow[1], narrow[2:5]


def plain_weights(units, gate_weight, ffn_bias, gate_bias, gains):
    _, rows, d = units.shape
    packed = lax.all_gather(jnp.concatenate([units, gate_weight.reshape(2, rows, d)], 0), "dp", axis=0)
    n = packed.shape[0]

    def by_rows(first, last):
        return packed[:, first:last].transpose(1, 0, 2, 3).reshape(last - first, n * rows, d)

    small = jnp.concatenate([ffn_bias.reshape(4, rows), gate_bias[None], gains], 0).astype(F32)
    small = lax.all_gather(small, "dp", axis=0)
    b1 = small[:, 0:4].reshape(4, 1, d)
    small = small.transpose(1, 0, 2).reshape(8, d)
    return (
        by_rows(0, 4), by_rows(4, 8), packed[:, 8:12].reshape(4, d, d), by_rows(12, 16), packed[:, 16:18].reshape(2, d, d),
        b1, small[4:5], small[5:8],
    )


def plain_grads(rows, gattn, gw1, gw2, gwr, ggate, gb, ggb, ggains):
    d = gattn.shape[-1]
    n = d // rows

    def by_rows(grad):
        return grad.reshape(-1, n, rows, d).transpose(1, 0, 2, 3)

    packed = jnp.concatenate(
        [by_rows(gattn), by_rows(gw1), gw2.reshape(n, 4, rows, d), by_rows(gwr), ggate.reshape(n, 2, rows, d)], 1
    )
    owned = lax.psum_scatter(packed.astype(F32), "dp", scatter_dimension=0, tiled=False)
    owned = lax.psum(owned.astype(BF16), "outer").astype(F32)
    small = jnp.concatenate(
        [gb.reshape(n, 4 * rows), ggb.reshape(n, rows), ggains.reshape(3, n, rows).transpose(1, 0, 2).reshape(n, 3 * rows)], 1
    )
    small = lax.psum(lax.psum_scatter(small, "dp", scatter_dimension=0, tiled=False), "outer")
    return (
        own_weights(owned[0:16].reshape(4, 4, rows, d), owned[16:18]),
        small[0:4 * rows], small[4 * rows:5 * rows], small[5 * rows:].reshape(3, rows),
    )


def body(
    tokens, memory, doc_ids, resets, out_grad, memory_grad,
    attn_qkv, attn_out, ffn_in, ffn_bias, ffn_out, writer_qkv, writer_out, gate_weight, gate_bias, gains,
):
    micro, segs, seg, d = tokens.shape
    slots = memory.shape[2]
    rows = attn_out.shape[0]
    ring = lax.axis_size("dp") == 16 and lax.axis_size("outer") == 2 and rows == 32
    units = pack_weights(attn_qkv, attn_out, ffn_in, ffn_out, writer_qkv, writer_out)
    spread = ring_weights if ring else plain_weights
    attn, w1, w2, wr, gate, b1, gbias, gain = spread(units, gate_weight, ffn_bias, gate_bias, gains)
    out, new_memory, grad_tokens, grad_memory, gattn, gw1, gw2, gwr, ggate, gb, ggb, ggains = local_layer(
        tokens.reshape(micro * segs, seg, d), memory.reshape(micro * segs, slots, d), doc_ids.reshape(micro * segs, seg),
        resets.reshape(micro * segs), out_grad.reshape(micro * segs, seg, d), memory_grad.reshape(micro * segs, slots, d),
        attn, w1, w2, wr, gate, b1, gbias, gain,
    )
    collect = ring_grads if ring else plain_grads
    (gqkv, gout, gin, gffn, gwqkv, gwout, ggw), gb, ggb, ggains = collect(
        rows, gattn, gw1, gw2, gwr, ggate, gb, ggb, ggains
    )
    return (
        out.reshape(micro, segs, seg, d), new_memory.reshape(micro, segs, slots, d),
        grad_tokens.reshape(micro, segs, seg, d), grad_memory.reshape(micro, segs, slots, d),
        gqkv, gout, gin, gb, gffn, gwqkv, gwout, ggw, ggb, ggains,
    )


def solution(mesh):
    split = ("dp", "outer")
    whole = P(None, split, None, None)
    weights = (
        P(None, "dp", None), P("dp", None), P("dp", None), P("dp"), P("dp", None), P(None, "dp", None),
        P("dp", None), P("dp", None), P("dp"), P(None, "dp"),
    )
    return jax.shard_map(
        body,
        mesh=mesh,
        in_specs=(whole, whole, P(None, split, None), P(None, split), whole, whole) + weights,
        out_specs=(whole, whole, whole, whole) + weights,
        check_vma=False,
    )
```

```python
import functools

import jax
import jax.numpy as jnp
from jax import lax
from jax.experimental import pallas as pl
from jax.experimental.pallas import tpu as pltpu
from jax.sharding import PartitionSpec as P

HEADS = 8
BLOCK = 128
SPANS = ((0, 256), (0, 384), (128, 512), (256, 640))
STARTS = (0, 256, 640, 1024)
LIVE = 1408
F32 = jnp.float32
BF16 = jnp.bfloat16
VMEM_LIMIT = 60 * 1024 * 1024


def dot(a, b):
    return jnp.dot(a, b, preferred_element_type=F32)


def dot_nt(a, b):
    return lax.dot_general(a, b, (((1,), (1,)), ((), ())), preferred_element_type=F32)


def dot_tn(a, b):
    return lax.dot_general(a, b, (((0,), (0,)), ((), ())), preferred_element_type=F32)


def norm_parts(rows):
    centred = rows - jnp.mean(rows, axis=-1, keepdims=True)
    rstd = lax.rsqrt(jnp.mean(centred * centred, axis=-1, keepdims=True) + 1e-05)
    return centred * rstd, rstd


def norm_back(grad, hat, rstd, gain):
    scaled = grad * gain
    return rstd * (
        scaled
        - jnp.mean(scaled, axis=-1, keepdims=True)
        - hat * jnp.mean(scaled * hat, axis=-1, keepdims=True)
    )


def diagonal_pair(ref, top):
    ref[0:64, 0:128] = top[0:64]
    ref[64:128, 128:256] = top[64:128]


MESH = pl.DeviceIdType.MESH
EVERY = slice(None)


class Place:
    def __init__(self):
        self.dp = lax.axis_index("dp")
        self.core = lax.axis_index("outer")
        self.z, self.y, self.x = self.dp // 4, (self.dp // 2) % 2, self.dp % 2

    def sibling(self):
        return (self.dp, 1 - self.core)

    def along_x(self):
        return (self.dp + 1 - 2 * self.x, self.core)

    def along_y(self):
        return (self.dp + 2 - 4 * self.y, self.core)

    def other_z(self, shift):
        return lax.rem(self.z + shift, 4)

    def along_z(self, shift):
        return (self.dp + 4 * (self.other_z(shift) - self.z), self.core)

    def greet(self):
        barrier = pltpu.get_barrier_semaphore()
        everyone = [self.sibling(), self.along_x(), self.along_y()] + [self.along_z(shift) for shift in (1, 2, 3)]
        for device in everyone:
            pl.semaphore_signal(barrier, inc=1, device_id=device, device_id_type=MESH)
        pl.semaphore_wait(barrier, len(everyone))


class Travel:
    def __init__(self, place, send, recv):
        self.place, self.send, self.recv = place, send, recv

    def copy(self, stage, src, dst, device):
        return pltpu.make_async_remote_copy(
            src_ref=src, dst_ref=dst, send_sem=self.send.at[stage], recv_sem=self.recv.at[stage], device_id=device,
            device_id_type=MESH,
        )

    def go(self, stage, src, dst, device):
        self.copy(stage, src, dst, device).start()

    def arrived(self, stage, dst):
        self.copy(stage, dst, dst, self.place.sibling()).wait_recv()

    def left(self, stage, src):
        self.copy(stage, src, src, self.place.sibling()).wait_send()


class Gather(Travel):
    def __init__(self, place, view, own, lane, send, recv, local):
        super().__init__(place, send, recv)
        self.view, self.own, self.lane, self.local = view, own, lane, local
        self.unit = 2 * place.core + lane

    def mine(self):
        at = self.place
        return self.view(self.unit, at.z, at.y, at.x)

    def stage_z(self):
        at = self.place
        pltpu.make_async_copy(self.own(self.unit), self.mine(), self.local).start()
        for shift in (1, 2, 3):
            self.go(shift - 1, self.own(self.unit), self.mine(), at.along_z(shift))

    def wait_z(self):
        at = self.place
        pltpu.make_async_copy(self.own(self.unit), self.mine(), self.local).wait()
        for shift in (1, 2, 3):
            self.arrived(shift - 1, self.view(self.unit, at.other_z(4 - shift), at.y, at.x))

    def column(self, far):
        at = self.place
        if self.lane:
            return self.view(self.unit, EVERY, 1 - at.y if far else at.y, at.x)
        return self.view(self.unit, EVERY, at.y, 1 - at.x if far else at.x)

    def half(self, unit, far):
        at = self.place
        if self.lane:
            return self.view(unit, EVERY, EVERY, 1 - at.x if far else at.x)
        return self.view(unit, EVERY, 1 - at.y if far else at.y, EVERY)

    def stage_first(self):
        part = self.column(False)
        self.go(3, part, part, self.place.along_y() if self.lane else self.place.along_x())

    def wait_first(self):
        self.arrived(3, self.column(True))

    def stage_second(self):
        part = self.half(self.unit, False)
        self.go(4, part, part, self.place.along_x() if self.lane else self.place.along_y())
        self.go(5, part, part, self.place.sibling())

    def wait_second(self):
        self.arrived(4, self.half(self.unit, True))

    def stage_share(self):
        part = self.half(self.unit, True)
        self.go(6, part, part, self.place.sibling())

    def wait_share(self):
        other = 2 * (1 - self.place.core) + self.lane
        self.arrived(5, self.half(other, False))
        self.arrived(6, self.half(other, True))

    def finish(self):
        for stage in range(3):
            self.left(stage, self.own(self.unit))
        self.left(3, self.column(False))
        self.left(4, self.half(self.unit, False))
        self.left(5, self.half(self.unit, False))
        self.left(6, self.half(self.unit, True))


class GatherSmall(Travel):
    def __init__(self, place, ref, own, send, recv):
        super().__init__(place, send, recv)
        self.ref, self.own = ref, own

    def stage_z(self):
        at = self.place
        self.ref[at.z, at.y, at.x] = self.own[...]
        for shift in (1, 2, 3):
            self.go(shift - 1, self.own, self.ref.at[at.z, at.y, at.x], at.along_z(shift))

    def wait_z(self):
        at = self.place
        for shift in (1, 2, 3):
            self.arrived(shift - 1, self.ref.at[at.other_z(4 - shift), at.y, at.x])

    def stage_first(self):
        at = self.place
        part = self.ref.at[:, at.y, at.x]
        self.go(3, part, part, at.along_x())

    def wait_first(self):
        at = self.place
        self.arrived(3, self.ref.at[:, at.y, 1 - at.x])

    def stage_second(self):
        at = self.place
        part = self.ref.at[:, at.y]
        self.go(4, part, part, at.along_y())

    def wait_second(self):
        at = self.place
        self.arrived(4, self.ref.at[:, 1 - at.y])

    def finish(self):
        at = self.place
        for stage in range(3):
            self.left(stage, self.own)
        self.left(3, self.ref.at[:, at.y, at.x])
        self.left(4, self.ref.at[:, at.y])


def unit_first(ref):
    return lambda u, z, y, x: ref.at[u, z, y, x]


def unit_last(ref):
    return lambda u, z, y, x: ref.at[z, y, x, u]


class Reduce(Travel):
    def __init__(self, place, grad, lane, acc, wide, mid, narrow, final, send, recv, local):
        super().__init__(place, send, recv)
        self.grad, self.lane, self.local = grad, lane, local
        self.acc, self.wide, self.mid, self.narrow, self.final = acc, wide, mid, narrow, final
        self.unit = 2 * place.core + lane
        self.other = 2 * (1 - place.core) + lane

    def whole(self, unit):
        return self.grad(unit, EVERY, EVERY, EVERY)

    def stage_share(self):
        self.go(0, self.whole(self.other), self.wide, self.place.sibling())
        pltpu.make_async_copy(self.whole(self.unit), self.acc, self.local).start()

    def wait_share(self):
        pltpu.make_async_copy(self.whole(self.unit), self.acc, self.local).wait()
        self.arrived(0, self.wide)

        def add(z, carry):
            self.acc[z] = self.acc[z] + self.wide[z]
            return carry

        lax.fori_loop(0, 4, add, 0)

    def half(self, far):
        at = self.place
        if self.lane:
            return self.acc.at[:, :, 1 - at.x if far else at.x]
        return self.acc.at[:, 1 - at.y if far else at.y]

    def stage_first(self):
        at = self.place
        self.go(1, self.half(True), self.mid, at.along_x() if self.lane else at.along_y())

    def wait_first(self):
        at = self.place
        self.arrived(1, self.mid)

        def add(z, carry):
            for i in range(2):
                part = self.acc.at[z, i, at.x] if self.lane else self.acc.at[z, at.y, i]
                part[...] = part[...] + self.mid[z, i]
            return carry

        lax.fori_loop(0, 4, add, 0)

    def quarter(self):
        at = self.place
        if self.lane:
            return self.acc.at[:, 1 - at.y, at.x]
        return self.acc.at[:, at.y, 1 - at.x]

    def stage_second(self):
        self.go(2, self.quarter(), self.narrow.at[0:4], self.place.along_y() if self.lane else self.place.along_x())

    def wait_second(self):
        at = self.place
        self.arrived(2, self.narrow.at[0:4])
        part = self.acc.at[:, at.y, at.x]
        part[...] = part[...] + self.narrow[0:4]

    def block(self, shift):
        at = self.place
        return self.acc.at[at.other_z(shift), at.y, at.x]

    def stage_z(self):
        for shift in (1, 2, 3):
            self.go(2 + shift, self.block(shift), self.narrow.at[3 + shift], self.place.along_z(shift))

    def wait_z(self):
        total = self.block(0)[...].astype(F32)
        for shift in (1, 2, 3):
            self.arrived(2 + shift, self.narrow.at[3 + shift])
            total = total + self.narrow[3 + shift].astype(F32)
        self.final[self.unit] = total

    def stage_final(self):
        self.go(6, self.final.at[self.unit], self.final.at[self.unit], self.place.sibling())

    def wait_final(self):
        self.arrived(6, self.final.at[self.other])
        self.left(0, self.whole(self.other))
        self.left(1, self.half(True))
        self.left(2, self.quarter())
        for shift in (1, 2, 3):
            self.left(2 + shift, self.block(shift))
        self.left(6, self.final.at[self.unit])


class ReduceSmall(Travel):
    def __init__(self, place, own, acc, wide, mid, narrow, final, send, recv):
        super().__init__(place, send, recv)
        self.own, self.acc, self.wide, self.mid, self.narrow, self.final = own, acc, wide, mid, narrow, final

    def stage_share(self):
        self.go(0, self.own, self.wide, self.place.sibling())

    def wait_share(self):
        self.arrived(0, self.wide)
        self.acc[...] = self.own[...] + self.wide[...]

    def stage_first(self):
        at = self.place
        self.go(1, self.acc.at[:, 1 - at.y], self.mid, at.along_y())

    def wait_first(self):
        at = self.place
        self.arrived(1, self.mid)
        half = self.acc.at[:, at.y]
        half[...] = half[...] + self.mid[...]

    def stage_second(self):
        at = self.place
        self.go(2, self.acc.at[:, at.y, 1 - at.x], self.narrow.at[0:4], at.along_x())

    def wait_second(self):
        at = self.place
        self.arrived(2, self.narrow.at[0:4])
        part = self.acc.at[:, at.y, at.x]
        part[...] = part[...] + self.narrow[0:4]

    def block(self, shift):
        at = self.place
        return self.acc.at[at.other_z(shift), at.y, at.x]

    def stage_z(self):
        for shift in (1, 2, 3):
            self.go(2 + shift, self.block(shift), self.narrow.at[3 + shift], self.place.along_z(shift))

    def wait_z(self):
        at = self.place
        total = self.block(0)[...]
        for shift in (1, 2, 3):
            self.arrived(2 + shift, self.narrow.at[3 + shift])
            total = total + self.narrow[3 + shift]
        self.final[...] = total
        self.left(0, self.own)
        self.left(1, self.acc.at[:, 1 - at.y])
        self.left(2, self.acc.at[:, at.y, 1 - at.x])
        for shift in (1, 2, 3):
            self.left(2 + shift, self.block(shift))


def reduce_scratch(rounds, rows, d):
    return [
        pltpu.VMEM((rounds, 2, 4, 2, 2, rows, d), BF16), pltpu.VMEM((rounds, 2, 4, 2, 2, rows, d), BF16),
        pltpu.VMEM((rounds, 2, 4, 2, rows, d), BF16), pltpu.VMEM((rounds, 2, 7, rows, d), BF16),
        pltpu.SemaphoreType.DMA((rounds, 2, 7)), pltpu.SemaphoreType.DMA((rounds, 2, 7)),
        pltpu.SemaphoreType.DMA((rounds, 2)),
    ]


def reduce_round(place, grad, scratch, index, final):
    acc, wide, mid, narrow, send, recv, local = scratch
    return [
        Reduce(
            place, grad, lane, acc.at[index, lane], wide.at[index, lane], mid.at[index, lane], narrow.at[index, lane], final,
            send.at[index, lane], recv.at[index, lane], local.at[index, lane],
        )
        for lane in range(2)
    ]


def both(lanes, *names):
    for name in names:
        for lane in lanes:
            getattr(lane, name)()


def matrix(block):
    return block.reshape(-1, block.shape[-1])


def at_places(beats, step, last):
    def hook(slot):
        for when, where, beat in beats:
            if where == slot:

                @pl.when(step == min(when, last))
                def _(beat=beat):
                    beat()

    return hook


def forward_kernel(ring, count, *refs):
    refs = list(refs)

    def take(number):
        out = refs[:number]
        del refs[:number]
        return out

    tok_ref, mem_ref, doc_ref, keep_ref = take(4)
    if ring:
        shards = take(7)
        narrow_refs = take(3)
    else:
        attn_ref, w1_ref, w2_ref, vec_in_ref, b1_in_ref = take(5)
    n1_ref, qt_ref, k_ref, v_ref, e_ref, linv_ref, ot_ref, h1_ref, out_ref, res_ref, act_ref, slope_ref, vec_ref = take(13)
    if ring:
        attn_ref, w1_ref, w2_ref, wr_ref, gate_ref = take(5)
    bias_ref, pair_ref, vt_ref, hidden_ref, b1_ref, attn_v, w1_v, w2_v, wsem = take(9)
    seg = tok_ref.shape[1]
    slots = mem_ref.shape[1]
    step = pl.program_id(0)
    load_attn = lambda: pltpu.make_async_copy(attn_ref, attn_v, wsem.at[0])
    load_w1 = lambda: pltpu.make_async_copy(w1_ref, w1_v, wsem.at[1])
    load_w2 = lambda: pltpu.make_async_copy(w2_ref, w2_v, wsem.at[2])
    hook = None
    if ring:
        units, psem, sown_ref, sall_ref, send, recv, local, ssend, srecv = take(9)
        place = Place()
        views = [unit_first(attn_ref), unit_first(w1_ref), unit_last(w2_ref), unit_first(wr_ref), unit_last(gate_ref)]
        rounds = []
        for r, view in enumerate(views):
            own = (lambda u: shards[6].at[u]) if r == 4 else (lambda u, r=r: units.at[4 * r + u])
            rounds.append([Gather(place, view, own, l, send.at[r, l], recv.at[r, l], local.at[r, l]) for l in range(2)])
        small = GatherSmall(place, sall_ref, sown_ref, ssend, srecv)
        packs = [(shards[0], units.at[0:3]), (shards[1], units.at[3])]
        packs += [(shards[2].at[:, j * 512:(j + 1) * 512], units.at[4 + j]) for j in range(4)]
        packs += [(shards[3], units.at[8:12]), (shards[4], units.at[12:15]), (shards[5], units.at[15])]

        def pack(i):
            return pltpu.make_async_copy(packs[i][0], packs[i][1], psem.at[i])

        last = len(rounds) - 1

        def advance(r):
            if r > 0:
                both(rounds[r - 1], "wait_second", "stage_share")
            if r <= last:
                both(rounds[r], "wait_first", "stage_second")
            if r + 1 <= last:
                both(rounds[r + 1], "wait_z", "stage_first")
            if r + 2 <= last:
                both(rounds[r + 2], "stage_z")

        def third():
            advance(3)
            both(rounds[1], "wait_share")
            load_w1().start()

        def fourth():
            advance(4)
            both(rounds[2], "wait_share")
            load_w2().start()

        beats = [
            (0, 1, lambda: (both(rounds[1], "wait_first", "stage_second"), both(rounds[2], "wait_z", "stage_first"), both(rounds[3], "stage_z"))),
            (1, 0, lambda: advance(2)), (2, 0, third), (3, 0, fourth), (3, 1, lambda: advance(5)),
        ]
        hook = at_places(beats, step, count - 1)

    @pl.when(step < count)
    def _():
        if ring:

            @pl.when(step == 0)
            def _():
                for i in range(len(packs)):
                    pack(i).start()
                bias, gbias, gains = (ref[...].astype(F32) for ref in narrow_refs)
                narrow = jnp.concatenate([gbias, gains], 0)
                lane = lax.broadcasted_iota(jnp.int32, (4, 128), 1) // narrow.shape[1]
                narrow = jnp.where(lane == lax.rem(place.dp, 4), jnp.concatenate([narrow] * 4, 1), 0.0)
                sown_ref[...] = jnp.concatenate([bias, narrow, jnp.zeros((3, 128), F32)], 0)
                place.greet()
                small.stage_z()
                pack(0).wait()
                pack(1).wait()
                both(rounds[0], "stage_z")
                for i in range(2, len(packs)):
                    pack(i).wait()
        else:

            @pl.when(step == 0)
            def _():
                load_attn().start()
                load_w1().start()
                load_w2().start()
                vec_ref[...] = vec_in_ref[...]
                b1_ref[...] = b1_in_ref[...]
                load_attn().wait()

        keep = keep_ref[0][:, 0:1]
        docs = doc_ref[0].astype(F32)
        key_docs = jnp.broadcast_to(docs, (128, seg)).T
        slot_docs = jnp.broadcast_to(keep - 1.0, (slots, 128))
        key_docs = jnp.concatenate([slot_docs, jnp.full((128 - slots, 128), -1.0, F32), key_docs], 0)
        for block, (first, last_row) in enumerate(SPANS):
            length = last_row - first
            position = lax.broadcasted_iota(jnp.int32, (length, BLOCK), 0) + (first - 128 - block * BLOCK)
            position = position <= lax.broadcasted_iota(jnp.int32, (length, BLOCK), 1)
            same = key_docs[first:last_row] == docs[:, block * BLOCK:(block + 1) * BLOCK]
            bias_ref[STARTS[block]:STARTS[block] + length, :] = jnp.where(same & position, 0.0, -1e30)
        if ring:

            @pl.when(step == 0)
            def _():
                small.wait_z()
                small.stage_first()
                both(rounds[0], "wait_z", "stage_first")
                both(rounds[1], "stage_z")
                small.wait_first()
                small.stage_second()
                both(rounds[0], "wait_first", "stage_second")
                small.wait_second()
                for m in range(4):
                    total = sall_ref[m, 0, 0] + sall_ref[m, 0, 1] + sall_ref[m, 1, 0] + sall_ref[m, 1, 1]
                    vec_ref[:, m * 128:(m + 1) * 128] = jnp.concatenate([total[1:8], total[0:1]], 0)
                    for i in range(4):
                        b1_ref[m, :, i * 128:(i + 1) * 128] = sall_ref[m, i // 2, i % 2, 0:1, :]
                both(rounds[0], "wait_second", "stage_share")
                both(rounds[1], "wait_z", "stage_first")
                both(rounds[2], "stage_z")
                both(rounds[0], "wait_share")
                load_attn().start()
                load_attn().wait()

        x = tok_ref[0].astype(F32)
        gain_one = vec_ref[1:2, :]
        hat, _ = norm_parts(x)
        n1t = (hat * gain_one).astype(BF16)
        hat, _ = norm_parts(mem_ref[0] * keep)
        n1_ref[0, 0:slots, :] = (hat * gain_one).astype(BF16)
        n1_ref[0, slots:128, :] = jnp.zeros((128 - slots, x.shape[1]), BF16)
        n1_ref[0, 128:, :] = n1t
        qt_ref[0] = (dot_nt(matrix(attn_v[0]).T, n1t) * 0.125).astype(BF16)
        n1 = n1_ref[0]
        k_ref[0] = dot(n1, matrix(attn_v[1])).astype(BF16)
        v = dot(n1, matrix(attn_v[2])).astype(BF16)
        v_ref[0] = v
        vt_ref[...] = v.T
        pair_ref[...] = jnp.zeros_like(pair_ref)
        if hook:
            hook(0)

        def one_pair(pair, carry):
            lanes = pl.ds(pl.multiple_of(pair * 128, 128), 128)
            for block, (first, last_row) in enumerate(SPANS):
                start = STARTS[block]
                held = pair_ref.at[block]
                columns = pl.ds(block * BLOCK, BLOCK)
                diagonal_pair(held, qt_ref[0, lanes, columns])
                scores = dot(k_ref[0, first:last_row, lanes], held[...])
                bias = bias_ref[start:start + last_row - first, :]
                scores = scores + jnp.concatenate([bias, bias], 1)
                largest = jnp.max(scores, axis=0, keepdims=True)
                e = jnp.exp(scores - largest)
                linv = 1.0 / jnp.sum(e, axis=0, keepdims=True)
                e = e.astype(BF16)
                e_ref[0, pair, start:start + last_row - first, :] = e
                linv_ref[0, pair, block, :, :] = linv
                mixed = dot(vt_ref[lanes, first:last_row], e) * linv
                ot_ref[0, lanes, columns] = jnp.concatenate(
                    [mixed[0:64, 0:128], mixed[64:128, 128:256]], 0
                ).astype(BF16)
            return carry

        lax.fori_loop(0, 4, one_pair, 0)
        h1 = x + dot(ot_ref[0].T, matrix(attn_v[3]))
        h1_ref[0] = h1
        hidden_ref[step] = h1
        if hook:
            hook(1)

    @pl.when(step >= count)
    def _():
        @pl.when(step == count)
        def _():
            load_w1().wait()
            load_w2().wait()

        h1 = hidden_ref[step - count]
        hat, _ = norm_parts(h1)
        n2 = (hat * vec_ref[2:3, :]).astype(BF16)
        result = h1
        for part in range(4):
            before = dot(n2, matrix(w1_v[part])) + b1_ref[part]
            cdf = 0.5 + 0.5 * lax.erf(before * 0.7071067811865476)
            active = (before * cdf).astype(BF16)
            act_ref[0, part] = active
            slope = cdf + before * jnp.exp(before * before * -0.5) * 0.3989422804014327
            slope_ref[0, part] = slope.astype(BF16)
            result = result + dot(active, matrix(w2_v[part]))
        out_ref[0] = result.astype(BF16)
        res_ref[0] = result[seg // 2:]
        if ring:

            @pl.when(step == 2 * count - 1)
            def _():
                both(rounds[3], "wait_share")
                both(rounds[4], "wait_share")
                for lanes in rounds:
                    both(lanes, "finish")
                small.finish()


ANY = pl.BlockSpec(memory_space=pl.ANY)


def full_spec(shape):
    return pl.BlockSpec(shape, lambda i: (0,) * len(shape), pipeline_mode=pl.Buffered(1))


def phase_spec(shape, first, count):
    return pl.BlockSpec((1,) + shape, lambda i: (jnp.clip(i - first, 0, count - 1),) + (0,) * len(shape))


def call_forward(ring, tokens, memory, docs, keep, weights):
    n, seg, d = tokens.shape
    slots = memory.shape[1]
    early = [
        ((seg + 128, d), BF16), ((d, seg), BF16), ((seg + 128, d), BF16), ((seg + 128, d), BF16), ((4, LIVE, 256), BF16),
        ((4, 4, 1, 256), F32), ((d, seg), BF16), ((seg, d), F32),
    ]
    late = [((seg, d), BF16), ((seg // 2, d), F32), ((4, seg, 512), BF16), ((4, seg, 512), BF16)]
    units = (4, 4, 2, 2, 32, d)
    unit_shapes = [units, units, (4, 2, 2, 4, 32, d), units, (4, 2, 2, 4, 16, d)]
    out_shape = [jax.ShapeDtypeStruct((n,) + shape, kind) for shape, kind in early + late]
    out_shape += [jax.ShapeDtypeStruct((8, d), F32)]
    out_specs = [phase_spec(shape, 0, n) for shape, _ in early] + [phase_spec(shape, n, n) for shape, _ in late]
    out_specs += [full_spec((8, d))]
    in_specs = [phase_spec((seg, d), 0, n), phase_spec((slots, d), 0, n), phase_spec((1, seg), 0, n), phase_spec((1, 128), 0, n)]
    scratch = [
        pltpu.VMEM((LIVE, 128), F32), pltpu.VMEM((4, 128, 256), BF16), pltpu.VMEM((d, seg + 128), BF16),
        pltpu.VMEM((n, seg, d), F32), pltpu.VMEM((4, 1, d), F32), pltpu.VMEM(unit_shapes[0], BF16),
        pltpu.VMEM(unit_shapes[1], BF16), pltpu.VMEM(unit_shapes[2], BF16), pltpu.SemaphoreType.DMA((3,)),
    ]
    params = dict(vmem_limit_bytes=VMEM_LIMIT)
    if ring:
        in_specs += [ANY] * 7 + [full_spec(array.shape) for array in weights[7:]]
        out_shape += [jax.ShapeDtypeStruct(shape, BF16) for shape in unit_shapes]
        out_specs += [ANY] * 5
        scratch += [
            pltpu.VMEM((16, 32, d), BF16), pltpu.SemaphoreType.DMA((9,)), pltpu.VMEM((8, 128), F32),
            pltpu.VMEM((4, 2, 2, 8, 128), F32), pltpu.SemaphoreType.DMA((5, 2, 7)), pltpu.SemaphoreType.DMA((5, 2, 7)),
            pltpu.SemaphoreType.DMA((5, 2)), pltpu.SemaphoreType.DMA((5,)), pltpu.SemaphoreType.DMA((5,)),
        ]
        params.update(collective_id=0, has_side_effects=True)
    else:
        in_specs += [ANY] * 3 + [full_spec((8, d)), full_spec((4, 1, d))]
    return pl.pallas_call(
        functools.partial(forward_kernel, ring, n),
        grid=(2 * n,),
        out_shape=out_shape,
        in_specs=in_specs,
        out_specs=out_specs,
        scratch_shapes=scratch,
        compiler_params=pltpu.CompilerParams(**params),
        name="gather_forward" if ring else "forward_rows",
    )(tokens, memory, docs, keep, *weights)


def writer_all(
    res_ref, mem_ref, memgrad_ref, doc_ref, keep_ref, wr_ref, gate_ref, vec_ref,
    newmem_ref, dres_ref, dkept_ref, gwr_ref, ggate_ref, gvec_ref,
    n3_ref, ns_ref, kept_ref, sq_ref, tk_ref, tv_ref, p_ref, wt_ref, dsq_ref, dtk_ref, dtv_ref, dlog_ref, dw_ref,
):
    n, half, d = res_ref.shape
    slots = mem_ref.shape[1]
    gain = vec_ref[3:4, :]

    def norm(i, carry):
        rows = pl.ds(pl.multiple_of(i * half, half), half)
        small = pl.ds(pl.multiple_of(i * slots, slots), slots)
        hat, _ = norm_parts(res_ref[i])
        n3_ref[rows, :] = (hat * gain).astype(BF16)
        kept = mem_ref[i] * keep_ref[i][:, 0:1]
        kept_ref[small, :] = kept
        hat, _ = norm_parts(kept)
        ns_ref[small, :] = (hat * gain).astype(BF16)
        tk_ref[rows, :] = dot(n3_ref[rows, :], wr_ref[1]).astype(BF16)
        tv_ref[rows, :] = dot(n3_ref[rows, :], wr_ref[2]).astype(BF16)
        return carry

    lax.fori_loop(0, n, norm, 0)
    sq_ref[...] = (dot(ns_ref[...], wr_ref[0]) * 0.125).astype(BF16)
    low_half = lax.broadcasted_iota(jnp.int32, (1, 128), 1) < 64

    def halves(rows):
        zero = jnp.zeros_like(rows)
        return jnp.concatenate([jnp.where(low_half, rows, zero), jnp.where(low_half, zero, rows)], 0)

    def read(i, carry):
        rows = pl.ds(pl.multiple_of(i * half, half), half)
        small = pl.ds(pl.multiple_of(i * slots, slots), slots)
        docs = doc_ref[i].astype(F32)
        bias = jnp.where(docs == jnp.max(docs), 0.0, -1e30)[:, docs.shape[1] - half:]
        for pair in range(4):
            lanes = slice(pair * 128, pair * 128 + 128)
            scores = dot_nt(halves(sq_ref[small, lanes]), tk_ref[rows, lanes]) + bias
            e = jnp.exp(scores - jnp.max(scores, axis=1, keepdims=True))
            p = e * (1.0 / jnp.sum(e, axis=1, keepdims=True))
            p_ref[i, pair] = p
            mixed = dot(p.astype(BF16), tv_ref[rows, lanes])
            wt_ref[small, lanes] = jnp.where(low_half, mixed[:slots], mixed[slots:]).astype(BF16)
        return carry

    lax.fori_loop(0, n, read, 0)

    def put(ref, index, value):
        ref[index] = value.astype(BF16).reshape(ref.shape[1:])

    write = dot(wt_ref[...], wr_ref[3])
    kept = kept_ref[...]
    write_low = write.astype(BF16)
    kept_low = kept.astype(BF16)
    logit = dot(kept_low, gate_ref[0]) + dot(write_low, gate_ref[1]) + vec_ref[0:1, :]
    gate = jax.nn.sigmoid(logit)
    new = gate * kept + (1.0 - gate) * write
    memgrad = memgrad_ref[...].reshape(n * slots, d)
    newmem_ref[...] = new.reshape(n, slots, d)
    dlogit = memgrad * (kept - write) * gate * (1.0 - gate)
    dlog_ref[...] = dlogit.astype(BF16)
    dlow = dlog_ref[...]
    gvec_ref[0:1, :] = jnp.sum(dlow.astype(F32), axis=0, keepdims=True)
    ggate_ref[0:2] = dot_tn(kept_low, dlow).astype(BF16).reshape((2,) + ggate_ref.shape[1:])
    ggate_ref[2:4] = dot_tn(write_low, dlow).astype(BF16).reshape((2,) + ggate_ref.shape[1:])
    dkept = memgrad * gate + dot_nt(dlow, gate_ref[0])
    dwrite = memgrad * (1.0 - gate) + dot_nt(dlow, gate_ref[1])
    dkept_ref[...] = dkept.reshape(n, slots, d)
    dw_low = dwrite.astype(BF16)
    put(gwr_ref, 3, dot_tn(wt_ref[...], dw_low))
    dw_ref[...] = dot_nt(dw_low, wr_ref[3]).astype(BF16)

    def read_back(i, carry):
        rows = pl.ds(pl.multiple_of(i * half, half), half)
        small = pl.ds(pl.multiple_of(i * slots, slots), slots)
        for pair in range(4):
            lanes = slice(pair * 128, pair * 128 + 128)
            p = p_ref[i, pair]
            grads = halves(dw_ref[small, lanes])
            dp = dot_nt(grads, tv_ref[rows, lanes])
            ds = (p * (dp - jnp.sum(dp * p, axis=1, keepdims=True))).astype(BF16)
            dq = dot(ds, tk_ref[rows, lanes]) * 0.125
            dsq_ref[small, lanes] = jnp.where(low_half, dq[:slots], dq[slots:]).astype(BF16)
            dtk_ref[rows, lanes] = dot_tn(ds, halves(sq_ref[small, lanes])).astype(BF16)
            dtv_ref[rows, lanes] = dot_tn(p.astype(BF16), grads).astype(BF16)
        return carry

    lax.fori_loop(0, n, read_back, 0)
    put(gwr_ref, 0, dot_tn(ns_ref[...], dsq_ref[...]))
    put(gwr_ref, 1, dot_tn(n3_ref[...], dtk_ref[...]))
    put(gwr_ref, 2, dot_tn(n3_ref[...], dtv_ref[...]))
    grad = dot_nt(dsq_ref[...], wr_ref[0])
    hat, rstd = norm_parts(kept_ref[...])
    dkept_ref[...] += norm_back(grad, hat, rstd, gain).reshape(n, slots, d)
    ggain = jnp.sum(grad * hat, axis=0, keepdims=True)

    def back(i, ggain):
        rows = pl.ds(pl.multiple_of(i * half, half), half)
        grad = dot_nt(dtk_ref[rows, :], wr_ref[1]) + dot_nt(dtv_ref[rows, :], wr_ref[2])
        hat, rstd = norm_parts(res_ref[i])
        dres_ref[i] = norm_back(grad, hat, rstd, gain)
        return ggain + jnp.sum(grad * hat, axis=0, keepdims=True)

    gvec_ref[3:4, :] = lax.fori_loop(0, n, back, ggain)


def ffn_back_kernel(ring, count, *refs):
    refs = list(refs)

    def take(number):
        out = refs[:number]
        del refs[:number]
        return out

    writer_in = take(8)
    vec_ref = writer_in[7]
    og_ref, h1_ref, act_ref, slope_ref, w1_ref, w2_ref = take(6)
    newmem_ref, dkept_ref, gvec_ref, gb_ref, gw1_ref, gw2_ref, dh_ref, gwr_out, ggate_out = take(9)
    writer_scratch = take(13)
    dres_ref, acc1_ref, acc2_ref, w1_v, w2_v, wsem = take(6)
    step = pl.program_id(0)
    seg = og_ref.shape[1]
    load_w1 = lambda: pltpu.make_async_copy(w1_ref, w1_v, wsem.at[0])
    load_w2 = lambda: pltpu.make_async_copy(w2_ref, w2_v, wsem.at[1])
    hook = None
    if ring:
        gwr_ref, ggate_ref, fwr_ref, fgate_ref = take(4)
        wide_scratch, slim_scratch = take(7), take(7)
        place = Place()
        writer_round = reduce_round(place, unit_first(gwr_ref), wide_scratch, 0, fwr_ref)
        gate_round = reduce_round(place, unit_last(ggate_ref), slim_scratch, 0, fgate_ref)

        def hand_back():
            both(writer_round, "wait_final")
            both(gate_round, "wait_final")
            gwr_out[...] = fwr_ref[...]
            ggate_out[...] = fgate_ref[...]

        beats = [
            (0, 0, lambda: both(writer_round, "wait_share", "stage_first")),
            (0, 1, lambda: both(gate_round, "wait_share", "stage_first")),
            (1, 0, lambda: (both(writer_round, "wait_first", "stage_second"), both(gate_round, "wait_first", "stage_second"))),
            (1, 1, lambda: both(writer_round, "wait_second", "stage_z")),
            (2, 0, lambda: both(gate_round, "wait_second", "stage_z")),
            (2, 1, lambda: both(writer_round, "wait_z", "stage_final")),
            (3, 0, lambda: both(gate_round, "wait_z", "stage_final")),
            (3, 1, hand_back),
        ]
        hook = at_places(beats, step - 1, count - 1)
    else:
        gwr_ref, ggate_ref = gwr_out, ggate_out

    @pl.when(step == 0)
    def _():
        load_w1().start()
        load_w2().start()
        if ring:
            place.greet()
        acc1_ref[...] = jnp.zeros_like(acc1_ref)
        acc2_ref[...] = jnp.zeros_like(acc2_ref)
        gb_ref[...] = jnp.zeros_like(gb_ref)
        gvec_ref[...] = jnp.zeros_like(gvec_ref)
        writer_all(*writer_in, newmem_ref, dres_ref, dkept_ref, gwr_ref, ggate_ref, gvec_ref, *writer_scratch)
        if ring:
            both(writer_round, "stage_share")
            both(gate_round, "stage_share")
        load_w1().wait()
        load_w2().wait()

    @pl.when(step > 0)
    def _():
        if hook:
            hook(0)
        top = og_ref[0, 0:seg // 2, :].astype(F32)
        bottom = og_ref[0, seg // 2:, :].astype(F32) + dres_ref[step - 1]
        dresult = jnp.concatenate([top, bottom], 0)
        low = dresult.astype(BF16)
        h1 = h1_ref[0]
        hat, rstd = norm_parts(h1)
        gain = vec_ref[2:3, :]
        n2t = (hat * gain).astype(BF16).T
        lowt = low.T
        grad = jnp.zeros_like(dresult)
        for part in range(4):
            acc2_ref[part] += dot(lowt, act_ref[0, part])
            dbefore = (dot_nt(low, w2_v[part]) * slope_ref[0, part].astype(F32)).astype(BF16)
            gb_ref[part] += jnp.sum(dbefore.astype(F32), axis=0, keepdims=True)
            acc1_ref[part] += dot(n2t, dbefore)
            grad = grad + dot_nt(dbefore, w1_v[part])
            if part == 1 and hook:
                hook(1)
        gvec_ref[2:3, :] += jnp.sum(grad * hat, axis=0, keepdims=True)
        dh_ref[0] = dresult + norm_back(grad, hat, rstd, gain)

        @pl.when(step == count)
        def _():
            gw1_ref[...] = acc1_ref[...].astype(BF16)
            for part in range(4):
                gw2_ref[part] = acc2_ref[part].T.astype(BF16)


def call_ffn_back(ring, res, memory, memory_grad, docs, keep, wr, gate, vec, out_grad, h1, act, slope, w1, w2):
    n, half, d = res.shape
    seg = 2 * half
    slots = memory.shape[1]
    rows, small = n * half, n * slots
    writer_args = (res, memory, memory_grad, docs, keep, wr, gate, vec)
    units = (4, 4, 2, 2, 32, d)
    gate_units = (4, 2, 2, 4, 16, d)
    if ring:
        grads = [((4, 32, d), F32), ((4, 16, d), F32)]
    else:
        grads = [(units, BF16), (gate_units, BF16)]
    whole = [
        ((n, slots, d), F32), ((n, slots, d), F32), ((8, d), F32), ((4, 1, d), F32), ((4, d, d), BF16), ((4, d, d), BF16),
    ]
    scratch = [
        pltpu.VMEM((rows, d), BF16), pltpu.VMEM((small, d), BF16), pltpu.VMEM((small, d), F32), pltpu.VMEM((small, d), BF16),
        pltpu.VMEM((rows, d), BF16), pltpu.VMEM((rows, d), BF16), pltpu.VMEM((n, 4, 2 * slots, half), F32),
        pltpu.VMEM((small, d), BF16), pltpu.VMEM((small, d), BF16), pltpu.VMEM((rows, d), BF16),
        pltpu.VMEM((rows, d), BF16), pltpu.VMEM((small, d), BF16), pltpu.VMEM((small, d), BF16),
        pltpu.VMEM((n, half, d), F32), pltpu.VMEM((4, d, d), F32), pltpu.VMEM((4, d, d), F32),
        pltpu.VMEM((4, d, d), BF16), pltpu.VMEM((4, d, d), BF16), pltpu.SemaphoreType.DMA((2,)),
    ]
    params = dict(vmem_limit_bytes=VMEM_LIMIT)
    if ring:
        scratch += [pltpu.VMEM(units, BF16), pltpu.VMEM(gate_units, BF16)]
        scratch += [pltpu.VMEM((4, 32, d), F32), pltpu.VMEM((4, 16, d), F32)]
        scratch += reduce_scratch(1, 32, d) + reduce_scratch(1, 16, d)
        params.update(collective_id=1, has_side_effects=True)
    return pl.pallas_call(
        functools.partial(ffn_back_kernel, ring, n),
        grid=(n + 1,),
        out_shape=[jax.ShapeDtypeStruct(shape, kind) for shape, kind in whole]
        + [jax.ShapeDtypeStruct((n, seg, d), F32)] + [jax.ShapeDtypeStruct(shape, kind) for shape, kind in grads],
        in_specs=[full_spec(array.shape) for array in writer_args] + [
            phase_spec((seg, d), 1, n), phase_spec((seg, d), 1, n), phase_spec((4, seg, 512), 1, n),
            phase_spec((4, seg, 512), 1, n), ANY, ANY,
        ],
        out_specs=[full_spec(shape) for shape, _ in whole] + [phase_spec((seg, d), 1, n)]
        + [full_spec(shape) for shape, _ in grads],
        scratch_shapes=scratch,
        compiler_params=pltpu.CompilerParams(**params),
        name="ffn_back",
    )(*writer_args, out_grad, h1, act, slope, w1, w2)


def attn_back_kernel(ring, count, *refs):
    refs = list(refs)

    def take(number):
        out = refs[:number]
        del refs[:number]
        return out

    n1_ref, qt_ref, k_ref, v_ref, e_ref, linv_ref, ot_ref = take(7)
    tok_ref, mem_ref, keep_ref, dkept_ref, dh_ref = take(5)
    attn_ref, vec_ref, gvec_in_ref = take(3)
    if ring:
        gb_ref, gw1_ref, gw2_ref = take(3)
    gtok_ref, gmem_ref = take(2)
    if ring:
        fattn_ref, fw1_ref, fw2_ref, fsmall_ref = take(4)
    else:
        gattn_ref, gvec_ref = take(2)
    dot_ref, kt_ref, dqt_ref, dk_ref, dv_ref, dkl_ref, dvl_ref, qp_ref, dp_ref, acc_ref, accg_ref = take(11)
    step = pl.program_id(0)
    seg = tok_ref.shape[1]
    slots = mem_ref.shape[1]
    hook = late_hook = None
    if ring:
        gattn_ref, final_ref = take(2)
        scratch = take(7)
        sown, sacc, swide, smid, snarrow, ssend, srecv = take(7)
        place = Place()
        attn_round = reduce_round(place, unit_first(gattn_ref), scratch, 0, final_ref.at[0])
        w1_round = reduce_round(place, unit_first(gw1_ref), scratch, 1, final_ref.at[1])
        w2_round = reduce_round(place, unit_last(gw2_ref), scratch, 2, final_ref.at[2])
        small = ReduceSmall(place, sown, sacc, swide, smid, snarrow, fsmall_ref, ssend, srecv)
        beats = [
            (0, 0, lambda: both(w2_round, "wait_share", "stage_first")),
            (0, 1, lambda: (both(w2_round, "wait_first", "stage_second"), both(w1_round, "wait_share", "stage_first"))),
            (1, 1, lambda: (both(w2_round, "wait_second", "stage_z"), both(w1_round, "wait_first", "stage_second"))),
            (2, 1, lambda: (both(w2_round, "wait_z", "stage_final"), both(w1_round, "wait_second", "stage_z"))),
            (3, 0, lambda: both(w1_round, "wait_z", "stage_final")),
            (3, 1, lambda: (both(w2_round, "wait_final"), both(w1_round, "wait_final"))),
        ]
        hook = at_places(beats, step, count - 1)
        late_beats = [
            (0, 0, lambda: both(attn_round, "wait_share", "stage_first")),
            (2, 0, lambda: both(attn_round, "wait_first", "stage_second")),
            (3, 0, lambda: both(attn_round, "wait_second", "stage_z")),
        ]
        late_hook = at_places(late_beats, step - count, count - 1)

    @pl.when(step < count)
    def _():
        @pl.when(step == 0)
        def _():
            if ring:
                place.greet()
                both(w2_round, "stage_share")
                both(w1_round, "stage_share")
            acc_ref[...] = jnp.zeros_like(acc_ref)
            accg_ref[...] = jnp.zeros_like(accg_ref)

        low = dh_ref[0].astype(BF16)
        acc_ref[3] += dot(ot_ref[0], low)
        dot_ref[...] = dot_nt(attn_ref[3], low)
        kt_ref[...] = k_ref[0].T
        qp_ref[...] = jnp.zeros_like(qp_ref)
        dp_ref[...] = jnp.zeros_like(dp_ref)
        if hook:
            hook(0)

        def one_pair(pair, carry):
            lanes = pl.ds(pl.multiple_of(pair * 128, 128), 128)
            dk_ref[:, lanes] = jnp.zeros((seg + 128, 128), F32)
            dv_ref[:, lanes] = jnp.zeros((seg + 128, 128), F32)
            for block, (first, last) in enumerate(SPANS):
                start = STARTS[block]
                columns = pl.ds(block * BLOCK, BLOCK)
                linv = linv_ref[0, pair, block, :, :]
                mixed_grad = dot_ref[lanes, columns]
                top = (mixed_grad[0:64] * linv[:, 0:128]).astype(BF16)
                bottom = (mixed_grad[64:128] * linv[:, 128:256]).astype(BF16)
                mixed = ot_ref[0, lanes, columns].astype(F32)
                delta = jnp.concatenate(
                    [
                        jnp.sum(top.astype(F32) * mixed[0:64], axis=0, keepdims=True),
                        jnp.sum(bottom.astype(F32) * mixed[64:128], axis=0, keepdims=True),
                    ],
                    1,
                )
                held = dp_ref.at[block]
                held[0:64, 0:128] = top
                held[64:128, 128:256] = bottom
                query = qp_ref.at[block]
                diagonal_pair(query, qt_ref[0, lanes, columns])
                e = e_ref[0, pair, start:start + last - first, :]
                dp = dot(v_ref[0, first:last, lanes], held[...])
                ds = (e.astype(F32) * (dp - delta)).astype(BF16)
                dv_ref[first:last, lanes] += dot_nt(e, held[...])
                dk_ref[first:last, lanes] += dot_nt(ds, query[...])
                dq = dot(kt_ref[lanes, first:last], ds) * 0.125
                dqt_ref[step, lanes, columns] = jnp.concatenate([dq[0:64, 0:128], dq[64:128, 128:256]], 0).astype(BF16)
            return carry

        lax.fori_loop(0, 4, one_pair, 0)
        n1t = n1_ref[0].T
        dk = dk_ref[...].astype(BF16)
        dv = dv_ref[...].astype(BF16)
        dkl_ref[step] = dk
        dvl_ref[step] = dv
        acc_ref[0] += dot_nt(n1t[:, 128:], dqt_ref[step])
        acc_ref[1] += dot(n1t, dk)
        acc_ref[2] += dot(n1t, dv)
        if hook:
            hook(1)

        @pl.when(step == count - 1)
        def _():
            gattn_ref[...] = acc_ref[...].astype(BF16).reshape(gattn_ref.shape)
            if ring:
                both(attn_round, "stage_share")

    @pl.when(step >= count)
    def _():
        here = step - count
        gain = vec_ref[1:2, :]
        dk = dkl_ref[here]
        dv = dvl_ref[here]
        grad = dot_nt(dk, attn_ref[1]) + dot_nt(dv, attn_ref[2])
        slot_grad = grad[0:slots]
        kept = mem_ref[0] * keep_ref[0][:, 0:1]
        hat, rstd = norm_parts(kept)
        ggain = jnp.sum(slot_grad * hat, axis=0, keepdims=True)
        gmem_ref[0] = (dkept_ref[0] + norm_back(slot_grad, hat, rstd, gain)) * keep_ref[0][:, 0:1]
        grad = grad[128:] + dot_nt(dqt_ref[here].T, attn_ref[0])
        hat, rstd = norm_parts(tok_ref[0].astype(F32))
        accg_ref[...] += ggain + jnp.sum(grad * hat, axis=0, keepdims=True)
        gtok_ref[0] = dh_ref[0] + norm_back(grad, hat, rstd, gain)
        if late_hook:
            late_hook(0)

        @pl.when(step == 2 * count - 1)
        def _():
            if not ring:
                gvec_ref[...] = gvec_in_ref[...]
                gvec_ref[1:2, :] = accg_ref[...]
                return
            vector = gvec_in_ref[...]
            vector = jnp.concatenate([vector[0:1], accg_ref[...], vector[2:4], jnp.zeros((3, vector.shape[1]), F32)], 0)
            for m in range(4):
                for i in range(4):
                    sown[m, i // 2, i % 2] = jnp.concatenate(
                        [gb_ref[m, :, i * 128:(i + 1) * 128], vector[:, m * 128:(m + 1) * 128]], 0
                    )
            small.stage_share()
            small.wait_share()
            small.stage_first()
            both(attn_round, "wait_z", "stage_final")
            small.wait_first()
            small.stage_second()
            small.wait_second()
            small.stage_z()
            both(attn_round, "wait_final")
            fattn_ref[...] = final_ref[0]
            fw1_ref[...] = final_ref[1]
            fw2_ref[...] = final_ref[2]
            small.wait_z()


def call_attn_back(ring, dh, tokens, memory, keep, n1, qt, k, v, e, linv, ot, dkept, attn, vec, gvec, extra):
    n, seg, d = tokens.shape
    slots = memory.shape[1]
    shapes = [((n, seg, d), F32), ((n, slots, d), F32)]
    out_specs = [phase_spec((seg, d), n, n), phase_spec((slots, d), n, n)]
    in_specs = [
        phase_spec((seg + 128, d), 0, n), phase_spec((d, seg), 0, n), phase_spec((seg + 128, d), 0, n),
        phase_spec((seg + 128, d), 0, n), phase_spec((4, LIVE, 256), 0, n), phase_spec((4, 4, 1, 256), 0, n),
        phase_spec((d, seg), 0, n), phase_spec((seg, d), n, n), phase_spec((slots, d), n, n), phase_spec((1, 128), n, n),
        phase_spec((slots, d), n, n), pl.BlockSpec((1, seg, d), lambda i: (lax.rem(i, n), 0, 0)),
        full_spec(attn.shape), full_spec(vec.shape), full_spec(gvec.shape),
    ]
    units = (4, 4, 2, 2, 32, d)
    scratch = [
        pltpu.VMEM((d, seg), F32), pltpu.VMEM((d, seg + 128), BF16), pltpu.VMEM((n, d, seg), BF16),
        pltpu.VMEM((seg + 128, d), F32), pltpu.VMEM((seg + 128, d), F32), pltpu.VMEM((n, seg + 128, d), BF16),
        pltpu.VMEM((n, seg + 128, d), BF16), pltpu.VMEM((4, 128, 256), BF16), pltpu.VMEM((4, 128, 256), BF16),
        pltpu.VMEM((4, d, d), F32), pltpu.VMEM((1, d), F32),
    ]
    params = dict(vmem_limit_bytes=VMEM_LIMIT)
    if ring:
        in_specs += [full_spec(extra[0].shape), ANY, ANY]
        more = [((4, 32, d), F32)] * 3 + [((8, 128), F32)]
        scratch += [pltpu.VMEM(units, BF16), pltpu.VMEM((3, 4, 32, d), F32)] + reduce_scratch(3, 32, d)
        scratch += [pltpu.VMEM((4, 2, 2, 8, 128), F32)] * 3 + [
            pltpu.VMEM((4, 2, 8, 128), F32), pltpu.VMEM((7, 8, 128), F32),
            pltpu.SemaphoreType.DMA((6,)), pltpu.SemaphoreType.DMA((6,)),
        ]
        params.update(collective_id=2, has_side_effects=True)
    else:
        more = [(units, BF16), ((8, d), F32)]
    return pl.pallas_call(
        functools.partial(attn_back_kernel, ring, n),
        grid=(2 * n,),
        out_shape=[jax.ShapeDtypeStruct(shape, kind) for shape, kind in shapes + more],
        in_specs=in_specs,
        out_specs=out_specs + [full_spec(shape) for shape, _ in more],
        scratch_shapes=scratch,
        compiler_params=pltpu.CompilerParams(**params),
        name="attn_back",
    )(n1, qt, k, v, e, linv, ot, tokens, memory, keep, dkept, dh, attn, vec, gvec, *extra)


def hand_out_kernel(
    fattn_ref, fw1_ref, fw2_ref, fwr_ref, fgate_ref, small_ref,
    gqkv_ref, gout_ref, gin_ref, gffn_ref, gwqkv_ref, gwout_ref, ggate_ref, gb_ref, ggb_ref, ggain_ref,
):
    gqkv_ref[...] = fattn_ref[0:3]
    gout_ref[...] = fattn_ref[3]
    for j in range(4):
        gin_ref[:, j * 512:(j + 1) * 512] = fw1_ref[j]
    gffn_ref[...] = fw2_ref[...]
    gwqkv_ref[...] = fwr_ref[0:3]
    gwout_ref[...] = fwr_ref[3]
    ggate_ref[...] = fgate_ref[...]
    gb_ref[...] = small_ref[0:1, :]
    rows = ggb_ref.shape[1]
    place = lax.rem(lax.axis_index("dp"), 4)
    narrow = jnp.zeros((4, rows), F32)
    for i in range(4):
        narrow = narrow + small_ref[1:5, i * rows:(i + 1) * rows] * (place == i).astype(F32)
    ggb_ref[...] = narrow[0:1]
    ggain_ref[...] = narrow[1:4]


def call_hand_out(*args):
    rows, d = args[0].shape[1:]
    vmem = pl.BlockSpec(memory_space=pltpu.VMEM)
    shapes = [
        (3, rows, d), (rows, d), (rows, 4 * d), (4, rows, d), (3, rows, d), (rows, d), (4, rows // 2, d), (1, 128), (1, rows),
        (3, rows),
    ]
    return pl.pallas_call(
        hand_out_kernel,
        out_shape=[jax.ShapeDtypeStruct(shape, F32) for shape in shapes],
        in_specs=[vmem] * 6,
        out_specs=[vmem] * 10,
        name="hand_out",
    )(*args)


def plain_weights(attn_qkv, attn_out, ffn_in, ffn_out, writer_qkv, writer_out, gate_weight, ffn_bias, gate_bias, gains):
    rows, d = attn_out.shape
    packed = jnp.concatenate(
        [
            attn_qkv, attn_out[None], ffn_in.reshape(rows, 4, d).transpose(1, 0, 2), ffn_out.reshape(4, rows, d),
            writer_qkv, writer_out[None], gate_weight.reshape(2, rows, d),
        ],
        0,
    )
    packed = lax.all_gather(packed, "dp", axis=0)
    n = packed.shape[0]

    def by_rows(first, last):
        return packed[:, first:last].transpose(1, 0, 2, 3).reshape(last - first, n * rows, d)

    small = jnp.concatenate([ffn_bias.reshape(4, rows), gate_bias[None], gains], 0).astype(F32)
    small = lax.all_gather(small, "dp", axis=0)
    b1 = small[:, 0:4].reshape(4, 1, d)
    vec = small.transpose(1, 0, 2).reshape(8, d)
    vec = jnp.concatenate([vec[4:8], jnp.zeros((4, d), F32)], 0)
    w2 = packed[:, 8:12].reshape(4, d, d)
    return by_rows(0, 4), by_rows(4, 8), w2, by_rows(12, 16), packed[:, 16:18].reshape(2, d, d), vec, b1


def plain_grads(rows, gattn, gw1, gw2, gwr, ggate, gb, gvec):
    d = gattn.shape[-1]
    n = d // rows

    def by_rows(grad):
        return grad.reshape(-1, n, rows, d).transpose(1, 0, 2, 3)

    packed = jnp.concatenate(
        [by_rows(gattn), by_rows(gw1), gw2.reshape(n, 4, rows, d), by_rows(gwr), ggate.reshape(n, 2, rows, d)], 1
    )
    owned = lax.psum_scatter(packed.astype(F32), "dp", scatter_dimension=0, tiled=False)
    owned = lax.psum(owned.astype(BF16), "outer").astype(F32)
    vectors = gvec[0:4].reshape(4, n, rows).transpose(1, 0, 2).reshape(n, 4 * rows)
    small = jnp.concatenate([gb.reshape(n, 4 * rows), vectors], 1)
    small = lax.psum(lax.psum_scatter(small, "dp", scatter_dimension=0, tiled=False), "outer")
    return (
        owned[0:3], owned[3], owned[4:8].transpose(1, 0, 2).reshape(rows, 4 * d), owned[8:12].reshape(4 * rows, d),
        owned[12:15], owned[15], owned[16:18].reshape(2 * rows, d),
        small[0:4 * rows], small[4 * rows:5 * rows], small[5 * rows:].reshape(3, rows),
    )


def body(
    tokens, memory, doc_ids, resets, out_grad, memory_grad,
    attn_qkv, attn_out, ffn_in, ffn_bias, ffn_out, writer_qkv, writer_out, gate_weight, gate_bias, gains,
):
    micro, segs, seg, d = tokens.shape
    slots = memory.shape[2]
    rows = attn_out.shape[0]
    n = micro * segs
    ring = lax.axis_size("dp") == 16 and lax.axis_size("outer") == 2 and rows == 32
    tokens, out_grad = tokens.reshape(n, seg, d), out_grad.reshape(n, seg, d)
    memory, memory_grad = memory.reshape(n, slots, d), memory_grad.reshape(n, slots, d)
    docs = doc_ids.reshape(n, 1, seg)
    keep = jnp.broadcast_to((1 - resets).astype(F32).reshape(n, 1, 1), (n, 1, 128))
    if ring:
        weights = (
            attn_qkv, attn_out, ffn_in, ffn_out.reshape(4, rows, d), writer_qkv, writer_out,
            gate_weight.reshape(4, rows // 2, d), ffn_bias.reshape(1, 4 * rows), gate_bias.reshape(1, rows), gains,
        )
    else:
        attn, w1, w2, wr, gate, vec, b1 = plain_weights(
            attn_qkv, attn_out, ffn_in, ffn_out, writer_qkv, writer_out, gate_weight, ffn_bias, gate_bias, gains
        )
        units = (4, 4, 2, 2, 32, d)
        weights = (attn.reshape(units), w1.reshape(units), w2.reshape(4, 2, 2, 4, 32, d), vec, b1)
    n1, qt, k, v, e, linv, ot, h1, out, res, act, slope, vec, *whole = call_forward(ring, tokens, memory, docs, keep, weights)
    if ring:
        attn, w1, w2, wr = (array.reshape(4, d, d) for array in whole[:4])
        gate = whole[4].reshape(2, d, d)
    new_memory, dkept, gvec, gb, gw1, gw2, dh, gwr, ggate = call_ffn_back(
        ring, res, memory, memory_grad, docs, keep, wr, gate, vec, out_grad, h1, act, slope, w1, w2
    )
    extra = (gb, gw1.reshape(4, 4, 2, 2, 32, d), gw2.reshape(4, 2, 2, 4, 32, d)) if ring else ()
    grad_tokens, grad_memory, *rest = call_attn_back(
        ring, dh, tokens, memory, keep, n1, qt, k, v, e, linv, ot, dkept, attn, vec, gvec, extra
    )
    if ring:
        fattn, fw1, fw2, small = rest
        grads = call_hand_out(fattn, fw1, fw2, gwr, ggate, small)
    else:
        gattn, gvec = rest
        grads = plain_grads(rows, gattn.reshape(4, d, d), gw1, gw2, gwr, ggate, gb, gvec)
    gqkv, gout, gin, gffn, gwqkv, gwout, ggw, gb, ggb, ggains = grads
    return (
        out.reshape(micro, segs, seg, d), new_memory.reshape(micro, segs, slots, d),
        grad_tokens.reshape(micro, segs, seg, d), grad_memory.reshape(micro, segs, slots, d),
        gqkv, gout, gin, gb.reshape(4 * rows), gffn.reshape(4 * rows, d), gwqkv, gwout, ggw.reshape(2 * rows, d),
        ggb.reshape(rows), ggains,
    )


def solution(mesh):
    split = ("dp", "outer")
    whole = P(None, split, None, None)
    weights = (
        P(None, "dp", None), P("dp", None), P("dp", None), P("dp"), P("dp", None), P(None, "dp", None),
        P("dp", None), P("dp", None), P("dp"), P(None, "dp"),
    )
    return jax.shard_map(
        body,
        mesh=mesh,
        in_specs=(whole, whole, P(None, split, None), P(None, split), whole, whole) + weights,
        out_specs=(whole, whole, whole, whole) + weights,
        check_vma=False,
    )
```

```python
import functools

import jax
import jax.numpy as jnp
from jax import lax
from jax.experimental import pallas as pl
from jax.experimental.pallas import tpu as pltpu
from jax.sharding import PartitionSpec as P

HEADS = 8
BLOCK = 128
SPANS = ((0, 256), (0, 384), (128, 512), (256, 640))
STARTS = (0, 256, 640, 1024)
LIVE = 1408
F32 = jnp.float32
BF16 = jnp.bfloat16
VMEM_LIMIT = 60 * 1024 * 1024


def dot(a, b):
    return jnp.dot(a, b, preferred_element_type=F32)


def dot_nt(a, b):
    return lax.dot_general(a, b, (((1,), (1,)), ((), ())), preferred_element_type=F32)


def dot_tn(a, b):
    return lax.dot_general(a, b, (((0,), (0,)), ((), ())), preferred_element_type=F32)


def norm_parts(rows):
    centred = rows - jnp.mean(rows, axis=-1, keepdims=True)
    rstd = lax.rsqrt(jnp.mean(centred * centred, axis=-1, keepdims=True) + 1e-05)
    return centred * rstd, rstd


def norm_back(grad, hat, rstd, gain):
    scaled = grad * gain
    return rstd * (
        scaled
        - jnp.mean(scaled, axis=-1, keepdims=True)
        - hat * jnp.mean(scaled * hat, axis=-1, keepdims=True)
    )


def diagonal_pair(ref, top):
    ref[0:64, 0:128] = top[0:64]
    ref[64:128, 128:256] = top[64:128]


MESH = pl.DeviceIdType.MESH
EVERY = slice(None)


class Place:
    def __init__(self):
        self.dp = lax.axis_index("dp")
        self.core = lax.axis_index("outer")
        self.z, self.y, self.x = self.dp // 4, (self.dp // 2) % 2, self.dp % 2

    def sibling(self):
        return (self.dp, 1 - self.core)

    def along_x(self):
        return (self.dp + 1 - 2 * self.x, self.core)

    def along_y(self):
        return (self.dp + 2 - 4 * self.y, self.core)

    def other_z(self, shift):
        return lax.rem(self.z + shift, 4)

    def along_z(self, shift):
        return (self.dp + 4 * (self.other_z(shift) - self.z), self.core)

    def greet(self):
        barrier = pltpu.get_barrier_semaphore()
        everyone = [self.sibling(), self.along_x(), self.along_y()] + [self.along_z(shift) for shift in (1, 2, 3)]
        for device in everyone:
            pl.semaphore_signal(barrier, inc=1, device_id=device, device_id_type=MESH)
        pl.semaphore_wait(barrier, len(everyone))


class Travel:
    def __init__(self, place, send, recv):
        self.place, self.send, self.recv = place, send, recv

    def copy(self, stage, src, dst, device):
        return pltpu.make_async_remote_copy(
            src_ref=src, dst_ref=dst, send_sem=self.send.at[stage], recv_sem=self.recv.at[stage], device_id=device,
            device_id_type=MESH,
        )

    def go(self, stage, src, dst, device):
        self.copy(stage, src, dst, device).start()

    def arrived(self, stage, dst):
        self.copy(stage, dst, dst, self.place.sibling()).wait_recv()

    def left(self, stage, src):
        self.copy(stage, src, src, self.place.sibling()).wait_send()


class Gather(Travel):
    def __init__(self, place, view, own, lane, send, recv, local):
        super().__init__(place, send, recv)
        self.view, self.own, self.lane, self.local = view, own, lane, local
        self.unit = 2 * place.core + lane

    def mine(self):
        at = self.place
        return self.view(self.unit, at.z, at.y, at.x)

    def stage_z(self):
        at = self.place
        pltpu.make_async_copy(self.own(self.unit), self.mine(), self.local).start()
        for shift in (1, 2, 3):
            self.go(shift - 1, self.own(self.unit), self.mine(), at.along_z(shift))

    def wait_z(self):
        at = self.place
        pltpu.make_async_copy(self.own(self.unit), self.mine(), self.local).wait()
        for shift in (1, 2, 3):
            self.arrived(shift - 1, self.view(self.unit, at.other_z(4 - shift), at.y, at.x))

    def column(self, far):
        at = self.place
        if self.lane:
            return self.view(self.unit, EVERY, 1 - at.y if far else at.y, at.x)
        return self.view(self.unit, EVERY, at.y, 1 - at.x if far else at.x)

    def half(self, unit, far):
        at = self.place
        if self.lane:
            return self.view(unit, EVERY, EVERY, 1 - at.x if far else at.x)
        return self.view(unit, EVERY, 1 - at.y if far else at.y, EVERY)

    def stage_first(self):
        part = self.column(False)
        self.go(3, part, part, self.place.along_y() if self.lane else self.place.along_x())

    def wait_first(self):
        self.arrived(3, self.column(True))

    def stage_second(self):
        part = self.half(self.unit, False)
        self.go(4, part, part, self.place.along_x() if self.lane else self.place.along_y())
        self.go(5, part, part, self.place.sibling())

    def wait_second(self):
        self.arrived(4, self.half(self.unit, True))

    def stage_share(self):
        part = self.half(self.unit, True)
        self.go(6, part, part, self.place.sibling())

    def wait_share(self):
        other = 2 * (1 - self.place.core) + self.lane
        self.arrived(5, self.half(other, False))
        self.arrived(6, self.half(other, True))

    def finish(self):
        for stage in range(3):
            self.left(stage, self.own(self.unit))
        self.left(3, self.column(False))
        self.left(4, self.half(self.unit, False))
        self.left(5, self.half(self.unit, False))
        self.left(6, self.half(self.unit, True))


class FirstGather(Travel):
    SHIFTS = (0, 3, 1, 2)

    def __init__(self, place, view, own, lane, send, recv, local):
        super().__init__(place, send, recv)
        self.view, self.own, self.lane, self.local = view, own, lane, local
        self.unit = 2 * place.core + lane

    def part(self, unit, z, far_first, far_second):
        at = self.place
        far_x, far_y = (far_second, far_first) if self.lane else (far_first, far_second)
        return self.view(unit, z, 1 - at.y if far_y else at.y, 1 - at.x if far_x else at.x)

    def block(self, shift, far_first, far_second):
        return self.part(self.unit, self.place.other_z(4 - shift), far_first, far_second)

    def first_partner(self):
        return self.place.along_y() if self.lane else self.place.along_x()

    def second_partner(self):
        return self.place.along_x() if self.lane else self.place.along_y()

    def keep(self):
        return pltpu.make_async_copy(self.own(self.unit), self.block(0, False, False), self.local)

    def begin(self):
        mine = self.own(self.unit)
        there = self.block(0, False, False)
        for shift in (3, 1, 2):
            self.go(shift - 1, mine, there, self.place.along_z(shift))
        self.go(4, mine, there, self.first_partner())
        self.go(8, mine, there, self.second_partner())
        self.keep().start()

    def column_block(self, shift):
        here = self.block(shift, False, False)
        self.arrived(shift - 1, here)
        self.go(4 + shift, here, here, self.first_partner())
        self.go(8 + shift, here, here, self.second_partner())

    def column_done(self):
        self.keep().wait()
        self.share(0, False, False)

    def share(self, index, far_first, far_second):
        part = self.part(self.unit, EVERY, far_first, far_second)
        self.go(16 + index, part, part, self.place.sibling())

    def far_block(self, shift):
        here = self.block(shift, True, False)
        self.arrived(4 + shift, here)
        self.go(12 + shift, here, here, self.second_partner())

    def far_done(self):
        self.share(1, True, False)
        for shift in self.SHIFTS:
            self.arrived(8 + shift, self.block(shift, False, True))
        self.share(2, False, True)

    def rest(self):
        for shift in self.SHIFTS:
            self.arrived(12 + shift, self.block(shift, True, True))
        self.share(3, True, True)

    def done(self):
        other = 2 * (1 - self.place.core) + self.lane
        for index, (far_first, far_second) in enumerate(((False, False), (True, False), (False, True), (True, True))):
            self.arrived(16 + index, self.part(other, EVERY, far_first, far_second))

    def finish(self):
        for stage in range(3):
            self.left(stage, self.own(self.unit))
        for leg in (4, 8):
            self.left(leg, self.own(self.unit))
            for shift in (1, 2, 3):
                self.left(leg + shift, self.block(shift, False, False))
        for shift in range(4):
            self.left(12 + shift, self.block(shift, True, False))
        for index, (far_first, far_second) in enumerate(((False, False), (True, False), (False, True), (True, True))):
            self.left(16 + index, self.part(self.unit, EVERY, far_first, far_second))


class GatherSmall(Travel):
    def __init__(self, place, ref, own, send, recv):
        super().__init__(place, send, recv)
        self.ref, self.own = ref, own

    def stage_z(self):
        at = self.place
        self.ref[at.z, at.y, at.x] = self.own[...]
        for shift in (1, 2, 3):
            self.go(shift - 1, self.own, self.ref.at[at.z, at.y, at.x], at.along_z(shift))

    def wait_z(self):
        at = self.place
        for shift in (1, 2, 3):
            self.arrived(shift - 1, self.ref.at[at.other_z(4 - shift), at.y, at.x])

    def stage_first(self):
        at = self.place
        part = self.ref.at[:, at.y, at.x]
        self.go(3, part, part, at.along_x())

    def wait_first(self):
        at = self.place
        self.arrived(3, self.ref.at[:, at.y, 1 - at.x])

    def stage_second(self):
        at = self.place
        part = self.ref.at[:, at.y]
        self.go(4, part, part, at.along_y())

    def wait_second(self):
        at = self.place
        self.arrived(4, self.ref.at[:, 1 - at.y])

    def finish(self):
        at = self.place
        for stage in range(3):
            self.left(stage, self.own)
        self.left(3, self.ref.at[:, at.y, at.x])
        self.left(4, self.ref.at[:, at.y])


def unit_first(ref):
    return lambda u, z, y, x: ref.at[u, z, y, x]


def unit_last(ref):
    return lambda u, z, y, x: ref.at[z, y, x, u]


class Reduce(Travel):
    def __init__(self, place, own, other, lane, acc, wide, mid, narrow, final, final_other, send, recv, local):
        super().__init__(place, send, recv)
        self.own, self.other, self.lane, self.local = own, other, lane, local
        self.acc, self.wide, self.mid, self.narrow = acc, wide, mid, narrow
        self.final, self.final_other = final, final_other

    def stage_share(self):
        self.go(0, self.other, self.wide, self.place.sibling())
        pltpu.make_async_copy(self.own, self.acc, self.local).start()

    def wait_share(self):
        pltpu.make_async_copy(self.own, self.acc, self.local).wait()
        self.arrived(0, self.wide)

        def add(z, carry):
            self.acc[z] = self.acc[z] + self.wide[z]
            return carry

        lax.fori_loop(0, 4, add, 0)

    def half(self, far):
        at = self.place
        if self.lane:
            return self.acc.at[:, :, 1 - at.x if far else at.x]
        return self.acc.at[:, 1 - at.y if far else at.y]

    def stage_first(self):
        at = self.place
        self.go(1, self.half(True), self.mid, at.along_x() if self.lane else at.along_y())

    def wait_first(self):
        at = self.place
        self.arrived(1, self.mid)

        def add(z, carry):
            for i in range(2):
                part = self.acc.at[z, i, at.x] if self.lane else self.acc.at[z, at.y, i]
                part[...] = part[...] + self.mid[z, i]
            return carry

        lax.fori_loop(0, 4, add, 0)

    def quarter(self):
        at = self.place
        if self.lane:
            return self.acc.at[:, 1 - at.y, at.x]
        return self.acc.at[:, at.y, 1 - at.x]

    def stage_second(self):
        self.go(2, self.quarter(), self.narrow.at[0:4], self.place.along_y() if self.lane else self.place.along_x())

    def wait_second(self):
        at = self.place
        self.arrived(2, self.narrow.at[0:4])
        part = self.acc.at[:, at.y, at.x]
        part[...] = part[...] + self.narrow[0:4]

    def block(self, shift):
        at = self.place
        return self.acc.at[at.other_z(shift), at.y, at.x]

    def stage_z(self):
        for shift in (1, 2, 3):
            self.go(2 + shift, self.block(shift), self.narrow.at[3 + shift], self.place.along_z(shift))

    def wait_z(self):
        total = self.block(0)[...].astype(F32)
        for shift in (1, 2, 3):
            self.arrived(2 + shift, self.narrow.at[3 + shift])
            total = total + self.narrow[3 + shift].astype(F32)
        self.final[...] = total

    def stage_final(self):
        self.go(6, self.final, self.final, self.place.sibling())

    def wait_final(self):
        self.arrived(6, self.final_other)
        self.left(0, self.other)
        self.left(1, self.half(True))
        self.left(2, self.quarter())
        for shift in (1, 2, 3):
            self.left(2 + shift, self.block(shift))
        self.left(6, self.final)


class ReduceSmall(Travel):
    def __init__(self, place, own, acc, wide, mid, narrow, final, send, recv):
        super().__init__(place, send, recv)
        self.own, self.acc, self.wide, self.mid, self.narrow, self.final = own, acc, wide, mid, narrow, final

    def stage_share(self):
        self.go(0, self.own, self.wide, self.place.sibling())

    def wait_share(self):
        self.arrived(0, self.wide)
        self.acc[...] = self.own[...] + self.wide[...]

    def stage_first(self):
        at = self.place
        self.go(1, self.acc.at[:, 1 - at.y], self.mid, at.along_y())

    def wait_first(self):
        at = self.place
        self.arrived(1, self.mid)
        half = self.acc.at[:, at.y]
        half[...] = half[...] + self.mid[...]

    def stage_second(self):
        at = self.place
        self.go(2, self.acc.at[:, at.y, 1 - at.x], self.narrow.at[0:4], at.along_x())

    def wait_second(self):
        at = self.place
        self.arrived(2, self.narrow.at[0:4])
        part = self.acc.at[:, at.y, at.x]
        part[...] = part[...] + self.narrow[0:4]

    def block(self, shift):
        at = self.place
        return self.acc.at[at.other_z(shift), at.y, at.x]

    def stage_z(self):
        for shift in (1, 2, 3):
            self.go(2 + shift, self.block(shift), self.narrow.at[3 + shift], self.place.along_z(shift))

    def wait_z(self):
        at = self.place
        total = self.block(0)[...]
        for shift in (1, 2, 3):
            self.arrived(2 + shift, self.narrow.at[3 + shift])
            total = total + self.narrow[3 + shift]
        self.final[...] = total
        self.left(0, self.own)
        self.left(1, self.acc.at[:, 1 - at.y])
        self.left(2, self.acc.at[:, at.y, 1 - at.x])
        for shift in (1, 2, 3):
            self.left(2 + shift, self.block(shift))


def reduce_scratch(count, rows, d):
    return [
        pltpu.VMEM((count, 4, 2, 2, rows, d), BF16), pltpu.VMEM((count, 4, 2, 2, rows, d), BF16),
        pltpu.VMEM((count, 4, 2, rows, d), BF16), pltpu.VMEM((count, 7, rows, d), BF16),
        pltpu.SemaphoreType.DMA((count, 7)), pltpu.SemaphoreType.DMA((count, 7)), pltpu.SemaphoreType.DMA((count,)),
    ]


def reduce_unit(place, grad, scratch, index, lane, final, unit, other, columns=None):
    acc, wide, mid, narrow, send, recv, local = scratch
    own, theirs = grad(unit, EVERY, EVERY, EVERY), grad(other, EVERY, EVERY, EVERY)
    final_own, final_other = final.at[unit], final.at[other]
    if columns is not None:
        own, theirs = own.at[:, :, :, :, columns], theirs.at[:, :, :, :, columns]
        final_own, final_other = final_own.at[:, columns], final_other.at[:, columns]
    return Reduce(
        place, own, theirs, lane, acc.at[index], wide.at[index], mid.at[index], narrow.at[index], final_own, final_other,
        send.at[index], recv.at[index], local.at[index],
    )


def reduce_round(place, grad, scratch, index, final, columns=None):
    return [
        reduce_unit(
            place, grad, scratch, index + l, l, final, 2 * place.core + l, 2 * (1 - place.core) + l, columns
        )
        for l in range(2)
    ]


def both(lanes, *names):
    for name in names:
        for lane in lanes:
            getattr(lane, name)()


REDUCE_STEPS = (
    ("stage_share",), ("wait_share", "stage_first"), ("wait_first", "stage_second"), ("wait_second", "stage_z"),
    ("wait_z", "stage_final"), ("wait_final",),
)
GATHER_STEPS = (
    ("stage_z",), ("wait_z", "stage_first"), ("wait_first", "stage_second"), ("wait_second", "stage_share"), ("wait_share",),
)


def job(lanes, steps):
    return [lambda names=names: both(lanes, *names) for names in steps]


def plan(jobs, places):
    found, late = {}, []
    for number, (steps, start, spans, *latest) in enumerate(jobs):
        time = start
        allowed = places[:places.index(latest[0]) + 1] if latest else places
        for i, step in enumerate(steps):
            fitting = [place for place in allowed if place[1] >= time] or allowed[-1:] * len(latest)
            if fitting:
                name, time = fitting[0]
                found.setdefault(name, []).append(step)
            else:
                late.append((time, number, step))
            time = time + (spans[i] if i < len(spans) else 0.0)
    return found, [step for _, _, step in sorted(late, key=lambda entry: entry[:2])]


def hook_in(found, name, condition):
    if name in found:

        @pl.when(condition)
        def _():
            for step in found[name]:
                step()


GATHER_PACE = 9.5
GATHER_SPANS = (6.0, 7.0, 10.0, 4.0)
PASS_TIME, PASS_TIMES = 8.5, (1.5, 3.0, 4.5, 6.0, 7.5, 8.5)
FFN_TIME = 5.0
FFN_BACK_TIME = 6.0
REDUCE_SPANS = (4.0, 8.0, 6.0, 8.0, 3.0)
SLIM_SPANS = (3.0, 6.0, 5.0, 6.0, 3.0)
HALVES = (slice(0, 256), slice(256, 512))
HEADS_TIME, HEADS_TIMES = 8.0, (0.0, 1.7, 3.4, 5.1, 6.8)
LAST_TIME = 2.0
FFN_REDUCE_PACE = 4.5


def matrix(block):
    return block.reshape(-1, block.shape[-1])


def forward_kernel(ring, count, *refs):
    refs = list(refs)

    def take(number):
        out = refs[:number]
        del refs[:number]
        return out

    tok_ref, mem_ref, doc_ref, keep_ref = take(4)
    if ring:
        shards = take(7)
        narrow_refs = take(3)
    else:
        attn_ref, w1_ref, w2_ref, vec_in_ref, b1_in_ref = take(5)
    n1_ref, qt_ref, k_ref, v_ref, e_ref, linv_ref, ot_ref, h1_ref, out_ref, res_ref, act_ref, slope_ref, vec_ref = take(13)
    if ring:
        attn_ref, w1_ref, w2_ref, wr_ref, gate_ref = take(5)
    bias_ref, pair_ref, vt_ref, hidden_ref, b1_ref, attn_v, w1_v, w2_v, wsem = take(9)
    seg = tok_ref.shape[1]
    slots = mem_ref.shape[1]
    step = pl.program_id(0)
    load_attn = lambda: pltpu.make_async_copy(attn_ref, attn_v, wsem.at[0])
    load_w1 = lambda: pltpu.make_async_copy(w1_ref, w1_v, wsem.at[1])
    load_w2 = lambda: pltpu.make_async_copy(w2_ref, w2_v, wsem.at[2])
    if ring:
        units, psem, sown_ref, sall_ref, send, recv, local, ssend, srecv, fsend, frecv = take(11)
        place = Place()
        views = [unit_first(attn_ref), unit_first(w1_ref), unit_last(w2_ref), unit_first(wr_ref), unit_last(gate_ref)]
        rounds = []
        for r, view in enumerate(views):
            own = (lambda u: shards[6].at[u]) if r == 4 else (lambda u, r=r: units.at[4 * r + u])
            if r == 0:
                lanes = [
                    FirstGather(place, unit_first(attn_v), own, l, fsend.at[l], frecv.at[l], local.at[r, l]) for l in range(2)
                ]
            else:
                lanes = [Gather(place, view, own, l, send.at[r, l], recv.at[r, l], local.at[r, l]) for l in range(2)]
            rounds.append(lanes)
        small = GatherSmall(place, sall_ref, sown_ref, ssend, srecv)
        packs = [(shards[0], units.at[0:3]), (shards[1], units.at[3])]
        packs += [(shards[2].at[:, j * 512:(j + 1) * 512], units.at[4 + j]) for j in range(4)]
        packs += [(shards[3], units.at[8:12]), (shards[4], units.at[12:15]), (shards[5], units.at[15])]

        def pack(i):
            return pltpu.make_async_copy(packs[i][0], packs[i][1], psem.at[i])

        passes = [((s, i), PASS_TIME * s + PASS_TIMES[i]) for s in range(count) for i in range(len(PASS_TIMES))]
        jobs = []
        for r in range(1, 5):
            steps = job(rounds[r], GATHER_STEPS)
            if r in (1, 2):
                share = steps[-1]
                load = load_w1 if r == 1 else load_w2
                steps[-1] = lambda share=share, load=load: (share(), load().start())
            latest = (passes[-1],) if r in (1, 2) else ()
            if r == 1:
                jobs.append((steps[1:], 0.0, GATHER_SPANS[1:]) + latest)
            else:
                jobs.append((steps, GATHER_PACE * (r - 1) - GATHER_SPANS[0], GATHER_SPANS) + latest)
        places = list(passes)
        at_load = PASS_TIME * count
        places += [((count + s, i), at_load + FFN_TIME * (s + i / 4)) for s in range(count) for i in range(4)]
        found, rest = plan(jobs, places)

    def hook(name, extra=True):
        if ring:
            hook_in(found, name, (step == name[0]) & extra)

    @pl.when(step < count)
    def _():
        if ring:

            @pl.when(step == 0)
            def _():
                for i in range(len(packs)):
                    pack(i).start()
                bias, gbias, gains = (ref[...].astype(F32) for ref in narrow_refs)
                narrow = jnp.concatenate([gbias, gains], 0)
                lane = lax.broadcasted_iota(jnp.int32, (4, 128), 1) // narrow.shape[1]
                narrow = jnp.where(lane == lax.rem(place.dp, 4), jnp.concatenate([narrow] * 4, 1), 0.0)
                sown_ref[...] = jnp.concatenate([bias, narrow, jnp.zeros((3, 128), F32)], 0)
                place.greet()
                small.stage_z()
                pack(0).wait()
                pack(1).wait()
                both(rounds[0], "begin")
                for i in range(2, len(packs)):
                    pack(i).wait()
        else:

            @pl.when(step == 0)
            def _():
                load_attn().start()
                load_w1().start()
                load_w2().start()
                vec_ref[...] = vec_in_ref[...]
                b1_ref[...] = b1_in_ref[...]
                load_attn().wait()

        keep = keep_ref[0][:, 0:1]
        docs = doc_ref[0].astype(F32)
        key_docs = jnp.broadcast_to(docs, (128, seg)).T
        slot_docs = jnp.broadcast_to(keep - 1.0, (slots, 128))
        key_docs = jnp.concatenate([slot_docs, jnp.full((128 - slots, 128), -1.0, F32), key_docs], 0)
        for block, (first, last_row) in enumerate(SPANS):
            length = last_row - first
            position = lax.broadcasted_iota(jnp.int32, (length, BLOCK), 0) + (first - 128 - block * BLOCK)
            position = position <= lax.broadcasted_iota(jnp.int32, (length, BLOCK), 1)
            same = key_docs[first:last_row] == docs[:, block * BLOCK:(block + 1) * BLOCK]
            bias_ref[STARTS[block]:STARTS[block] + length, :] = jnp.where(same & position, 0.0, -1e30)
        if ring:

            @pl.when(step == 0)
            def _():
                small.wait_z()
                small.stage_first()
                for shift in FirstGather.SHIFTS[1:]:
                    for lane in rounds[0]:
                        lane.column_block(shift)
                both(rounds[0], "column_done")
                small.wait_first()
                small.stage_second()
                for shift in FirstGather.SHIFTS:
                    for lane in rounds[0]:
                        lane.far_block(shift)
                both(rounds[1], "stage_z")
                both(rounds[0], "far_done")
                small.wait_second()
                for m in range(4):
                    total = sall_ref[m, 0, 0] + sall_ref[m, 0, 1] + sall_ref[m, 1, 0] + sall_ref[m, 1, 1]
                    vec_ref[:, m * 128:(m + 1) * 128] = jnp.concatenate([total[1:8], total[0:1]], 0)
                    for i in range(4):
                        b1_ref[m, :, i * 128:(i + 1) * 128] = sall_ref[m, i // 2, i % 2, 0:1, :]
                both(rounds[0], "rest")
                both(rounds[0], "done")
                pltpu.make_async_copy(attn_v, attn_ref, wsem.at[0]).start()

        x = tok_ref[0].astype(F32)
        gain_one = vec_ref[1:2, :]
        hat, _ = norm_parts(x)
        n1t = (hat * gain_one).astype(BF16)
        hat, _ = norm_parts(mem_ref[0] * keep)
        n1_ref[0, 0:slots, :] = (hat * gain_one).astype(BF16)
        n1_ref[0, slots:128, :] = jnp.zeros((128 - slots, x.shape[1]), BF16)
        n1_ref[0, 128:, :] = n1t
        qt_ref[0] = (dot_nt(matrix(attn_v[0]).T, n1t) * 0.125).astype(BF16)
        n1 = n1_ref[0]
        keys = dot(n1, matrix(attn_v[1])).astype(BF16)
        v = dot(n1, matrix(attn_v[2])).astype(BF16)
        for pair in range(4):
            k_ref[0, pair] = keys[:, pair * 128:(pair + 1) * 128]
            v_ref[0, pair] = v[:, pair * 128:(pair + 1) * 128]
        vt_ref[...] = v.T
        pair_ref[...] = jnp.zeros_like(pair_ref)
        for s in range(count):
            hook((s, 0))

        def one_pair(pair, carry):
            lanes = pl.ds(pl.multiple_of(pair * 128, 128), 128)
            for block, (first, last_row) in enumerate(SPANS):
                start = STARTS[block]
                held = pair_ref.at[block]
                columns = pl.ds(block * BLOCK, BLOCK)
                diagonal_pair(held, qt_ref[0, lanes, columns])
                scores = dot(k_ref[0, pair, first:last_row, :], held[...])
                bias = bias_ref[start:start + last_row - first, :]
                scores = scores + jnp.concatenate([bias, bias], 1)
                largest = jnp.max(scores, axis=0, keepdims=True)
                e = jnp.exp(scores - largest)
                linv = 1.0 / jnp.sum(e, axis=0, keepdims=True)
                e = e.astype(BF16)
                e_ref[0, pair, start:start + last_row - first, :] = e
                linv_ref[0, pair, block, :, :] = linv
                mixed = dot(vt_ref[lanes, first:last_row], e) * linv
                ot_ref[0, lanes, columns] = jnp.concatenate(
                    [mixed[0:64, 0:128], mixed[64:128, 128:256]], 0
                ).astype(BF16)
            for s in range(count):
                for i in range(4):
                    hook((s, 1 + i), pair == i)
            return carry

        lax.fori_loop(0, 4, one_pair, 0)
        h1 = x + dot(ot_ref[0].T, matrix(attn_v[3]))
        h1_ref[0] = h1
        hidden_ref[step] = h1
        for s in range(count):
            hook((s, 5))

    @pl.when(step >= count)
    def _():
        @pl.when(step == count)
        def _():
            load_w1().wait()
            load_w2().wait()

        h1 = hidden_ref[step - count]
        hat, _ = norm_parts(h1)
        n2 = (hat * vec_ref[2:3, :]).astype(BF16)
        tall = seg // 2
        for block in range(2):
            rows = slice(block * tall, (block + 1) * tall)
            result = h1[rows]
            for part in range(8):
                columns = slice((part % 2) * 256, (part % 2) * 256 + 256)
                before = dot(n2[rows], matrix(w1_v[part // 2])[:, columns]) + b1_ref[part // 2][:, columns]
                cdf = 0.5 + 0.5 * lax.erf(before * 0.7071067811865476)
                active = (before * cdf).astype(BF16)
                act_ref[0, part // 2, rows, columns] = active
                slope = cdf + before * jnp.exp(before * before * -0.5) * 0.3989422804014327
                slope_ref[0, part // 2, rows, columns] = slope.astype(BF16)
                result = result + dot(active, matrix(w2_v[part // 2])[columns, :])
                if part in (3, 7):
                    for s in range(count, 2 * count):
                        hook((s, 2 * block + (part == 7)))
            out_ref[0, rows, :] = result.astype(BF16)
        res_ref[0] = result
        if ring:

            @pl.when(step == 2 * count - 1)
            def _():
                pltpu.make_async_copy(attn_v, attn_ref, wsem.at[0]).wait()
                for step_left in rest:
                    step_left()
                for lanes in rounds:
                    both(lanes, "finish")
                small.finish()


ANY = pl.BlockSpec(memory_space=pl.ANY)


def full_spec(shape):
    return pl.BlockSpec(shape, lambda i: (0,) * len(shape), pipeline_mode=pl.Buffered(1))


def phase_spec(shape, first, count):
    return pl.BlockSpec((1,) + shape, lambda i: (jnp.clip(i - first, 0, count - 1),) + (0,) * len(shape))


def call_forward(ring, tokens, memory, docs, keep, weights):
    n, seg, d = tokens.shape
    slots = memory.shape[1]
    early = [
        ((seg + 128, d), BF16), ((d, seg), BF16), ((4, seg + 128, 128), BF16), ((4, seg + 128, 128), BF16), ((4, LIVE, 256), BF16),
        ((4, 4, 1, 256), F32), ((d, seg), BF16), ((seg, d), F32),
    ]
    late = [((seg, d), BF16), ((seg // 2, d), F32), ((4, seg, 512), BF16), ((4, seg, 512), BF16)]
    units = (4, 4, 2, 2, 32, d)
    unit_shapes = [units, units, (4, 2, 2, 4, 32, d), units, (4, 2, 2, 4, 16, d)]
    out_shape = [jax.ShapeDtypeStruct((n,) + shape, kind) for shape, kind in early + late]
    out_shape += [jax.ShapeDtypeStruct((8, d), F32)]
    out_specs = [phase_spec(shape, 0, n) for shape, _ in early] + [phase_spec(shape, n, n) for shape, _ in late]
    out_specs += [full_spec((8, d))]
    in_specs = [phase_spec((seg, d), 0, n), phase_spec((slots, d), 0, n), phase_spec((1, seg), 0, n), phase_spec((1, 128), 0, n)]
    scratch = [
        pltpu.VMEM((LIVE, 128), F32), pltpu.VMEM((4, 128, 256), BF16), pltpu.VMEM((d, seg + 128), BF16),
        pltpu.VMEM((n, seg, d), F32), pltpu.VMEM((4, 1, d), F32), pltpu.VMEM(unit_shapes[0], BF16),
        pltpu.VMEM(unit_shapes[1], BF16), pltpu.VMEM(unit_shapes[2], BF16), pltpu.SemaphoreType.DMA((3,)),
    ]
    params = dict(vmem_limit_bytes=VMEM_LIMIT)
    if ring:
        in_specs += [ANY] * 7 + [full_spec(array.shape) for array in weights[7:]]
        out_shape += [jax.ShapeDtypeStruct(shape, BF16) for shape in unit_shapes]
        out_specs += [ANY] * 5
        scratch += [
            pltpu.VMEM((16, 32, d), BF16), pltpu.SemaphoreType.DMA((9,)), pltpu.VMEM((8, 128), F32),
            pltpu.VMEM((4, 2, 2, 8, 128), F32), pltpu.SemaphoreType.DMA((5, 2, 7)), pltpu.SemaphoreType.DMA((5, 2, 7)),
            pltpu.SemaphoreType.DMA((5, 2)), pltpu.SemaphoreType.DMA((5,)), pltpu.SemaphoreType.DMA((5,)),
            pltpu.SemaphoreType.DMA((2, 20)), pltpu.SemaphoreType.DMA((2, 20)),
        ]
        params.update(collective_id=0, has_side_effects=True)
    else:
        in_specs += [ANY] * 3 + [full_spec((8, d)), full_spec((4, 1, d))]
    return pl.pallas_call(
        functools.partial(forward_kernel, ring, n),
        grid=(2 * n,),
        out_shape=out_shape,
        in_specs=in_specs,
        out_specs=out_specs,
        scratch_shapes=scratch,
        compiler_params=pltpu.CompilerParams(**params),
        name="gather_forward" if ring else "forward_rows",
    )(tokens, memory, docs, keep, *weights)


def writer_all(
    gate_done, read_done, res_ref, mem_ref, memgrad_ref, doc_ref, keep_ref, wr_ref, gate_ref, vec_ref,
    newmem_ref, dres_ref, dkept_ref, gwr_ref, ggate_ref, ggb_ref,
    n3_ref, ns_ref, kept_ref, sq_ref, tk_ref, tv_ref, p_ref, wt_ref, dsq_ref, dlog_ref, dw_ref,
):
    n, half, d = res_ref.shape
    slots = mem_ref.shape[1]
    gain = vec_ref[3:4, :]

    def norm(i, carry):
        rows = pl.ds(pl.multiple_of(i * half, half), half)
        small = pl.ds(pl.multiple_of(i * slots, slots), slots)
        hat, _ = norm_parts(res_ref[i])
        n3_ref[rows, :] = (hat * gain).astype(BF16)
        kept = mem_ref[i] * keep_ref[i][:, 0:1]
        kept_ref[small, :] = kept
        hat, _ = norm_parts(kept)
        ns_ref[small, :] = (hat * gain).astype(BF16)
        tk_ref[rows, :] = dot(n3_ref[rows, :], wr_ref[1]).astype(BF16)
        tv_ref[rows, :] = dot(n3_ref[rows, :], wr_ref[2]).astype(BF16)
        return carry

    lax.fori_loop(0, n, norm, 0)
    sq_ref[...] = (dot(ns_ref[...], wr_ref[0]) * 0.125).astype(BF16)
    low_half = lax.broadcasted_iota(jnp.int32, (1, 128), 1) < 64

    def halves(rows):
        zero = jnp.zeros_like(rows)
        return jnp.concatenate([jnp.where(low_half, rows, zero), jnp.where(low_half, zero, rows)], 0)

    def read(i, carry):
        rows = pl.ds(pl.multiple_of(i * half, half), half)
        small = pl.ds(pl.multiple_of(i * slots, slots), slots)
        docs = doc_ref[i].astype(F32)
        bias = jnp.where(docs == jnp.max(docs), 0.0, -1e30)[:, docs.shape[1] - half:]
        for pair in range(4):
            lanes = slice(pair * 128, pair * 128 + 128)
            scores = dot_nt(halves(sq_ref[small, lanes]), tk_ref[rows, lanes]) + bias
            e = jnp.exp(scores - jnp.max(scores, axis=1, keepdims=True))
            p = e * (1.0 / jnp.sum(e, axis=1, keepdims=True))
            p_ref[i, pair] = p
            mixed = dot(p.astype(BF16), tv_ref[rows, lanes])
            wt_ref[small, lanes] = jnp.where(low_half, mixed[:slots], mixed[slots:]).astype(BF16)
        return carry

    lax.fori_loop(0, n, read, 0)

    def put(ref, index, value):
        ref[index] = value.astype(BF16).reshape(ref.shape[1:])

    write = dot(wt_ref[...], wr_ref[3])
    kept = kept_ref[...]
    write_low = write.astype(BF16)
    kept_low = kept.astype(BF16)
    logit = dot(kept_low, gate_ref[0]) + dot(write_low, gate_ref[1]) + vec_ref[0:1, :]
    gate = jax.nn.sigmoid(logit)
    new = gate * kept + (1.0 - gate) * write
    memgrad = memgrad_ref[...].reshape(n * slots, d)
    newmem_ref[...] = new.reshape(n, slots, d)
    dlogit = memgrad * (kept - write) * gate * (1.0 - gate)
    dlog_ref[...] = dlogit.astype(BF16)
    dlow = dlog_ref[...]
    ggb_ref[...] = jnp.sum(dlow.astype(F32), axis=0, keepdims=True)
    ggate_ref[0:2] = dot_tn(kept_low, dlow).astype(BF16).reshape((2,) + ggate_ref.shape[1:])
    ggate_ref[2:4] = dot_tn(write_low, dlow).astype(BF16).reshape((2,) + ggate_ref.shape[1:])
    gate_done()
    dkept = memgrad * gate + dot_nt(dlow, gate_ref[0])
    dwrite = memgrad * (1.0 - gate) + dot_nt(dlow, gate_ref[1])
    dkept_ref[...] = dkept.reshape(n, slots, d)
    dw_low = dwrite.astype(BF16)
    put(gwr_ref, 3, dot_tn(wt_ref[...], dw_low))
    dw_ref[...] = dot_nt(dw_low, wr_ref[3]).astype(BF16)

    def read_back(i, carry):
        rows = pl.ds(pl.multiple_of(i * half, half), half)
        small = pl.ds(pl.multiple_of(i * slots, slots), slots)
        for pair in range(4):
            lanes = slice(pair * 128, pair * 128 + 128)
            p = p_ref[i, pair]
            grads = halves(dw_ref[small, lanes])
            dp = dot_nt(grads, tv_ref[rows, lanes])
            ds = (p * (dp - jnp.sum(dp * p, axis=1, keepdims=True))).astype(BF16)
            dq = dot(ds, tk_ref[rows, lanes]) * 0.125
            dsq_ref[small, lanes] = jnp.where(low_half, dq[:slots], dq[slots:]).astype(BF16)
            tk_ref[rows, lanes] = dot_tn(ds, halves(sq_ref[small, lanes])).astype(BF16)
            tv_ref[rows, lanes] = dot_tn(p.astype(BF16), grads).astype(BF16)
        return carry

    lax.fori_loop(0, n, read_back, 0)
    read_done()
    put(gwr_ref, 0, dot_tn(ns_ref[...], dsq_ref[...]))
    put(gwr_ref, 1, dot_tn(n3_ref[...], tk_ref[...]))
    put(gwr_ref, 2, dot_tn(n3_ref[...], tv_ref[...]))
    grad = dot_nt(dsq_ref[...], wr_ref[0])
    hat, rstd = norm_parts(kept_ref[...])
    dkept_ref[...] += norm_back(grad, hat, rstd, gain).reshape(n, slots, d)

    def back(i, carry):
        rows = pl.ds(pl.multiple_of(i * half, half), half)
        grad = dot_nt(tk_ref[rows, :], wr_ref[1]) + dot_nt(tv_ref[rows, :], wr_ref[2])
        hat, rstd = norm_parts(res_ref[i])
        dres_ref[i] = norm_back(grad, hat, rstd, gain)
        return carry

    lax.fori_loop(0, n, back, 0)


def ffn_back_kernel(ring, count, *refs):
    refs = list(refs)

    def take(number):
        out = refs[:number]
        del refs[:number]
        return out

    writer_in = take(8)
    vec_ref = writer_in[7]
    og_ref, h1_ref, act_ref, slope_ref, ot_ref, linv_ref, w1_ref, w2_ref, attn_ref = take(9)
    newmem_ref, dkept_ref, ggb_ref, gb_ref, gw1_ref, gw2_ref, gwo_ref, dh_ref, dot_ref, gwr_out, ggate_out = take(11)
    writer_scratch = take(11)
    dres_ref, acc1_ref, acc2_ref, acco_ref, w1_v, w2_v, wo_v, wsem = take(8)
    step = pl.program_id(0)
    seg = og_ref.shape[1]
    loads = lambda: [
        pltpu.make_async_copy(w1_ref, w1_v, wsem.at[0]), pltpu.make_async_copy(w2_ref, w2_v, wsem.at[1]),
        pltpu.make_async_copy(attn_ref.at[3], wo_v, wsem.at[2]),
    ]
    if ring:
        gwr_ref, ggate_ref, fwr_ref, fgate_ref = take(4)
        wide_scratch, slim_scratch = take(7), take(7)
        place = Place()
        writer_rounds = [
            reduce_round(place, unit_first(gwr_ref), wide_scratch, 2 * i, fwr_ref, half) for i, half in enumerate(HALVES)
        ]
        gate_round = reduce_round(place, unit_last(ggate_ref), slim_scratch, 0, fgate_ref)
        jobs = [
            (job(gate_round, REDUCE_STEPS)[2:], 0.0, REDUCE_SPANS[2:]),
            (job(writer_rounds[0], REDUCE_STEPS)[1:], 1.5, REDUCE_SPANS[1:]),
            (job(writer_rounds[1], REDUCE_STEPS)[1:], 4.5, REDUCE_SPANS[1:]),
        ]
        places = [((1 + s, i), FFN_BACK_TIME * (s + i / 4)) for s in range(count) for i in range(4)]
        found, rest = plan(jobs, places)
    else:
        gwr_ref, ggate_ref = gwr_out, ggate_out

    @pl.when(step == 0)
    def _():
        for load in loads():
            load.start()
        if ring:
            place.greet()
        acc1_ref[...] = jnp.zeros_like(acc1_ref)
        acc2_ref[...] = jnp.zeros_like(acc2_ref)
        acco_ref[...] = jnp.zeros_like(acco_ref)
        gb_ref[...] = jnp.zeros_like(gb_ref)
        gate_done = (lambda: both(gate_round, "stage_share")) if ring else (lambda: None)
        read_done = (lambda: both(gate_round, "wait_share", "stage_first")) if ring else (lambda: None)
        writer_all(
            gate_done, read_done, *writer_in, newmem_ref, dres_ref, dkept_ref, gwr_ref, ggate_ref, ggb_ref, *writer_scratch
        )
        if ring:
            both(writer_rounds[0] + writer_rounds[1], "stage_share")
        for load in loads():
            load.wait()

    @pl.when(step > 0)
    def _():
        top = og_ref[0, 0:seg // 2, :].astype(F32)
        bottom = og_ref[0, seg // 2:, :].astype(F32) + dres_ref[step - 1]
        dresult = jnp.concatenate([top, bottom], 0)
        low = dresult.astype(BF16)
        h1 = h1_ref[0]
        hat, rstd = norm_parts(h1)
        gain = vec_ref[2:3, :]
        n2t = (hat * gain).astype(BF16).T
        lowt = low.T
        grad = jnp.zeros_like(dresult)
        for part in range(4):
            if ring:
                for s in range(1, 1 + count):
                    hook_in(found, (s, part), step == s)
            acc2_ref[part] += dot(lowt, act_ref[0, part])
            dbefore = (dot_nt(low, w2_v[part]) * slope_ref[0, part].astype(F32)).astype(BF16)
            gb_ref[part] += jnp.sum(dbefore.astype(F32), axis=0, keepdims=True)
            acc1_ref[part] += dot(n2t, dbefore)
            grad = grad + dot_nt(dbefore, w1_v[part])
        dh = dresult + norm_back(grad, hat, rstd, gain)
        dh_ref[0] = dh
        dlow = dh.astype(BF16)
        mixed_grad = dot_nt(wo_v[...], dlow)
        for pair in range(4):
            for block in range(seg // BLOCK):
                columns = slice(block * BLOCK, (block + 1) * BLOCK)
                for i in range(2):
                    features = slice(pair * 128 + i * 64, pair * 128 + i * 64 + 64)
                    scale = linv_ref[0, pair, block, :, i * 128:(i + 1) * 128]
                    dot_ref[0, features, columns] = (mixed_grad[features, columns] * scale).astype(BF16)
        acco_ref[...] += dot(ot_ref[0], dlow)

        @pl.when(step == count)
        def _():
            stores = [
                pltpu.make_async_copy(w1_v, gw1_ref, wsem.at[0]), pltpu.make_async_copy(w2_v, gw2_ref, wsem.at[1]),
                pltpu.make_async_copy(wo_v, gwo_ref, wsem.at[2]),
            ]
            w1_v[...] = acc1_ref[...].astype(BF16)
            stores[0].start()
            for part in range(4):
                w2_v[part] = acc2_ref[part].T.astype(BF16)
            stores[1].start()
            wo_v[...] = acco_ref[...].astype(BF16)
            stores[2].start()
            if ring:
                for step_left in rest:
                    step_left()
                gwr_out[...] = fwr_ref[...]
                ggate_out[...] = fgate_ref[...]
            for store in stores:
                store.wait()


def call_ffn_back(ring, res, memory, memory_grad, docs, keep, wr, gate, vec, out_grad, h1, act, slope, ot, linv, w1, w2, attn):
    n, half, d = res.shape
    seg = 2 * half
    slots = memory.shape[1]
    rows, small = n * half, n * slots
    writer_args = (res, memory, memory_grad, docs, keep, wr, gate, vec)
    units = (4, 4, 2, 2, 32, d)
    gate_units = (4, 2, 2, 4, 16, d)
    if ring:
        grads = [((4, 32, d), F32), ((4, 16, d), F32)]
    else:
        grads = [(units, BF16), (gate_units, BF16)]
    whole = [((n, slots, d), F32), ((n, slots, d), F32), ((1, d), F32), ((4, 1, d), F32)]
    stored = [((4, d, d), BF16), ((4, d, d), BF16), ((d, d), BF16)]
    scratch = [
        pltpu.VMEM((rows, d), BF16), pltpu.VMEM((small, d), BF16), pltpu.VMEM((small, d), F32), pltpu.VMEM((small, d), BF16),
        pltpu.VMEM((rows, d), BF16), pltpu.VMEM((rows, d), BF16), pltpu.VMEM((n, 4, 2 * slots, half), F32),
        pltpu.VMEM((small, d), BF16), pltpu.VMEM((small, d), BF16), pltpu.VMEM((small, d), BF16), pltpu.VMEM((small, d), BF16),
        pltpu.VMEM((n, half, d), F32), pltpu.VMEM((4, d, d), F32), pltpu.VMEM((4, d, d), F32), pltpu.VMEM((d, d), F32),
        pltpu.VMEM((4, d, d), BF16), pltpu.VMEM((4, d, d), BF16), pltpu.VMEM((d, d), BF16), pltpu.SemaphoreType.DMA((3,)),
    ]
    params = dict(vmem_limit_bytes=VMEM_LIMIT)
    if ring:
        scratch += [pltpu.VMEM(units, BF16), pltpu.VMEM(gate_units, BF16)]
        scratch += [pltpu.VMEM((4, 32, d), F32), pltpu.VMEM((4, 16, d), F32)]
        scratch += reduce_scratch(4, 32, d // 2) + reduce_scratch(2, 16, d)
        params.update(collective_id=1, has_side_effects=True)
    return pl.pallas_call(
        functools.partial(ffn_back_kernel, ring, n),
        grid=(n + 1,),
        out_shape=[jax.ShapeDtypeStruct(shape, kind) for shape, kind in whole + stored]
        + [jax.ShapeDtypeStruct((n, seg, d), F32), jax.ShapeDtypeStruct((n, d, seg), BF16)]
        + [jax.ShapeDtypeStruct(shape, kind) for shape, kind in grads],
        in_specs=[full_spec(array.shape) for array in writer_args] + [
            phase_spec((seg, d), 1, n), phase_spec((seg, d), 1, n), phase_spec((4, seg, 512), 1, n),
            phase_spec((4, seg, 512), 1, n), phase_spec((d, seg), 1, n), phase_spec((4, 4, 1, 256), 1, n), ANY, ANY, ANY,
        ],
        out_specs=[full_spec(shape) for shape, _ in whole] + [ANY] * 3 + [phase_spec((seg, d), 1, n), phase_spec((d, seg), 1, n)]
        + [full_spec(shape) for shape, _ in grads],
        scratch_shapes=scratch,
        compiler_params=pltpu.CompilerParams(**params),
        name="ffn_back",
    )(*writer_args, out_grad, h1, act, slope, ot, linv, w1, w2, attn)


def attn_back_kernel(ring, count, *refs):
    refs = list(refs)

    def take(number):
        out = refs[:number]
        del refs[:number]
        return out

    qt_ref, k_ref, v_ref, e_ref, ot_ref, dot_ref = take(6)
    tok_ref, mem_ref, keep_ref, dkept_ref, dh_ref = take(5)
    n1_ref, attn_ref, vec_ref = take(3)
    if ring:
        ggb_ref, gb_ref, gw1_ref, gw2_ref, gwo_ref = take(5)
    gtok_ref, gmem_ref = take(2)
    if ring:
        fqkv_ref, fo_ref, fw1_ref, fw2_ref, fsmall_ref = take(5)
    else:
        (gqkv_ref,) = take(1)
    dqt_ref, dkl_ref, dvl_ref, dk_ref, dv_ref, qp_ref, dp_ref = take(7)
    step = pl.program_id(0)
    seg = tok_ref.shape[1]
    d = tok_ref.shape[2]
    slots = mem_ref.shape[1]
    if ring:
        gqkv_ref, ffn_final, out_final, heads_final = take(4)
        wide_scratch, out_scratch, heads_scratch = take(7), take(7), take(7)
        sown, sacc, swide, smid, snarrow, ssend, srecv = take(7)
        place = Place()
        ffn_rounds = [
            reduce_round(place, grad, wide_scratch, 4 * j + 2 * i, ffn_final.at[j], half)
            for j, grad in ((1, unit_last(gw2_ref)), (0, unit_first(gw1_ref))) for i, half in enumerate(HALVES)
        ]
        out_unit = reduce_unit(place, unit_last(gwo_ref), out_scratch, 0, 0, out_final, place.core, 1 - place.core)
        heads = [
            reduce_unit(
                place, unit_first(gqkv_ref.at[p]), heads_scratch, p, p % 2, heads_final.at[p], place.core, 1 - place.core
            )
            for p in range(4)
        ]
        small = ReduceSmall(place, sown, sacc, swide, smid, snarrow, fsmall_ref, ssend, srecv)
        jobs = [(job(ffn_rounds[i], REDUCE_STEPS), FFN_REDUCE_PACE * i, REDUCE_SPANS) for i in range(4)]
        jobs.append((job([out_unit], REDUCE_STEPS), FFN_REDUCE_PACE * 4, SLIM_SPANS))
        jobs.append((job([small], REDUCE_STEPS[:4] + (("wait_z",),)), FFN_REDUCE_PACE * 4 + 1.0, SLIM_SPANS))
        for p in range(4):
            jobs.append((job([heads[p]], REDUCE_STEPS)[1:], HEADS_TIME * (p + 1) + SLIM_SPANS[0], SLIM_SPANS[1:]))
        places = [((p, i), HEADS_TIME * p + HEADS_TIMES[i]) for p in range(4) for i in range(5)]
        places += [((4 + s, 0), 4 * HEADS_TIME + LAST_TIME * (s + 1)) for s in range(count)]
        found, rest = plan(jobs, places)

    def hook(name, extra=True):
        if ring:
            hook_in(found, name, (step == name[0]) & extra)

    @pl.when(step < 4)
    def _():
        @pl.when(step == 0)
        def _():
            if ring:
                place.greet()
                for m in range(4):
                    for i in range(4):
                        lanes = slice(i * 128, (i + 1) * 128)
                        sown[m, i // 2, i % 2] = jnp.concatenate(
                            [gb_ref[m, :, lanes], ggb_ref[:, m * 128:(m + 1) * 128], jnp.zeros((6, 128), F32)], 0
                        )
            qp_ref[...] = jnp.zeros_like(qp_ref)
            dp_ref[...] = jnp.zeros_like(dp_ref)

        features = pl.ds(pl.multiple_of(step * 128, 128), 128)

        def one_segment(s, carry):
            for p in range(4):
                for i in range(4):
                    hook((p, i), s == min(i, count - 1))
            dk_ref[...] = jnp.zeros_like(dk_ref)
            dv_ref[...] = jnp.zeros_like(dv_ref)
            for block, (first, last) in enumerate(SPANS):
                start = STARTS[block]
                columns = slice(block * BLOCK, (block + 1) * BLOCK)
                mixed_grad = dot_ref[s, :, columns]
                delta = mixed_grad.astype(F32) * ot_ref[s, :, columns].astype(F32)
                delta = jnp.concatenate(
                    [jnp.sum(delta[0:64], axis=0, keepdims=True), jnp.sum(delta[64:128], axis=0, keepdims=True)], 1
                )
                held = dp_ref.at[block]
                diagonal_pair(held, mixed_grad)
                query = qp_ref.at[block]
                diagonal_pair(query, qt_ref[s, :, columns])
                e = e_ref[s, 0, start:start + last - first, :]
                dp = dot(v_ref[s, 0, first:last, :], held[...])
                ds = (e.astype(F32) * (dp - delta)).astype(BF16)
                dv_ref[first:last, :] += dot_nt(e, held[...])
                dk_ref[first:last, :] += dot_nt(ds, query[...])
                dq = dot_tn(k_ref[s, 0, first:last, :], ds) * 0.125
                dqt_ref[s, features, columns] = jnp.concatenate([dq[0:64, 0:128], dq[64:128, 128:256]], 0).astype(BF16)
            dkl_ref[s, step] = dk_ref[...].astype(BF16)
            dvl_ref[s, step] = dv_ref[...].astype(BF16)
            return carry

        lax.fori_loop(0, count, one_segment, 0)
        for p in range(4):
            hook((p, 4))
        gq = dot(dqt_ref[0, features, :], n1_ref[0, 128:, :])
        gkv = dot_tn(n1_ref[0], jnp.concatenate([dkl_ref[0, step], dvl_ref[0, step]], 1))
        for s in range(1, count):
            gq = gq + dot(dqt_ref[s, features, :], n1_ref[s, 128:, :])
            gkv = gkv + dot_tn(n1_ref[s], jnp.concatenate([dkl_ref[s, step], dvl_ref[s, step]], 1))
        both_cores = (2, 16, 16, 128)
        parts = [part.astype(BF16).reshape(16, 2, 16, 128) for part in (gq.T, gkv[:, 0:128], gkv[:, 128:256])]
        for i, part in enumerate(parts):
            for core in range(2):
                gqkv_ref[step, core, :, :, :, i * 16:(i + 1) * 16, :] = part[:, core].reshape(4, 2, 2, 16, 128)
        if ring:
            for p in range(4):

                @pl.when(step == p)
                def _(p=p):
                    both([heads[p]], "stage_share")

    @pl.when(step >= 4)
    def _():
        here = step - 4
        gain = vec_ref[1:2, :]
        dk = jnp.concatenate([dkl_ref[here, p] for p in range(4)], 1)
        dv = jnp.concatenate([dvl_ref[here, p] for p in range(4)], 1)
        grad = dot_nt(dk, attn_ref[1]) + dot_nt(dv, attn_ref[2])
        slot_grad = grad[0:slots]
        kept = mem_ref[0] * keep_ref[0][:, 0:1]
        hat, rstd = norm_parts(kept)
        gmem_ref[0] = (dkept_ref[0] + norm_back(slot_grad, hat, rstd, gain)) * keep_ref[0][:, 0:1]
        grad = grad[128:] + dot_nt(dqt_ref[here].T, attn_ref[0])
        hat, rstd = norm_parts(tok_ref[0].astype(F32))
        gtok_ref[0] = dh_ref[0] + norm_back(grad, hat, rstd, gain)
        for s in range(count):
            hook((4 + s, 0))

        if ring:

            @pl.when(step == 3 + count)
            def _():
                for step_left in rest:
                    step_left()
                fqkv_ref[...] = heads_final[...]
                fo_ref[...] = out_final[...]
                fw1_ref[...] = ffn_final[0]
                fw2_ref[...] = ffn_final[1]


def call_attn_back(
    ring, dh, tokens, memory, keep, n1, qt, k, v, e, ot, mixed_grad, dkept, attn, vec, extra
):
    n, seg, d = tokens.shape
    slots = memory.shape[1]
    shapes = [((n, seg, d), F32), ((n, slots, d), F32)]
    out_specs = [phase_spec((seg, d), 4, n), phase_spec((slots, d), 4, n)]

    def pair_spec(shape, axis):
        return pl.BlockSpec(shape, lambda i: tuple(jnp.minimum(i, 3) if j == axis else 0 for j in range(len(shape))))

    in_specs = [
        pair_spec((n, 128, seg), 1), pair_spec((n, 1, seg + 128, 128), 1), pair_spec((n, 1, seg + 128, 128), 1),
        pair_spec((n, 1, LIVE, 256), 1), pair_spec((n, 128, seg), 1), pair_spec((n, 128, seg), 1),
        phase_spec((seg, d), 4, n), phase_spec((slots, d), 4, n), phase_spec((1, 128), 4, n), phase_spec((slots, d), 4, n),
        phase_spec((seg, d), 4, n),
        full_spec(n1.shape), full_spec((3, d, d)), full_spec(vec.shape),
    ]
    heads = (4, 2, 4, 2, 2, 48, 128)
    scratch = [
        pltpu.VMEM((n, d, seg), BF16), pltpu.VMEM((n, 4, seg + 128, 128), BF16), pltpu.VMEM((n, 4, seg + 128, 128), BF16),
        pltpu.VMEM((seg + 128, 128), F32), pltpu.VMEM((seg + 128, 128), F32), pltpu.VMEM((4, 128, 256), BF16),
        pltpu.VMEM((4, 128, 256), BF16),
    ]
    params = dict(vmem_limit_bytes=VMEM_LIMIT)
    if ring:
        in_specs += [full_spec(extra[0].shape), full_spec(extra[1].shape), ANY, ANY, ANY]
        more = [((4, 2, 48, 128), F32), ((2, 16, d), F32), ((4, 32, d), F32), ((4, 32, d), F32), ((8, 128), F32)]
        scratch += [
            pltpu.VMEM(heads, BF16), pltpu.VMEM((2, 4, 32, d), F32), pltpu.VMEM((2, 16, d), F32),
            pltpu.VMEM((4, 2, 48, 128), F32),
        ]
        scratch += reduce_scratch(8, 32, d // 2) + reduce_scratch(1, 16, d) + reduce_scratch(4, 48, 128)
        scratch += [pltpu.VMEM((4, 2, 2, 8, 128), F32)] * 3 + [
            pltpu.VMEM((4, 2, 8, 128), F32), pltpu.VMEM((7, 8, 128), F32),
            pltpu.SemaphoreType.DMA((6,)), pltpu.SemaphoreType.DMA((6,)),
        ]
        params.update(collective_id=2, has_side_effects=True)
    else:
        more = [(heads, BF16)]
    return pl.pallas_call(
        functools.partial(attn_back_kernel, ring, n),
        grid=(4 + n,),
        out_shape=[jax.ShapeDtypeStruct(shape, kind) for shape, kind in shapes + more],
        in_specs=in_specs,
        out_specs=out_specs + [full_spec(shape) for shape, _ in more],
        scratch_shapes=scratch,
        compiler_params=pltpu.CompilerParams(**params),
        name="attn_back",
    )(qt, k, v, e, ot, mixed_grad, tokens, memory, keep, dkept, dh, n1, attn, vec, *extra)


def hand_out_kernel(
    fqkv_ref, fo_ref, fw1_ref, fw2_ref, fwr_ref, fgate_ref, small_ref, qkv_ref, in_ref, wqkv_ref, gain_ref,
    gqkv_ref, gout_ref, gin_ref, gffn_ref, gwqkv_ref, gwout_ref, ggate_ref, gb_ref, ggb_ref, ggain_ref,
):
    for pair in range(4):
        for core in range(2):
            rows = slice(core * 16, core * 16 + 16)
            for i in range(3):
                gqkv_ref[i, rows, pair * 128:(pair + 1) * 128] = fqkv_ref[pair, core, i * 16:(i + 1) * 16, :]
    for core in range(2):
        gout_ref[core * 16:core * 16 + 16, :] = fo_ref[core]
    for j in range(4):
        gin_ref[:, j * 512:(j + 1) * 512] = fw1_ref[j]
    gffn_ref[...] = fw2_ref[...]
    gwqkv_ref[...] = fwr_ref[0:3]
    gwout_ref[...] = fwr_ref[3]
    ggate_ref[...] = fgate_ref[...]
    gb_ref[...] = small_ref[0:1, :]
    rows = ggb_ref.shape[1]
    place = lax.rem(lax.axis_index("dp"), 4)
    narrow = jnp.zeros((1, rows), F32)
    for i in range(4):
        narrow = narrow + small_ref[1:2, i * rows:(i + 1) * rows] * (place == i).astype(F32)
    ggb_ref[...] = narrow
    sums = [
        jnp.sum(jnp.sum(qkv_ref[...].astype(F32) * gqkv_ref[...], axis=0), axis=-1, keepdims=True),
        jnp.sum(in_ref[...].astype(F32) * gin_ref[...], axis=-1, keepdims=True),
        jnp.sum(jnp.sum(wqkv_ref[...].astype(F32) * gwqkv_ref[...], axis=0), axis=-1, keepdims=True),
    ]
    for i in range(3):
        across = jnp.broadcast_to(sums[i], (rows, 128)).T[0:1, :]
        ggain_ref[i:i + 1, :] = across / gain_ref[i:i + 1, :].astype(F32)


def call_hand_out(*args):
    rows, d = args[2].shape[1:]
    vmem = pl.BlockSpec(memory_space=pltpu.VMEM)
    shapes = [
        (3, rows, d), (rows, d), (rows, 4 * d), (4, rows, d), (3, rows, d), (rows, d), (4, rows // 2, d), (1, 128), (1, rows),
        (3, rows),
    ]
    return pl.pallas_call(
        hand_out_kernel,
        out_shape=[jax.ShapeDtypeStruct(shape, F32) for shape in shapes],
        in_specs=[vmem] * 11,
        out_specs=[vmem] * 10,
        name="hand_out",
    )(*args)


def plain_weights(attn_qkv, attn_out, ffn_in, ffn_out, writer_qkv, writer_out, gate_weight, ffn_bias, gate_bias, gains):
    rows, d = attn_out.shape
    packed = jnp.concatenate(
        [
            attn_qkv, attn_out[None], ffn_in.reshape(rows, 4, d).transpose(1, 0, 2), ffn_out.reshape(4, rows, d),
            writer_qkv, writer_out[None], gate_weight.reshape(2, rows, d),
        ],
        0,
    )
    packed = lax.all_gather(packed, "dp", axis=0)
    n = packed.shape[0]

    def by_rows(first, last):
        return packed[:, first:last].transpose(1, 0, 2, 3).reshape(last - first, n * rows, d)

    small = jnp.concatenate([ffn_bias.reshape(4, rows), gate_bias[None], gains], 0).astype(F32)
    small = lax.all_gather(small, "dp", axis=0)
    b1 = small[:, 0:4].reshape(4, 1, d)
    vec = small.transpose(1, 0, 2).reshape(8, d)
    vec = jnp.concatenate([vec[4:8], jnp.zeros((4, d), F32)], 0)
    w2 = packed[:, 8:12].reshape(4, d, d)
    return by_rows(0, 4), by_rows(4, 8), w2, by_rows(12, 16), packed[:, 16:18].reshape(2, d, d), vec, b1


def plain_grads(rows, attn_qkv, ffn_in, writer_qkv, gains, gattn, gw1, gw2, gwr, ggate, gb, ggb):
    d = gattn.shape[-1]
    n = d // rows

    def by_rows(grad):
        return grad.reshape(-1, n, rows, d).transpose(1, 0, 2, 3)

    packed = jnp.concatenate(
        [by_rows(gattn), by_rows(gw1), gw2.reshape(n, 4, rows, d), by_rows(gwr), ggate.reshape(n, 2, rows, d)], 1
    )
    owned = lax.psum_scatter(packed.astype(F32), "dp", scatter_dimension=0, tiled=False)
    owned = lax.psum(owned.astype(BF16), "outer").astype(F32)
    small = jnp.concatenate([gb.reshape(n, 4 * rows), ggb.reshape(n, rows)], 1)
    small = lax.psum(lax.psum_scatter(small, "dp", scatter_dimension=0, tiled=False), "outer")
    gin = owned[4:8].transpose(1, 0, 2).reshape(rows, 4 * d)
    ggains = jnp.stack(
        [
            jnp.sum(attn_qkv.astype(F32) * owned[0:3], (0, 2)), jnp.sum(ffn_in.astype(F32) * gin, 1),
            jnp.sum(writer_qkv.astype(F32) * owned[12:15], (0, 2)),
        ]
    )
    return (
        owned[0:3], owned[3], gin, owned[8:12].reshape(4 * rows, d), owned[12:15], owned[15], owned[16:18].reshape(2 * rows, d),
        small[0:4 * rows], small[4 * rows:], ggains / gains.astype(F32),
    )


def body(
    tokens, memory, doc_ids, resets, out_grad, memory_grad,
    attn_qkv, attn_out, ffn_in, ffn_bias, ffn_out, writer_qkv, writer_out, gate_weight, gate_bias, gains,
):
    micro, segs, seg, d = tokens.shape
    slots = memory.shape[2]
    rows = attn_out.shape[0]
    n = micro * segs
    ring = lax.axis_size("dp") == 16 and lax.axis_size("outer") == 2 and rows == 32
    tokens, out_grad = tokens.reshape(n, seg, d), out_grad.reshape(n, seg, d)
    memory, memory_grad = memory.reshape(n, slots, d), memory_grad.reshape(n, slots, d)
    docs = doc_ids.reshape(n, 1, seg)
    keep = jnp.broadcast_to((1 - resets).astype(F32).reshape(n, 1, 1), (n, 1, 128))
    if ring:
        weights = (
            attn_qkv, attn_out, ffn_in, ffn_out.reshape(4, rows, d), writer_qkv, writer_out,
            gate_weight.reshape(4, rows // 2, d), ffn_bias.reshape(1, 4 * rows), gate_bias.reshape(1, rows), gains,
        )
    else:
        attn, w1, w2, wr, gate, vec, b1 = plain_weights(
            attn_qkv, attn_out, ffn_in, ffn_out, writer_qkv, writer_out, gate_weight, ffn_bias, gate_bias, gains
        )
        units = (4, 4, 2, 2, 32, d)
        weights = (attn.reshape(units), w1.reshape(units), w2.reshape(4, 2, 2, 4, 32, d), vec, b1)
    n1, qt, k, v, e, linv, ot, h1, out, res, act, slope, vec, *whole = call_forward(ring, tokens, memory, docs, keep, weights)
    if ring:
        attn, w1, w2, wr = (array.reshape(4, d, d) for array in whole[:4])
        gate = whole[4].reshape(2, d, d)
    new_memory, dkept, ggb, gb, gw1, gw2, gwo, dh, mixed_grad, gwr, ggate = call_ffn_back(
        ring, res, memory, memory_grad, docs, keep, wr, gate, vec, out_grad, h1, act, slope, ot, linv, w1, w2, attn
    )
    extra = ()
    if ring:
        extra = (ggb, gb, gw1.reshape(4, 4, 2, 2, 32, d), gw2.reshape(4, 2, 2, 4, 32, d), gwo.reshape(4, 2, 2, 2, 16, d))
    grad_tokens, grad_memory, *rest = call_attn_back(
        ring, dh, tokens, memory, keep, n1, qt, k, v, e, ot, mixed_grad, dkept, attn, vec, extra
    )
    if ring:
        grads = call_hand_out(*rest[:4], gwr, ggate, rest[4], attn_qkv, ffn_in, writer_qkv, gains)
    else:
        (heads,) = rest
        gattn = heads.reshape(4, 2, 16, 3, 16, 128).transpose(3, 2, 1, 4, 0, 5).reshape(3, d, d)
        gattn = jnp.concatenate([gattn, gwo[None]], 0)
        grads = plain_grads(rows, attn_qkv, ffn_in, writer_qkv, gains, gattn, gw1, gw2, gwr, ggate, gb, ggb)
    gqkv, gout, gin, gffn, gwqkv, gwout, ggw, gb, ggb, ggains = grads
    return (
        out.reshape(micro, segs, seg, d), new_memory.reshape(micro, segs, slots, d),
        grad_tokens.reshape(micro, segs, seg, d), grad_memory.reshape(micro, segs, slots, d),
        gqkv, gout, gin, gb.reshape(4 * rows), gffn.reshape(4 * rows, d), gwqkv, gwout, ggw.reshape(2 * rows, d),
        ggb.reshape(rows), ggains,
    )


def solution(mesh):
    split = ("dp", "outer")
    whole = P(None, split, None, None)
    weights = (
        P(None, "dp", None), P("dp", None), P("dp", None), P("dp"), P("dp", None), P(None, "dp", None),
        P("dp", None), P("dp", None), P("dp"), P(None, "dp"),
    )
    return jax.shard_map(
        body,
        mesh=mesh,
        in_specs=(whole, whole, P(None, split, None), P(None, split), whole, whole) + weights,
        out_specs=(whole, whole, whole, whole) + weights,
        check_vma=False,
    )
```

```python
import functools

import jax
import jax.numpy as jnp
from jax import lax
from jax.experimental import pallas as pl
from jax.experimental.pallas import tpu as pltpu
from jax.sharding import PartitionSpec as P

HEADS = 8
BLOCK = 128
SPANS = ((0, 256), (0, 384), (128, 512), (256, 640))
STARTS = (0, 256, 640, 1024)
LIVE = 1408
F32 = jnp.float32
BF16 = jnp.bfloat16
VMEM_LIMIT = 60 * 1024 * 1024


def dot(a, b):
    return jnp.dot(a, b, preferred_element_type=F32)


def dot_nt(a, b):
    return lax.dot_general(a, b, (((1,), (1,)), ((), ())), preferred_element_type=F32)


def dot_tn(a, b):
    return lax.dot_general(a, b, (((0,), (0,)), ((), ())), preferred_element_type=F32)


def norm_parts(rows):
    centred = rows - jnp.mean(rows, axis=-1, keepdims=True)
    rstd = lax.rsqrt(jnp.mean(centred * centred, axis=-1, keepdims=True) + 1e-05)
    return centred * rstd, rstd


def norm_back(grad, hat, rstd, gain):
    scaled = grad * gain
    return rstd * (
        scaled
        - jnp.mean(scaled, axis=-1, keepdims=True)
        - hat * jnp.mean(scaled * hat, axis=-1, keepdims=True)
    )


def diagonal_pair(ref, top):
    ref[0:64, 0:128] = top[0:64]
    ref[64:128, 128:256] = top[64:128]


MESH = pl.DeviceIdType.MESH
EVERY = slice(None)


class Place:
    def __init__(self):
        self.dp = lax.axis_index("dp")
        self.core = lax.axis_index("outer")
        self.z, self.y, self.x = self.dp // 4, (self.dp // 2) % 2, self.dp % 2

    def sibling(self):
        return (self.dp, 1 - self.core)

    def along_x(self):
        return (self.dp + 1 - 2 * self.x, self.core)

    def along_y(self):
        return (self.dp + 2 - 4 * self.y, self.core)

    def other_z(self, shift):
        return lax.rem(self.z + shift, 4)

    def along_z(self, shift):
        return (self.dp + 4 * (self.other_z(shift) - self.z), self.core)

    def greet(self):
        barrier = pltpu.get_barrier_semaphore()
        everyone = [self.sibling(), self.along_x(), self.along_y()] + [self.along_z(shift) for shift in (1, 2, 3)]
        for device in everyone:
            pl.semaphore_signal(barrier, inc=1, device_id=device, device_id_type=MESH)
        pl.semaphore_wait(barrier, len(everyone))


class Travel:
    def __init__(self, place, send, recv):
        self.place, self.send, self.recv = place, send, recv

    def copy(self, stage, src, dst, device):
        return pltpu.make_async_remote_copy(
            src_ref=src, dst_ref=dst, send_sem=self.send.at[stage], recv_sem=self.recv.at[stage], device_id=device,
            device_id_type=MESH,
        )

    def go(self, stage, src, dst, device):
        self.copy(stage, src, dst, device).start()

    def arrived(self, stage, dst):
        self.copy(stage, dst, dst, self.place.sibling()).wait_recv()

    def left(self, stage, src):
        self.copy(stage, src, src, self.place.sibling()).wait_send()


class Gather(Travel):
    def __init__(self, place, view, own, lane, send, recv, local):
        super().__init__(place, send, recv)
        self.view, self.own, self.lane, self.local = view, own, lane, local
        self.unit = 2 * place.core + lane

    def mine(self):
        at = self.place
        return self.view(self.unit, at.z, at.y, at.x)

    def stage_z(self):
        at = self.place
        pltpu.make_async_copy(self.own(self.unit), self.mine(), self.local).start()
        for shift in (1, 2, 3):
            self.go(shift - 1, self.own(self.unit), self.mine(), at.along_z(shift))

    def wait_z(self):
        at = self.place
        pltpu.make_async_copy(self.own(self.unit), self.mine(), self.local).wait()
        for shift in (1, 2, 3):
            self.arrived(shift - 1, self.view(self.unit, at.other_z(4 - shift), at.y, at.x))

    def column(self, far):
        at = self.place
        if self.lane:
            return self.view(self.unit, EVERY, 1 - at.y if far else at.y, at.x)
        return self.view(self.unit, EVERY, at.y, 1 - at.x if far else at.x)

    def half(self, unit, far):
        at = self.place
        if self.lane:
            return self.view(unit, EVERY, EVERY, 1 - at.x if far else at.x)
        return self.view(unit, EVERY, 1 - at.y if far else at.y, EVERY)

    def stage_first(self):
        part = self.column(False)
        self.go(3, part, part, self.place.along_y() if self.lane else self.place.along_x())

    def wait_first(self):
        self.arrived(3, self.column(True))

    def stage_second(self):
        part = self.half(self.unit, False)
        self.go(4, part, part, self.place.along_x() if self.lane else self.place.along_y())
        self.go(5, part, part, self.place.sibling())

    def wait_second(self):
        self.arrived(4, self.half(self.unit, True))

    def stage_share(self):
        part = self.half(self.unit, True)
        self.go(6, part, part, self.place.sibling())

    def wait_share(self):
        other = 2 * (1 - self.place.core) + self.lane
        self.arrived(5, self.half(other, False))
        self.arrived(6, self.half(other, True))

    def finish(self):
        for stage in range(3):
            self.left(stage, self.own(self.unit))
        self.left(3, self.column(False))
        self.left(4, self.half(self.unit, False))
        self.left(5, self.half(self.unit, False))
        self.left(6, self.half(self.unit, True))


class FirstGather(Travel):
    SHIFTS = (0, 3, 1, 2)

    def __init__(self, place, view, own, lane, send, recv, local):
        super().__init__(place, send, recv)
        self.view, self.own, self.lane, self.local = view, own, lane, local
        self.unit = 2 * place.core + lane

    def part(self, unit, z, far_first, far_second):
        at = self.place
        far_x, far_y = (far_second, far_first) if self.lane else (far_first, far_second)
        return self.view(unit, z, 1 - at.y if far_y else at.y, 1 - at.x if far_x else at.x)

    def block(self, shift, far_first, far_second):
        return self.part(self.unit, self.place.other_z(4 - shift), far_first, far_second)

    def first_partner(self):
        return self.place.along_y() if self.lane else self.place.along_x()

    def second_partner(self):
        return self.place.along_x() if self.lane else self.place.along_y()

    def keep(self):
        return pltpu.make_async_copy(self.own(self.unit), self.block(0, False, False), self.local)

    def begin(self):
        mine = self.own(self.unit)
        there = self.block(0, False, False)
        for shift in (3, 1, 2):
            self.go(shift - 1, mine, there, self.place.along_z(shift))
        self.go(4, mine, there, self.first_partner())
        self.go(8, mine, there, self.second_partner())
        self.keep().start()

    def column_block(self, shift):
        here = self.block(shift, False, False)
        self.arrived(shift - 1, here)
        self.go(4 + shift, here, here, self.first_partner())
        self.go(8 + shift, here, here, self.second_partner())

    def column_done(self):
        self.keep().wait()
        self.share(0, False, False)

    def share(self, index, far_first, far_second):
        part = self.part(self.unit, EVERY, far_first, far_second)
        self.go(16 + index, part, part, self.place.sibling())

    def far_block(self, shift):
        here = self.block(shift, True, False)
        self.arrived(4 + shift, here)
        self.go(12 + shift, here, here, self.second_partner())

    def far_done(self):
        self.share(1, True, False)
        for shift in self.SHIFTS:
            self.arrived(8 + shift, self.block(shift, False, True))
        self.share(2, False, True)

    def rest(self):
        for shift in self.SHIFTS:
            self.arrived(12 + shift, self.block(shift, True, True))
        self.share(3, True, True)

    def done(self):
        other = 2 * (1 - self.place.core) + self.lane
        for index, (far_first, far_second) in enumerate(((False, False), (True, False), (False, True), (True, True))):
            self.arrived(16 + index, self.part(other, EVERY, far_first, far_second))

    def finish(self):
        for stage in range(3):
            self.left(stage, self.own(self.unit))
        for leg in (4, 8):
            self.left(leg, self.own(self.unit))
            for shift in (1, 2, 3):
                self.left(leg + shift, self.block(shift, False, False))
        for shift in range(4):
            self.left(12 + shift, self.block(shift, True, False))
        for index, (far_first, far_second) in enumerate(((False, False), (True, False), (False, True), (True, True))):
            self.left(16 + index, self.part(self.unit, EVERY, far_first, far_second))


class GatherSmall(Travel):
    def __init__(self, place, ref, own, send, recv):
        super().__init__(place, send, recv)
        self.ref, self.own = ref, own

    def stage_z(self):
        at = self.place
        self.ref[at.z, at.y, at.x] = self.own[...]
        for shift in (1, 2, 3):
            self.go(shift - 1, self.own, self.ref.at[at.z, at.y, at.x], at.along_z(shift))

    def wait_z(self):
        at = self.place
        for shift in (1, 2, 3):
            self.arrived(shift - 1, self.ref.at[at.other_z(4 - shift), at.y, at.x])

    def stage_first(self):
        at = self.place
        part = self.ref.at[:, at.y, at.x]
        self.go(3, part, part, at.along_x())

    def wait_first(self):
        at = self.place
        self.arrived(3, self.ref.at[:, at.y, 1 - at.x])

    def stage_second(self):
        at = self.place
        part = self.ref.at[:, at.y]
        self.go(4, part, part, at.along_y())

    def wait_second(self):
        at = self.place
        self.arrived(4, self.ref.at[:, 1 - at.y])

    def finish(self):
        at = self.place
        for stage in range(3):
            self.left(stage, self.own)
        self.left(3, self.ref.at[:, at.y, at.x])
        self.left(4, self.ref.at[:, at.y])


def unit_first(ref):
    return lambda u, z, y, x: ref.at[u, z, y, x]


def unit_last(ref):
    return lambda u, z, y, x: ref.at[z, y, x, u]


class Reduce(Travel):
    def __init__(self, place, own, other, lane, acc, wide, mid, narrow, final, final_other, send, recv, local):
        super().__init__(place, send, recv)
        self.own, self.other, self.lane, self.local = own, other, lane, local
        self.acc, self.wide, self.mid, self.narrow = acc, wide, mid, narrow
        self.final, self.final_other = final, final_other

    def stage_share(self):
        self.go(0, self.other, self.wide, self.place.sibling())
        pltpu.make_async_copy(self.own, self.acc, self.local).start()

    def wait_share(self):
        pltpu.make_async_copy(self.own, self.acc, self.local).wait()
        self.arrived(0, self.wide)

        def add(z, carry):
            self.acc[z] = self.acc[z] + self.wide[z]
            return carry

        lax.fori_loop(0, 4, add, 0)

    def half(self, far):
        at = self.place
        if self.lane:
            return self.acc.at[:, :, 1 - at.x if far else at.x]
        return self.acc.at[:, 1 - at.y if far else at.y]

    def stage_first(self):
        at = self.place
        self.go(1, self.half(True), self.mid, at.along_x() if self.lane else at.along_y())

    def wait_first(self):
        at = self.place
        self.arrived(1, self.mid)

        def add(z, carry):
            for i in range(2):
                part = self.acc.at[z, i, at.x] if self.lane else self.acc.at[z, at.y, i]
                part[...] = part[...] + self.mid[z, i]
            return carry

        lax.fori_loop(0, 4, add, 0)

    def quarter(self):
        at = self.place
        if self.lane:
            return self.acc.at[:, 1 - at.y, at.x]
        return self.acc.at[:, at.y, 1 - at.x]

    def stage_second(self):
        self.go(2, self.quarter(), self.narrow.at[0:4], self.place.along_y() if self.lane else self.place.along_x())

    def wait_second(self):
        at = self.place
        self.arrived(2, self.narrow.at[0:4])
        part = self.acc.at[:, at.y, at.x]
        part[...] = part[...] + self.narrow[0:4]

    def block(self, shift):
        at = self.place
        return self.acc.at[at.other_z(shift), at.y, at.x]

    def stage_z(self):
        for shift in (1, 2, 3):
            self.go(2 + shift, self.block(shift), self.narrow.at[3 + shift], self.place.along_z(shift))

    def wait_z(self):
        total = self.block(0)[...].astype(F32)
        for shift in (1, 2, 3):
            self.arrived(2 + shift, self.narrow.at[3 + shift])
            total = total + self.narrow[3 + shift].astype(F32)
        self.final[...] = total

    def stage_final(self):
        self.go(6, self.final, self.final, self.place.sibling())

    def wait_final(self):
        self.arrived(6, self.final_other)
        self.left(0, self.other)
        self.left(1, self.half(True))
        self.left(2, self.quarter())
        for shift in (1, 2, 3):
            self.left(2 + shift, self.block(shift))
        self.left(6, self.final)


class ReduceSmall(Travel):
    def __init__(self, place, own, acc, wide, mid, narrow, final, send, recv):
        super().__init__(place, send, recv)
        self.own, self.acc, self.wide, self.mid, self.narrow, self.final = own, acc, wide, mid, narrow, final

    def stage_share(self):
        self.go(0, self.own, self.wide, self.place.sibling())

    def wait_share(self):
        self.arrived(0, self.wide)
        self.acc[...] = self.own[...] + self.wide[...]

    def stage_first(self):
        at = self.place
        self.go(1, self.acc.at[:, 1 - at.y], self.mid, at.along_y())

    def wait_first(self):
        at = self.place
        self.arrived(1, self.mid)
        half = self.acc.at[:, at.y]
        half[...] = half[...] + self.mid[...]

    def stage_second(self):
        at = self.place
        self.go(2, self.acc.at[:, at.y, 1 - at.x], self.narrow.at[0:4], at.along_x())

    def wait_second(self):
        at = self.place
        self.arrived(2, self.narrow.at[0:4])
        part = self.acc.at[:, at.y, at.x]
        part[...] = part[...] + self.narrow[0:4]

    def block(self, shift):
        at = self.place
        return self.acc.at[at.other_z(shift), at.y, at.x]

    def stage_z(self):
        for shift in (1, 2, 3):
            self.go(2 + shift, self.block(shift), self.narrow.at[3 + shift], self.place.along_z(shift))

    def wait_z(self):
        at = self.place
        total = self.block(0)[...]
        for shift in (1, 2, 3):
            self.arrived(2 + shift, self.narrow.at[3 + shift])
            total = total + self.narrow[3 + shift]
        self.final[...] = total
        self.left(0, self.own)
        self.left(1, self.acc.at[:, 1 - at.y])
        self.left(2, self.acc.at[:, at.y, 1 - at.x])
        for shift in (1, 2, 3):
            self.left(2 + shift, self.block(shift))


def reduce_scratch(count, rows, d):
    return [
        pltpu.VMEM((count, 4, 2, 2, rows, d), BF16), pltpu.VMEM((count, 4, 2, 2, rows, d), BF16),
        pltpu.VMEM((count, 4, 2, rows, d), BF16), pltpu.VMEM((count, 7, rows, d), BF16),
        pltpu.SemaphoreType.DMA((count, 7)), pltpu.SemaphoreType.DMA((count, 7)), pltpu.SemaphoreType.DMA((count,)),
    ]


def reduce_unit(place, grad, scratch, index, lane, final, unit, other, columns=None):
    acc, wide, mid, narrow, send, recv, local = scratch
    own, theirs = grad(unit, EVERY, EVERY, EVERY), grad(other, EVERY, EVERY, EVERY)
    final_own, final_other = final.at[unit], final.at[other]
    if columns is not None:
        own, theirs = own.at[:, :, :, :, columns], theirs.at[:, :, :, :, columns]
        final_own, final_other = final_own.at[:, columns], final_other.at[:, columns]
    return Reduce(
        place, own, theirs, lane, acc.at[index], wide.at[index], mid.at[index], narrow.at[index], final_own, final_other,
        send.at[index], recv.at[index], local.at[index],
    )


def reduce_round(place, grad, scratch, index, final, columns=None):
    return [
        reduce_unit(
            place, grad, scratch, index + l, l, final, 2 * place.core + l, 2 * (1 - place.core) + l, columns
        )
        for l in range(2)
    ]


def both(lanes, *names):
    for name in names:
        for lane in lanes:
            getattr(lane, name)()


REDUCE_STEPS = (
    ("stage_share",), ("wait_share", "stage_first"), ("wait_first", "stage_second"), ("wait_second", "stage_z"),
    ("wait_z", "stage_final"), ("wait_final",),
)
GATHER_STEPS = (
    ("stage_z",), ("wait_z", "stage_first"), ("wait_first", "stage_second"), ("wait_second", "stage_share"), ("wait_share",),
)


def job(lanes, steps):
    return [lambda names=names: both(lanes, *names) for names in steps]


def plan(jobs, places):
    found, late = {}, []
    for number, (steps, start, spans, *latest) in enumerate(jobs):
        time = start
        allowed = places[:places.index(latest[0]) + 1] if latest else places
        for i, step in enumerate(steps):
            fitting = [place for place in allowed if place[1] >= time] or allowed[-1:] * len(latest)
            if fitting:
                name, time = fitting[0]
                found.setdefault(name, []).append(step)
            else:
                late.append((time, number, step))
            time = time + (spans[i] if i < len(spans) else 0.0)
    return found, [step for _, _, step in sorted(late, key=lambda entry: entry[:2])]


def hook_in(found, name, condition):
    if name in found:

        @pl.when(condition)
        def _():
            for step in found[name]:
                step()


GATHER_PACE = 9.5
GATHER_SPANS = (6.0, 7.0, 10.0, 4.0)
PASS_TIME, PASS_TIMES = 8.5, (1.5, 3.0, 4.5, 6.0, 7.5, 8.5)
FFN_TIME = 5.0
FFN_BACK_TIME = 6.0
REDUCE_SPANS = (4.0, 8.0, 6.0, 8.0, 3.0)
SLIM_SPANS = (3.0, 6.0, 5.0, 6.0, 3.0)
HALVES = (slice(0, 256), slice(256, 512))
HEADS_TIME, HEADS_TIMES = 8.0, (0.0, 1.7, 3.4, 5.1, 6.8)
LAST_TIME = 2.0
FFN_REDUCE_PACE = 4.5
WRITER_SPANS = (8.0, 6.0, 8.0, 3.0)
WRITER_PACE = 3.0


def matrix(block):
    return block.reshape(-1, block.shape[-1])


def forward_kernel(ring, count, *refs):
    refs = list(refs)

    def take(number):
        out = refs[:number]
        del refs[:number]
        return out

    tok_ref, mem_ref, doc_ref, keep_ref = take(4)
    if ring:
        shards = take(7)
        narrow_refs = take(3)
    else:
        attn_ref, w1_ref, w2_ref, vec_in_ref, b1_in_ref = take(5)
    n1_ref, qt_ref, k_ref, v_ref, e_ref, linv_ref, ot_ref, h1_ref, out_ref, res_ref, act_ref, slope_ref, vec_ref = take(13)
    if ring:
        attn_ref, w1_ref, w2_ref, wr_ref, gate_ref = take(5)
    bias_ref, vt_ref, hidden_ref, b1_ref, attn_v, w1_v, w2_v, wsem = take(8)
    seg = tok_ref.shape[1]
    slots = mem_ref.shape[1]
    step = pl.program_id(0)
    load_attn = lambda: pltpu.make_async_copy(attn_ref, attn_v, wsem.at[0])
    load_w1 = lambda: pltpu.make_async_copy(w1_ref, w1_v, wsem.at[1])
    load_w2 = lambda: pltpu.make_async_copy(w2_ref, w2_v, wsem.at[2])
    if ring:
        units, psem, sown_ref, sall_ref, send, recv, local, ssend, srecv, fsend, frecv = take(11)
        place = Place()
        views = [unit_first(attn_ref), unit_first(w1_ref), unit_last(w2_ref), unit_first(wr_ref), unit_last(gate_ref)]
        rounds = []
        for r, view in enumerate(views):
            own = (lambda u: shards[6].at[u]) if r == 4 else (lambda u, r=r: units.at[4 * r + u])
            if r == 0:
                lanes = [
                    FirstGather(place, unit_first(attn_v), own, l, fsend.at[l], frecv.at[l], local.at[r, l]) for l in range(2)
                ]
            else:
                lanes = [Gather(place, view, own, l, send.at[r, l], recv.at[r, l], local.at[r, l]) for l in range(2)]
            rounds.append(lanes)
        small = GatherSmall(place, sall_ref, sown_ref, ssend, srecv)
        packs = [(shards[0], units.at[0:3]), (shards[1], units.at[3])]
        packs += [(shards[2].at[:, j * 512:(j + 1) * 512], units.at[4 + j]) for j in range(4)]
        packs += [(shards[3], units.at[8:12]), (shards[4], units.at[12:15]), (shards[5], units.at[15])]

        def pack(i):
            return pltpu.make_async_copy(packs[i][0], packs[i][1], psem.at[i])

        passes = [((s, i), PASS_TIME * s + PASS_TIMES[i]) for s in range(count) for i in range(len(PASS_TIMES))]
        jobs = []
        for r in range(1, 5):
            steps = job(rounds[r], GATHER_STEPS)
            if r in (1, 2):
                share = steps[-1]
                load = load_w1 if r == 1 else load_w2
                steps[-1] = lambda share=share, load=load: (share(), load().start())
            latest = (passes[-1],) if r in (1, 2) else ()
            if r == 1:
                jobs.append((steps[1:], 0.0, GATHER_SPANS[1:]) + latest)
            else:
                jobs.append((steps, GATHER_PACE * (r - 1) - GATHER_SPANS[0], GATHER_SPANS) + latest)
        places = list(passes)
        at_load = PASS_TIME * count
        places += [((count + s, i), at_load + FFN_TIME * (s + i / 4)) for s in range(count) for i in range(4)]
        found, rest = plan(jobs, places)

    def hook(name, extra=True):
        if ring:
            hook_in(found, name, (step == name[0]) & extra)

    @pl.when(step < count)
    def _():
        if ring:

            @pl.when(step == 0)
            def _():
                for i in range(len(packs)):
                    pack(i).start()
                bias, gbias, gains = (ref[...].astype(F32) for ref in narrow_refs)
                narrow = jnp.concatenate([gbias, gains], 0)
                lane = lax.broadcasted_iota(jnp.int32, (4, 128), 1) // narrow.shape[1]
                narrow = jnp.where(lane == lax.rem(place.dp, 4), jnp.concatenate([narrow] * 4, 1), 0.0)
                sown_ref[...] = jnp.concatenate([bias, narrow, jnp.zeros((3, 128), F32)], 0)
                place.greet()
                small.stage_z()
                pack(0).wait()
                pack(1).wait()
                both(rounds[0], "begin")
                for i in range(2, len(packs)):
                    pack(i).wait()
        else:

            @pl.when(step == 0)
            def _():
                load_attn().start()
                load_w1().start()
                load_w2().start()
                vec_ref[...] = vec_in_ref[...]
                b1_ref[...] = b1_in_ref[...]
                load_attn().wait()

        keep = keep_ref[0][:, 0:1]
        docs = doc_ref[0].astype(F32)
        key_docs = jnp.broadcast_to(docs, (128, seg)).T
        slot_docs = jnp.broadcast_to(keep - 1.0, (slots, 128))
        key_docs = jnp.concatenate([slot_docs, jnp.full((128 - slots, 128), -1.0, F32), key_docs], 0)
        for block, (first, last_row) in enumerate(SPANS):
            length = last_row - first
            position = lax.broadcasted_iota(jnp.int32, (length, BLOCK), 0) + (first - 128 - block * BLOCK)
            position = position <= lax.broadcasted_iota(jnp.int32, (length, BLOCK), 1)
            same = key_docs[first:last_row] == docs[:, block * BLOCK:(block + 1) * BLOCK]
            bias_ref[STARTS[block]:STARTS[block] + length, :] = jnp.where(same & position, 0.0, -1e30)
        if ring:

            @pl.when(step == 0)
            def _():
                small.wait_z()
                small.stage_first()
                for shift in FirstGather.SHIFTS[1:]:
                    for lane in rounds[0]:
                        lane.column_block(shift)
                both(rounds[0], "column_done")
                small.wait_first()
                small.stage_second()
                for shift in FirstGather.SHIFTS:
                    for lane in rounds[0]:
                        lane.far_block(shift)
                both(rounds[1], "stage_z")
                both(rounds[0], "far_done")
                small.wait_second()
                for m in range(4):
                    total = sall_ref[m, 0, 0] + sall_ref[m, 0, 1] + sall_ref[m, 1, 0] + sall_ref[m, 1, 1]
                    vec_ref[:, m * 128:(m + 1) * 128] = jnp.concatenate([total[1:8], total[0:1]], 0)
                    for i in range(4):
                        b1_ref[m, :, i * 128:(i + 1) * 128] = sall_ref[m, i // 2, i % 2, 0:1, :]
                both(rounds[0], "rest")
                both(rounds[0], "done")
                pltpu.make_async_copy(attn_v, attn_ref, wsem.at[0]).start()

        x = tok_ref[0].astype(F32)
        gain_one = vec_ref[1:2, :]
        hat, _ = norm_parts(x)
        n1t = (hat * gain_one).astype(BF16)
        hat, _ = norm_parts(mem_ref[0] * keep)
        n1_ref[0, 0:slots, :] = (hat * gain_one).astype(BF16)
        n1_ref[0, slots:128, :] = jnp.zeros((128 - slots, x.shape[1]), BF16)
        n1_ref[0, 128:, :] = n1t
        qt_ref[0] = (dot_nt(matrix(attn_v[0]).T, n1t) * 0.125).astype(BF16)
        n1 = n1_ref[0]
        keys = dot(n1, matrix(attn_v[1])).astype(BF16)
        v = dot(n1, matrix(attn_v[2])).astype(BF16)
        for pair in range(4):
            k_ref[0, pair] = keys[:, pair * 128:(pair + 1) * 128]
            v_ref[0, pair] = v[:, pair * 128:(pair + 1) * 128]
        vt_ref[...] = v.T
        for s in range(count):
            hook((s, 0))

        def one_pair(pair, carry):
            lanes = pl.ds(pl.multiple_of(pair * 128, 128), 128)
            for block, (first, last_row) in enumerate(SPANS):
                start = STARTS[block] - first
                columns = pl.ds(block * BLOCK, BLOCK)
                query = qt_ref[0, lanes, columns]
                zero = jnp.zeros((64, BLOCK), BF16)
                query = jnp.concatenate(
                    [jnp.concatenate([query[0:64], zero], 1), jnp.concatenate([zero, query[64:128]], 1)], 0
                )
                scores, largest = [], None
                for row in range(first, last_row, 128):
                    bias = bias_ref[start + row:start + row + 128, :]
                    part = dot(k_ref[0, pair, row:row + 128, :], query) + jnp.concatenate([bias, bias], 1)
                    scores.append(part)
                    part = jnp.max(part.reshape(16, 8, 256), axis=0)
                    largest = part if largest is None else jnp.maximum(largest, part)
                largest = jnp.max(largest, axis=0, keepdims=True)
                es, total = [], None
                for i, row in enumerate(range(first, last_row, 128)):
                    e = jnp.exp(scores[i] - largest)
                    part = jnp.sum(e.reshape(16, 8, 256), axis=0)
                    total = part if total is None else total + part
                    es.append(e.astype(BF16))
                    e_ref[0, pair, start + row:start + row + 128, :] = es[-1]
                linv = 1.0 / jnp.sum(total, axis=0, keepdims=True)
                linv_ref[0, pair, block, :, :] = linv
                e = jnp.concatenate(es, 0)
                values = vt_ref[lanes, first:last_row]
                mixed = [
                    dot(values[i * 64:(i + 1) * 64], e[:, i * 128:(i + 1) * 128]) * linv[:, i * 128:(i + 1) * 128]
                    for i in range(2)
                ]
                ot_ref[0, lanes, columns] = jnp.concatenate(mixed, 0).astype(BF16)
            for s in range(count):
                for i in range(4):
                    hook((s, 1 + i), pair == i)
            return carry

        lax.fori_loop(0, 4, one_pair, 0)
        h1 = x + dot(ot_ref[0].T, matrix(attn_v[3]))
        h1_ref[0] = h1
        hidden_ref[step] = h1
        for s in range(count):
            hook((s, 5))

    @pl.when(step >= count)
    def _():
        @pl.when(step == count)
        def _():
            load_w1().wait()
            load_w2().wait()

        h1 = hidden_ref[step - count]
        hat, _ = norm_parts(h1)
        n2 = (hat * vec_ref[2:3, :]).astype(BF16)
        tall = seg // 2
        for block in range(2):
            rows = slice(block * tall, (block + 1) * tall)
            result = h1[rows]
            for part in range(8):
                columns = slice((part % 2) * 256, (part % 2) * 256 + 256)
                before = dot(n2[rows], matrix(w1_v[part // 2])[:, columns]) + b1_ref[part // 2][:, columns]
                cdf = 0.5 + 0.5 * lax.erf(before * 0.7071067811865476)
                active = (before * cdf).astype(BF16)
                act_ref[0, part // 2, rows, columns] = active
                slope = cdf + before * jnp.exp(before * before * -0.5) * 0.3989422804014327
                slope_ref[0, part // 2, rows, columns] = slope.astype(BF16)
                result = result + dot(active, matrix(w2_v[part // 2])[columns, :])
                if part in (3, 7):
                    for s in range(count, 2 * count):
                        hook((s, 2 * block + (part == 7)))
            out_ref[0, rows, :] = result.astype(BF16)
        res_ref[0] = result
        if ring:

            @pl.when(step == 2 * count - 1)
            def _():
                pltpu.make_async_copy(attn_v, attn_ref, wsem.at[0]).wait()
                for step_left in rest:
                    step_left()
                for lanes in rounds:
                    both(lanes, "finish")
                small.finish()


ANY = pl.BlockSpec(memory_space=pl.ANY)


def full_spec(shape):
    return pl.BlockSpec(shape, lambda i: (0,) * len(shape), pipeline_mode=pl.Buffered(1))


def phase_spec(shape, first, count):
    return pl.BlockSpec((1,) + shape, lambda i: (jnp.clip(i - first, 0, count - 1),) + (0,) * len(shape))


def call_forward(ring, tokens, memory, docs, keep, weights):
    n, seg, d = tokens.shape
    slots = memory.shape[1]
    early = [
        ((seg + 128, d), BF16), ((d, seg), BF16), ((4, seg + 128, 128), BF16), ((4, seg + 128, 128), BF16), ((4, LIVE, 256), BF16),
        ((4, 4, 1, 256), F32), ((d, seg), BF16), ((seg, d), F32),
    ]
    late = [((seg, d), BF16), ((seg // 2, d), F32), ((4, seg, 512), BF16), ((4, seg, 512), BF16)]
    units = (4, 4, 2, 2, 32, d)
    unit_shapes = [units, units, (4, 2, 2, 4, 32, d), units, (4, 2, 2, 4, 16, d)]
    out_shape = [jax.ShapeDtypeStruct((n,) + shape, kind) for shape, kind in early + late]
    out_shape += [jax.ShapeDtypeStruct((8, d), F32)]
    out_specs = [phase_spec(shape, 0, n) for shape, _ in early] + [phase_spec(shape, n, n) for shape, _ in late]
    out_specs += [full_spec((8, d))]
    in_specs = [phase_spec((seg, d), 0, n), phase_spec((slots, d), 0, n), phase_spec((1, seg), 0, n), phase_spec((1, 128), 0, n)]
    scratch = [
        pltpu.VMEM((LIVE, 128), F32), pltpu.VMEM((d, seg + 128), BF16), pltpu.VMEM((n, seg, d), F32), pltpu.VMEM((4, 1, d), F32), pltpu.VMEM(unit_shapes[0], BF16),
        pltpu.VMEM(unit_shapes[1], BF16), pltpu.VMEM(unit_shapes[2], BF16), pltpu.SemaphoreType.DMA((3,)),
    ]
    params = dict(vmem_limit_bytes=VMEM_LIMIT)
    if ring:
        in_specs += [ANY] * 7 + [full_spec(array.shape) for array in weights[7:]]
        out_shape += [jax.ShapeDtypeStruct(shape, BF16) for shape in unit_shapes]
        out_specs += [ANY] * 5
        scratch += [
            pltpu.VMEM((16, 32, d), BF16), pltpu.SemaphoreType.DMA((9,)), pltpu.VMEM((8, 128), F32),
            pltpu.VMEM((4, 2, 2, 8, 128), F32), pltpu.SemaphoreType.DMA((5, 2, 7)), pltpu.SemaphoreType.DMA((5, 2, 7)),
            pltpu.SemaphoreType.DMA((5, 2)), pltpu.SemaphoreType.DMA((5,)), pltpu.SemaphoreType.DMA((5,)),
            pltpu.SemaphoreType.DMA((2, 20)), pltpu.SemaphoreType.DMA((2, 20)),
        ]
        params.update(collective_id=0, has_side_effects=True)
    else:
        in_specs += [ANY] * 3 + [full_spec((8, d)), full_spec((4, 1, d))]
    return pl.pallas_call(
        functools.partial(forward_kernel, ring, n),
        grid=(2 * n,),
        out_shape=out_shape,
        in_specs=in_specs,
        out_specs=out_specs,
        scratch_shapes=scratch,
        compiler_params=pltpu.CompilerParams(**params),
        name="gather_forward" if ring else "forward_rows",
    )(tokens, memory, docs, keep, *weights)


def writer_all(
    gate_done, read_done, res_ref, mem_ref, memgrad_ref, doc_ref, keep_ref, wr_ref, gate_ref, vec_ref,
    newmem_ref, dres_ref, dkept_ref, gwr_ref, ggate_ref, ggb_ref,
    n3_ref, ns_ref, kept_ref, sq_ref, tk_ref, tv_ref, p_ref, wt_ref, dsq_ref, dlog_ref, dw_ref,
):
    n, half, d = res_ref.shape
    slots = mem_ref.shape[1]
    gain = vec_ref[3:4, :]

    biases = []
    for i in range(n):
        rows, small = slice(i * half, (i + 1) * half), slice(i * slots, (i + 1) * slots)
        hat, _ = norm_parts(res_ref[i])
        n3_ref[rows, :] = (hat * gain).astype(BF16)
        kept = mem_ref[i] * keep_ref[i][:, 0:1]
        kept_ref[small, :] = kept
        hat, _ = norm_parts(kept)
        ns_ref[small, :] = (hat * gain).astype(BF16)
        docs = doc_ref[i].astype(F32)
        bias = jnp.where(docs == jnp.max(docs), 0.0, -1e30)[:, docs.shape[1] - half:]
        biases.append(jnp.broadcast_to(bias, (128, half)).T)
    tk_ref[...] = dot(n3_ref[...], wr_ref[1]).astype(BF16)
    tv_ref[...] = dot(n3_ref[...], wr_ref[2]).astype(BF16)
    sq_ref[...] = (dot(ns_ref[...], wr_ref[0]) * 0.125).astype(BF16)
    low_half = lax.broadcasted_iota(jnp.int32, (1, 128), 1) < 64

    def halves(rows):
        zero = jnp.zeros_like(rows)
        return jnp.concatenate([jnp.where(low_half, rows, zero), jnp.where(low_half, zero, rows)], 0)

    for i in range(n):
        rows, small = slice(i * half, (i + 1) * half), slice(i * slots, (i + 1) * slots)
        for pair in range(4):
            lanes = slice(pair * 128, pair * 128 + 128)
            scores = dot_nt(tk_ref[rows, lanes], halves(sq_ref[small, lanes])) + biases[i]
            e = jnp.exp(scores - jnp.max(scores, axis=0, keepdims=True))
            p = e * (1.0 / jnp.sum(e, axis=0, keepdims=True))
            p_ref[i, pair] = p
            mixed = dot_tn(p.astype(BF16), tv_ref[rows, lanes])
            wt_ref[small, lanes] = jnp.where(low_half, mixed[:slots], mixed[slots:]).astype(BF16)

    def put(ref, index, value):
        ref[index] = value.astype(BF16).reshape(ref.shape[1:])

    write = dot(wt_ref[...], wr_ref[3])
    kept = kept_ref[...]
    write_low = write.astype(BF16)
    kept_low = kept.astype(BF16)
    logit = dot(kept_low, gate_ref[0]) + dot(write_low, gate_ref[1]) + vec_ref[0:1, :]
    gate = jax.nn.sigmoid(logit)
    new = gate * kept + (1.0 - gate) * write
    memgrad = memgrad_ref[...].reshape(n * slots, d)
    newmem_ref[...] = new.reshape(n, slots, d)
    dlogit = memgrad * (kept - write) * gate * (1.0 - gate)
    dlog_ref[...] = dlogit.astype(BF16)
    dlow = dlog_ref[...]
    ggb_ref[...] = jnp.sum(dlow.astype(F32), axis=0, keepdims=True)
    ggate_ref[0:2] = dot_tn(kept_low, dlow).astype(BF16).reshape((2,) + ggate_ref.shape[1:])
    ggate_ref[2:4] = dot_tn(write_low, dlow).astype(BF16).reshape((2,) + ggate_ref.shape[1:])
    gate_done()
    dkept = memgrad * gate + dot_nt(dlow, gate_ref[0])
    dwrite = memgrad * (1.0 - gate) + dot_nt(dlow, gate_ref[1])
    dkept_ref[...] = dkept.reshape(n, slots, d)
    dw_low = dwrite.astype(BF16)
    put(gwr_ref, 3, dot_tn(wt_ref[...], dw_low))
    dw_ref[...] = dot_nt(dw_low, wr_ref[3]).astype(BF16)

    for i in range(n):
        rows, small = slice(i * half, (i + 1) * half), slice(i * slots, (i + 1) * slots)
        for pair in range(4):
            lanes = slice(pair * 128, pair * 128 + 128)
            p = p_ref[i, pair]
            grads = halves(dw_ref[small, lanes])
            keys, values = tk_ref[rows, lanes], tv_ref[rows, lanes]
            dp = dot_nt(values, grads)
            ds = (p * (dp - jnp.sum(dp * p, axis=0, keepdims=True))).astype(BF16)
            dq = dot_tn(ds, keys) * 0.125
            dsq_ref[small, lanes] = jnp.where(low_half, dq[:slots], dq[slots:]).astype(BF16)
            tk_ref[rows, lanes] = dot(ds, halves(sq_ref[small, lanes])).astype(BF16)
            tv_ref[rows, lanes] = dot(p.astype(BF16), grads).astype(BF16)
    read_done()
    put(gwr_ref, 0, dot_tn(ns_ref[...], dsq_ref[...]))
    put(gwr_ref, 1, dot_tn(n3_ref[...], tk_ref[...]))
    put(gwr_ref, 2, dot_tn(n3_ref[...], tv_ref[...]))
    grad = dot_nt(dsq_ref[...], wr_ref[0])
    hat, rstd = norm_parts(kept_ref[...])
    dkept_ref[...] += norm_back(grad, hat, rstd, gain).reshape(n, slots, d)

    for i in range(n):
        rows = slice(i * half, (i + 1) * half)
        grad = dot_nt(tk_ref[rows, :], wr_ref[1]) + dot_nt(tv_ref[rows, :], wr_ref[2])
        hat, rstd = norm_parts(res_ref[i])
        dres_ref[i] = norm_back(grad, hat, rstd, gain)


def ffn_back_kernel(ring, count, *refs):
    refs = list(refs)

    def take(number):
        out = refs[:number]
        del refs[:number]
        return out

    writer_in = take(8)
    vec_ref = writer_in[7]
    og_ref, h1_ref, act_ref, slope_ref, ot_ref, linv_ref, w1_ref, w2_ref, attn_ref = take(9)
    newmem_ref, dkept_ref, ggb_ref, gb_ref, gw1_ref, gw2_ref, gwo_ref, dh_ref, dot_ref, gwr_out, ggate_out = take(11)
    writer_scratch = take(11)
    dres_ref, acc1_ref, acc2_ref, acco_ref, w1_v, w2_v, wo_v, wsem = take(8)
    step = pl.program_id(0)
    seg = og_ref.shape[1]
    loads = lambda: [
        pltpu.make_async_copy(w1_ref, w1_v, wsem.at[0]), pltpu.make_async_copy(w2_ref, w2_v, wsem.at[1]),
        pltpu.make_async_copy(attn_ref.at[3], wo_v, wsem.at[2]),
    ]
    if ring:
        gwr_ref, ggate_ref, fwr_ref, fgate_ref = take(4)
        wide_scratch, slim_scratch = take(7), take(7)
        place = Place()
        writer_rounds = [
            reduce_round(place, unit_first(gwr_ref), wide_scratch, 2 * i, fwr_ref, half) for i, half in enumerate(HALVES)
        ]
        gate_round = reduce_round(place, unit_last(ggate_ref), slim_scratch, 0, fgate_ref)
        jobs = [
            (job(gate_round, REDUCE_STEPS)[2:], 0.0, WRITER_SPANS[1:]),
            (job(writer_rounds[0], REDUCE_STEPS)[1:], 1.5, WRITER_SPANS),
            (job(writer_rounds[1], REDUCE_STEPS)[1:], 1.5 + WRITER_PACE, WRITER_SPANS),
        ]
        places = [((1 + s, i), FFN_BACK_TIME * (s + i / 4)) for s in range(count) for i in range(4)]
        found, rest = plan(jobs, places)
    else:
        gwr_ref, ggate_ref = gwr_out, ggate_out

    @pl.when(step == 0)
    def _():
        for load in loads():
            load.start()
        if ring:
            place.greet()
        acc1_ref[...] = jnp.zeros_like(acc1_ref)
        acc2_ref[...] = jnp.zeros_like(acc2_ref)
        acco_ref[...] = jnp.zeros_like(acco_ref)
        gb_ref[...] = jnp.zeros_like(gb_ref)
        gate_done = (lambda: both(gate_round, "stage_share")) if ring else (lambda: None)
        read_done = (lambda: both(gate_round, "wait_share", "stage_first")) if ring else (lambda: None)
        writer_all(
            gate_done, read_done, *writer_in, newmem_ref, dres_ref, dkept_ref, gwr_ref, ggate_ref, ggb_ref, *writer_scratch
        )
        if ring:
            both(writer_rounds[0] + writer_rounds[1], "stage_share")
        for load in loads():
            load.wait()

    @pl.when(step > 0)
    def _():
        top = og_ref[0, 0:seg // 2, :].astype(F32)
        bottom = og_ref[0, seg // 2:, :].astype(F32) + dres_ref[step - 1]
        dresult = jnp.concatenate([top, bottom], 0)
        low = dresult.astype(BF16)
        h1 = h1_ref[0]
        hat, rstd = norm_parts(h1)
        gain = vec_ref[2:3, :]
        n2t = (hat * gain).astype(BF16).T
        lowt = low.T
        grad = jnp.zeros_like(dresult)
        for part in range(4):
            if ring:
                for s in range(1, 1 + count):
                    hook_in(found, (s, part), step == s)
            acc2_ref[part] += dot(lowt, act_ref[0, part])
            dbefore = (dot_nt(low, w2_v[part]) * slope_ref[0, part].astype(F32)).astype(BF16)
            gb_ref[part] += jnp.sum(dbefore.astype(F32), axis=0, keepdims=True)
            acc1_ref[part] += dot(n2t, dbefore)
            grad = grad + dot_nt(dbefore, w1_v[part])
        dh = dresult + norm_back(grad, hat, rstd, gain)
        dh_ref[0] = dh
        dlow = dh.astype(BF16)
        mixed_grad = dot_nt(wo_v[...], dlow)
        for pair in range(4):
            for block in range(seg // BLOCK):
                columns = slice(block * BLOCK, (block + 1) * BLOCK)
                for i in range(2):
                    features = slice(pair * 128 + i * 64, pair * 128 + i * 64 + 64)
                    scale = linv_ref[0, pair, block, :, i * 128:(i + 1) * 128]
                    dot_ref[0, features, columns] = (mixed_grad[features, columns] * scale).astype(BF16)
        acco_ref[...] += dot(ot_ref[0], dlow)

        @pl.when(step == count)
        def _():
            stores = [
                pltpu.make_async_copy(w1_v, gw1_ref, wsem.at[0]), pltpu.make_async_copy(w2_v, gw2_ref, wsem.at[1]),
                pltpu.make_async_copy(wo_v, gwo_ref, wsem.at[2]),
            ]
            w1_v[...] = acc1_ref[...].astype(BF16)
            stores[0].start()
            for part in range(4):
                w2_v[part] = acc2_ref[part].T.astype(BF16)
            stores[1].start()
            wo_v[...] = acco_ref[...].astype(BF16)
            stores[2].start()
            if ring:
                for step_left in rest:
                    step_left()
                gwr_out[...] = fwr_ref[...]
                ggate_out[...] = fgate_ref[...]
            for store in stores:
                store.wait()


def call_ffn_back(ring, res, memory, memory_grad, docs, keep, wr, gate, vec, out_grad, h1, act, slope, ot, linv, w1, w2, attn):
    n, half, d = res.shape
    seg = 2 * half
    slots = memory.shape[1]
    rows, small = n * half, n * slots
    writer_args = (res, memory, memory_grad, docs, keep, wr, gate, vec)
    units = (4, 4, 2, 2, 32, d)
    gate_units = (4, 2, 2, 4, 16, d)
    if ring:
        grads = [((4, 32, d), F32), ((4, 16, d), F32)]
    else:
        grads = [(units, BF16), (gate_units, BF16)]
    whole = [((n, slots, d), F32), ((n, slots, d), F32), ((1, d), F32), ((4, 1, d), F32)]
    stored = [((4, d, d), BF16), ((4, d, d), BF16), ((d, d), BF16)]
    scratch = [
        pltpu.VMEM((rows, d), BF16), pltpu.VMEM((small, d), BF16), pltpu.VMEM((small, d), F32), pltpu.VMEM((small, d), BF16),
        pltpu.VMEM((rows, d), BF16), pltpu.VMEM((rows, d), BF16), pltpu.VMEM((n, 4, half, 2 * slots), F32),
        pltpu.VMEM((small, d), BF16), pltpu.VMEM((small, d), BF16), pltpu.VMEM((small, d), BF16), pltpu.VMEM((small, d), BF16),
        pltpu.VMEM((n, half, d), F32), pltpu.VMEM((4, d, d), F32), pltpu.VMEM((4, d, d), F32), pltpu.VMEM((d, d), F32),
        pltpu.VMEM((4, d, d), BF16), pltpu.VMEM((4, d, d), BF16), pltpu.VMEM((d, d), BF16), pltpu.SemaphoreType.DMA((3,)),
    ]
    params = dict(vmem_limit_bytes=VMEM_LIMIT)
    if ring:
        scratch += [pltpu.VMEM(units, BF16), pltpu.VMEM(gate_units, BF16)]
        scratch += [pltpu.VMEM((4, 32, d), F32), pltpu.VMEM((4, 16, d), F32)]
        scratch += reduce_scratch(4, 32, d // 2) + reduce_scratch(2, 16, d)
        params.update(collective_id=1, has_side_effects=True)
    return pl.pallas_call(
        functools.partial(ffn_back_kernel, ring, n),
        grid=(n + 1,),
        out_shape=[jax.ShapeDtypeStruct(shape, kind) for shape, kind in whole + stored]
        + [jax.ShapeDtypeStruct((n, seg, d), F32), jax.ShapeDtypeStruct((n, d, seg), BF16)]
        + [jax.ShapeDtypeStruct(shape, kind) for shape, kind in grads],
        in_specs=[full_spec(array.shape) for array in writer_args] + [
            phase_spec((seg, d), 1, n), phase_spec((seg, d), 1, n), phase_spec((4, seg, 512), 1, n),
            phase_spec((4, seg, 512), 1, n), phase_spec((d, seg), 1, n), phase_spec((4, 4, 1, 256), 1, n), ANY, ANY, ANY,
        ],
        out_specs=[full_spec(shape) for shape, _ in whole] + [ANY] * 3 + [phase_spec((seg, d), 1, n), phase_spec((d, seg), 1, n)]
        + [full_spec(shape) for shape, _ in grads],
        scratch_shapes=scratch,
        compiler_params=pltpu.CompilerParams(**params),
        name="ffn_back",
    )(*writer_args, out_grad, h1, act, slope, ot, linv, w1, w2, attn)


def attn_back_kernel(ring, count, *refs):
    refs = list(refs)

    def take(number):
        out = refs[:number]
        del refs[:number]
        return out

    qt_ref, k_ref, v_ref, e_ref, ot_ref, dot_ref = take(6)
    tok_ref, mem_ref, keep_ref, dkept_ref, dh_ref = take(5)
    n1_ref, attn_ref, vec_ref = take(3)
    if ring:
        ggb_ref, gb_ref, gw1_ref, gw2_ref, gwo_ref = take(5)
    gtok_ref, gmem_ref = take(2)
    if ring:
        fqkv_ref, fo_ref, fw1_ref, fw2_ref, fsmall_ref = take(5)
    else:
        (gqkv_ref,) = take(1)
    dqt_ref, dkl_ref, dvl_ref, dk_ref, dv_ref, qp_ref, dp_ref = take(7)
    step = pl.program_id(0)
    seg = tok_ref.shape[1]
    d = tok_ref.shape[2]
    slots = mem_ref.shape[1]
    if ring:
        gqkv_ref, ffn_final, out_final, heads_final = take(4)
        wide_scratch, out_scratch, heads_scratch = take(7), take(7), take(7)
        sown, sacc, swide, smid, snarrow, ssend, srecv = take(7)
        place = Place()
        ffn_rounds = [
            reduce_round(place, grad, wide_scratch, 4 * j + 2 * i, ffn_final.at[j], half)
            for j, grad in ((1, unit_last(gw2_ref)), (0, unit_first(gw1_ref))) for i, half in enumerate(HALVES)
        ]
        out_unit = reduce_unit(place, unit_last(gwo_ref), out_scratch, 0, 0, out_final, place.core, 1 - place.core)
        heads = [
            reduce_unit(
                place, unit_first(gqkv_ref.at[p]), heads_scratch, p, p % 2, heads_final.at[p], place.core, 1 - place.core
            )
            for p in range(4)
        ]
        small = ReduceSmall(place, sown, sacc, swide, smid, snarrow, fsmall_ref, ssend, srecv)
        jobs = [(job(ffn_rounds[i], REDUCE_STEPS), FFN_REDUCE_PACE * i, REDUCE_SPANS) for i in range(4)]
        jobs.append((job([out_unit], REDUCE_STEPS), FFN_REDUCE_PACE * 4, SLIM_SPANS))
        jobs.append((job([small], REDUCE_STEPS[:4] + (("wait_z",),)), FFN_REDUCE_PACE * 4 + 1.0, SLIM_SPANS))
        for p in range(4):
            jobs.append((job([heads[p]], REDUCE_STEPS)[1:], HEADS_TIME * (p + 1) + SLIM_SPANS[0], SLIM_SPANS[1:]))
        places = [((p, i), HEADS_TIME * p + HEADS_TIMES[i]) for p in range(4) for i in range(5)]
        places += [((4 + s, 0), 4 * HEADS_TIME + LAST_TIME * (s + 1)) for s in range(count)]
        found, rest = plan(jobs, places)

    def hook(name, extra=True):
        if ring:
            hook_in(found, name, (step == name[0]) & extra)

    @pl.when(step < 4)
    def _():
        @pl.when(step == 0)
        def _():
            if ring:
                place.greet()
                for m in range(4):
                    for i in range(4):
                        lanes = slice(i * 128, (i + 1) * 128)
                        sown[m, i // 2, i % 2] = jnp.concatenate(
                            [gb_ref[m, :, lanes], ggb_ref[:, m * 128:(m + 1) * 128], jnp.zeros((6, 128), F32)], 0
                        )
            qp_ref[...] = jnp.zeros_like(qp_ref)
            dp_ref[...] = jnp.zeros_like(dp_ref)

        features = pl.ds(pl.multiple_of(step * 128, 128), 128)

        def one_segment(s, carry):
            for p in range(4):
                for i in range(4):
                    hook((p, i), s == min(i, count - 1))
            dk_ref[...] = jnp.zeros_like(dk_ref)
            dv_ref[...] = jnp.zeros_like(dv_ref)
            for block, (first, last) in enumerate(SPANS):
                start = STARTS[block]
                columns = slice(block * BLOCK, (block + 1) * BLOCK)
                mixed_grad = dot_ref[s, :, columns]
                delta = mixed_grad.astype(F32) * ot_ref[s, :, columns].astype(F32)
                delta = jnp.concatenate(
                    [jnp.sum(delta[0:64], axis=0, keepdims=True), jnp.sum(delta[64:128], axis=0, keepdims=True)], 1
                )
                held = dp_ref.at[block]
                diagonal_pair(held, mixed_grad)
                query = qp_ref.at[block]
                diagonal_pair(query, qt_ref[s, :, columns])
                e = e_ref[s, 0, start:start + last - first, :]
                dp = dot(v_ref[s, 0, first:last, :], held[...])
                ds = (e.astype(F32) * (dp - delta)).astype(BF16)
                dv_ref[first:last, :] += dot_nt(e, held[...])
                dk_ref[first:last, :] += dot_nt(ds, query[...])
                dq = dot_tn(k_ref[s, 0, first:last, :], ds) * 0.125
                dqt_ref[s, features, columns] = jnp.concatenate([dq[0:64, 0:128], dq[64:128, 128:256]], 0).astype(BF16)
            dkl_ref[s, step] = dk_ref[...].astype(BF16)
            dvl_ref[s, step] = dv_ref[...].astype(BF16)
            return carry

        lax.fori_loop(0, count, one_segment, 0)
        for p in range(4):
            hook((p, 4))
        gq = dot(dqt_ref[0, features, :], n1_ref[0, 128:, :])
        gkv = dot_tn(n1_ref[0], jnp.concatenate([dkl_ref[0, step], dvl_ref[0, step]], 1))
        for s in range(1, count):
            gq = gq + dot(dqt_ref[s, features, :], n1_ref[s, 128:, :])
            gkv = gkv + dot_tn(n1_ref[s], jnp.concatenate([dkl_ref[s, step], dvl_ref[s, step]], 1))
        both_cores = (2, 16, 16, 128)
        parts = [part.astype(BF16).reshape(16, 2, 16, 128) for part in (gq.T, gkv[:, 0:128], gkv[:, 128:256])]
        for i, part in enumerate(parts):
            for core in range(2):
                gqkv_ref[step, core, :, :, :, i * 16:(i + 1) * 16, :] = part[:, core].reshape(4, 2, 2, 16, 128)
        if ring:
            for p in range(4):

                @pl.when(step == p)
                def _(p=p):
                    both([heads[p]], "stage_share")

    @pl.when(step >= 4)
    def _():
        here = step - 4
        gain = vec_ref[1:2, :]
        dk = jnp.concatenate([dkl_ref[here, p] for p in range(4)], 1)
        dv = jnp.concatenate([dvl_ref[here, p] for p in range(4)], 1)
        grad = dot_nt(dk, attn_ref[1]) + dot_nt(dv, attn_ref[2])
        slot_grad = grad[0:slots]
        kept = mem_ref[0] * keep_ref[0][:, 0:1]
        hat, rstd = norm_parts(kept)
        gmem_ref[0] = (dkept_ref[0] + norm_back(slot_grad, hat, rstd, gain)) * keep_ref[0][:, 0:1]
        grad = grad[128:] + dot_nt(dqt_ref[here].T, attn_ref[0])
        hat, rstd = norm_parts(tok_ref[0].astype(F32))
        gtok_ref[0] = dh_ref[0] + norm_back(grad, hat, rstd, gain)
        for s in range(count):
            hook((4 + s, 0))

        if ring:

            @pl.when(step == 3 + count)
            def _():
                for step_left in rest:
                    step_left()
                fqkv_ref[...] = heads_final[...]
                fo_ref[...] = out_final[...]
                fw1_ref[...] = ffn_final[0]
                fw2_ref[...] = ffn_final[1]


def call_attn_back(
    ring, dh, tokens, memory, keep, n1, qt, k, v, e, ot, mixed_grad, dkept, attn, vec, extra
):
    n, seg, d = tokens.shape
    slots = memory.shape[1]
    shapes = [((n, seg, d), F32), ((n, slots, d), F32)]
    out_specs = [phase_spec((seg, d), 4, n), phase_spec((slots, d), 4, n)]

    def pair_spec(shape, axis):
        return pl.BlockSpec(shape, lambda i: tuple(jnp.minimum(i, 3) if j == axis else 0 for j in range(len(shape))))

    in_specs = [
        pair_spec((n, 128, seg), 1), pair_spec((n, 1, seg + 128, 128), 1), pair_spec((n, 1, seg + 128, 128), 1),
        pair_spec((n, 1, LIVE, 256), 1), pair_spec((n, 128, seg), 1), pair_spec((n, 128, seg), 1),
        phase_spec((seg, d), 4, n), phase_spec((slots, d), 4, n), phase_spec((1, 128), 4, n), phase_spec((slots, d), 4, n),
        phase_spec((seg, d), 4, n),
        full_spec(n1.shape), full_spec((3, d, d)), full_spec(vec.shape),
    ]
    heads = (4, 2, 4, 2, 2, 48, 128)
    scratch = [
        pltpu.VMEM((n, d, seg), BF16), pltpu.VMEM((n, 4, seg + 128, 128), BF16), pltpu.VMEM((n, 4, seg + 128, 128), BF16),
        pltpu.VMEM((seg + 128, 128), F32), pltpu.VMEM((seg + 128, 128), F32), pltpu.VMEM((4, 128, 256), BF16),
        pltpu.VMEM((4, 128, 256), BF16),
    ]
    params = dict(vmem_limit_bytes=VMEM_LIMIT)
    if ring:
        in_specs += [full_spec(extra[0].shape), full_spec(extra[1].shape), ANY, ANY, ANY]
        more = [((4, 2, 48, 128), F32), ((2, 16, d), F32), ((4, 32, d), F32), ((4, 32, d), F32), ((8, 128), F32)]
        scratch += [
            pltpu.VMEM(heads, BF16), pltpu.VMEM((2, 4, 32, d), F32), pltpu.VMEM((2, 16, d), F32),
            pltpu.VMEM((4, 2, 48, 128), F32),
        ]
        scratch += reduce_scratch(8, 32, d // 2) + reduce_scratch(1, 16, d) + reduce_scratch(4, 48, 128)
        scratch += [pltpu.VMEM((4, 2, 2, 8, 128), F32)] * 3 + [
            pltpu.VMEM((4, 2, 8, 128), F32), pltpu.VMEM((7, 8, 128), F32),
            pltpu.SemaphoreType.DMA((6,)), pltpu.SemaphoreType.DMA((6,)),
        ]
        params.update(collective_id=2, has_side_effects=True)
    else:
        more = [(heads, BF16)]
    return pl.pallas_call(
        functools.partial(attn_back_kernel, ring, n),
        grid=(4 + n,),
        out_shape=[jax.ShapeDtypeStruct(shape, kind) for shape, kind in shapes + more],
        in_specs=in_specs,
        out_specs=out_specs + [full_spec(shape) for shape, _ in more],
        scratch_shapes=scratch,
        compiler_params=pltpu.CompilerParams(**params),
        name="attn_back",
    )(qt, k, v, e, ot, mixed_grad, tokens, memory, keep, dkept, dh, n1, attn, vec, *extra)


def hand_out_kernel(
    fqkv_ref, fo_ref, fw1_ref, fw2_ref, fwr_ref, fgate_ref, small_ref, qkv_ref, in_ref, wqkv_ref, gain_ref,
    gqkv_ref, gout_ref, gin_ref, gffn_ref, gwqkv_ref, gwout_ref, ggate_ref, gb_ref, ggb_ref, ggain_ref,
):
    for pair in range(4):
        for core in range(2):
            rows = slice(core * 16, core * 16 + 16)
            for i in range(3):
                gqkv_ref[i, rows, pair * 128:(pair + 1) * 128] = fqkv_ref[pair, core, i * 16:(i + 1) * 16, :]
    for core in range(2):
        gout_ref[core * 16:core * 16 + 16, :] = fo_ref[core]
    for j in range(4):
        gin_ref[:, j * 512:(j + 1) * 512] = fw1_ref[j]
    gffn_ref[...] = fw2_ref[...]
    gwqkv_ref[...] = fwr_ref[0:3]
    gwout_ref[...] = fwr_ref[3]
    ggate_ref[...] = fgate_ref[...]
    gb_ref[...] = small_ref[0:1, :]
    rows = ggb_ref.shape[1]
    place = lax.rem(lax.axis_index("dp"), 4)
    narrow = jnp.zeros((1, rows), F32)
    for i in range(4):
        narrow = narrow + small_ref[1:2, i * rows:(i + 1) * rows] * (place == i).astype(F32)
    ggb_ref[...] = narrow
    sums = [
        jnp.sum(jnp.sum(qkv_ref[...].astype(F32) * gqkv_ref[...], axis=0), axis=-1, keepdims=True),
        jnp.sum(in_ref[...].astype(F32) * gin_ref[...], axis=-1, keepdims=True),
        jnp.sum(jnp.sum(wqkv_ref[...].astype(F32) * gwqkv_ref[...], axis=0), axis=-1, keepdims=True),
    ]
    for i in range(3):
        across = jnp.broadcast_to(sums[i], (rows, 128)).T[0:1, :]
        ggain_ref[i:i + 1, :] = across / gain_ref[i:i + 1, :].astype(F32)


def call_hand_out(*args):
    rows, d = args[2].shape[1:]
    vmem = pl.BlockSpec(memory_space=pltpu.VMEM)
    shapes = [
        (3, rows, d), (rows, d), (rows, 4 * d), (4, rows, d), (3, rows, d), (rows, d), (4, rows // 2, d), (1, 128), (1, rows),
        (3, rows),
    ]
    return pl.pallas_call(
        hand_out_kernel,
        out_shape=[jax.ShapeDtypeStruct(shape, F32) for shape in shapes],
        in_specs=[vmem] * 11,
        out_specs=[vmem] * 10,
        name="hand_out",
    )(*args)


def plain_weights(attn_qkv, attn_out, ffn_in, ffn_out, writer_qkv, writer_out, gate_weight, ffn_bias, gate_bias, gains):
    rows, d = attn_out.shape
    packed = jnp.concatenate(
        [
            attn_qkv, attn_out[None], ffn_in.reshape(rows, 4, d).transpose(1, 0, 2), ffn_out.reshape(4, rows, d),
            writer_qkv, writer_out[None], gate_weight.reshape(2, rows, d),
        ],
        0,
    )
    packed = lax.all_gather(packed, "dp", axis=0)
    n = packed.shape[0]

    def by_rows(first, last):
        return packed[:, first:last].transpose(1, 0, 2, 3).reshape(last - first, n * rows, d)

    small = jnp.concatenate([ffn_bias.reshape(4, rows), gate_bias[None], gains], 0).astype(F32)
    small = lax.all_gather(small, "dp", axis=0)
    b1 = small[:, 0:4].reshape(4, 1, d)
    vec = small.transpose(1, 0, 2).reshape(8, d)
    vec = jnp.concatenate([vec[4:8], jnp.zeros((4, d), F32)], 0)
    w2 = packed[:, 8:12].reshape(4, d, d)
    return by_rows(0, 4), by_rows(4, 8), w2, by_rows(12, 16), packed[:, 16:18].reshape(2, d, d), vec, b1


def plain_grads(rows, attn_qkv, ffn_in, writer_qkv, gains, gattn, gw1, gw2, gwr, ggate, gb, ggb):
    d = gattn.shape[-1]
    n = d // rows

    def by_rows(grad):
        return grad.reshape(-1, n, rows, d).transpose(1, 0, 2, 3)

    packed = jnp.concatenate(
        [by_rows(gattn), by_rows(gw1), gw2.reshape(n, 4, rows, d), by_rows(gwr), ggate.reshape(n, 2, rows, d)], 1
    )
    owned = lax.psum_scatter(packed.astype(F32), "dp", scatter_dimension=0, tiled=False)
    owned = lax.psum(owned.astype(BF16), "outer").astype(F32)
    small = jnp.concatenate([gb.reshape(n, 4 * rows), ggb.reshape(n, rows)], 1)
    small = lax.psum(lax.psum_scatter(small, "dp", scatter_dimension=0, tiled=False), "outer")
    gin = owned[4:8].transpose(1, 0, 2).reshape(rows, 4 * d)
    ggains = jnp.stack(
        [
            jnp.sum(attn_qkv.astype(F32) * owned[0:3], (0, 2)), jnp.sum(ffn_in.astype(F32) * gin, 1),
            jnp.sum(writer_qkv.astype(F32) * owned[12:15], (0, 2)),
        ]
    )
    return (
        owned[0:3], owned[3], gin, owned[8:12].reshape(4 * rows, d), owned[12:15], owned[15], owned[16:18].reshape(2 * rows, d),
        small[0:4 * rows], small[4 * rows:], ggains / gains.astype(F32),
    )


def body(
    tokens, memory, doc_ids, resets, out_grad, memory_grad,
    attn_qkv, attn_out, ffn_in, ffn_bias, ffn_out, writer_qkv, writer_out, gate_weight, gate_bias, gains,
):
    micro, segs, seg, d = tokens.shape
    slots = memory.shape[2]
    rows = attn_out.shape[0]
    n = micro * segs
    ring = lax.axis_size("dp") == 16 and lax.axis_size("outer") == 2 and rows == 32
    tokens, out_grad = tokens.reshape(n, seg, d), out_grad.reshape(n, seg, d)
    memory, memory_grad = memory.reshape(n, slots, d), memory_grad.reshape(n, slots, d)
    docs = doc_ids.reshape(n, 1, seg)
    keep = jnp.broadcast_to((1 - resets).astype(F32).reshape(n, 1, 1), (n, 1, 128))
    if ring:
        weights = (
            attn_qkv, attn_out, ffn_in, ffn_out.reshape(4, rows, d), writer_qkv, writer_out,
            gate_weight.reshape(4, rows // 2, d), ffn_bias.reshape(1, 4 * rows), gate_bias.reshape(1, rows), gains,
        )
    else:
        attn, w1, w2, wr, gate, vec, b1 = plain_weights(
            attn_qkv, attn_out, ffn_in, ffn_out, writer_qkv, writer_out, gate_weight, ffn_bias, gate_bias, gains
        )
        units = (4, 4, 2, 2, 32, d)
        weights = (attn.reshape(units), w1.reshape(units), w2.reshape(4, 2, 2, 4, 32, d), vec, b1)
    n1, qt, k, v, e, linv, ot, h1, out, res, act, slope, vec, *whole = call_forward(ring, tokens, memory, docs, keep, weights)
    if ring:
        attn, w1, w2, wr = (array.reshape(4, d, d) for array in whole[:4])
        gate = whole[4].reshape(2, d, d)
    new_memory, dkept, ggb, gb, gw1, gw2, gwo, dh, mixed_grad, gwr, ggate = call_ffn_back(
        ring, res, memory, memory_grad, docs, keep, wr, gate, vec, out_grad, h1, act, slope, ot, linv, w1, w2, attn
    )
    extra = ()
    if ring:
        extra = (ggb, gb, gw1.reshape(4, 4, 2, 2, 32, d), gw2.reshape(4, 2, 2, 4, 32, d), gwo.reshape(4, 2, 2, 2, 16, d))
    grad_tokens, grad_memory, *rest = call_attn_back(
        ring, dh, tokens, memory, keep, n1, qt, k, v, e, ot, mixed_grad, dkept, attn, vec, extra
    )
    if ring:
        grads = call_hand_out(*rest[:4], gwr, ggate, rest[4], attn_qkv, ffn_in, writer_qkv, gains)
    else:
        (heads,) = rest
        gattn = heads.reshape(4, 2, 16, 3, 16, 128).transpose(3, 2, 1, 4, 0, 5).reshape(3, d, d)
        gattn = jnp.concatenate([gattn, gwo[None]], 0)
        grads = plain_grads(rows, attn_qkv, ffn_in, writer_qkv, gains, gattn, gw1, gw2, gwr, ggate, gb, ggb)
    gqkv, gout, gin, gffn, gwqkv, gwout, ggw, gb, ggb, ggains = grads
    return (
        out.reshape(micro, segs, seg, d), new_memory.reshape(micro, segs, slots, d),
        grad_tokens.reshape(micro, segs, seg, d), grad_memory.reshape(micro, segs, slots, d),
        gqkv, gout, gin, gb.reshape(4 * rows), gffn.reshape(4 * rows, d), gwqkv, gwout, ggw.reshape(2 * rows, d),
        ggb.reshape(rows), ggains,
    )


def solution(mesh):
    split = ("dp", "outer")
    whole = P(None, split, None, None)
    weights = (
        P(None, "dp", None), P("dp", None), P("dp", None), P("dp"), P("dp", None), P(None, "dp", None),
        P("dp", None), P("dp", None), P("dp"), P(None, "dp"),
    )
    return jax.shard_map(
        body,
        mesh=mesh,
        in_specs=(whole, whole, P(None, split, None), P(None, split), whole, whole) + weights,
        out_specs=(whole, whole, whole, whole) + weights,
        check_vma=False,
    )
```

```python
import functools

import jax
import jax.numpy as jnp
from jax import lax
from jax.experimental import pallas as pl
from jax.experimental.pallas import tpu as pltpu
from jax.sharding import PartitionSpec as P

HEADS = 8
BLOCK = 128
SPANS = ((0, 256), (0, 384), (128, 512), (256, 640))
STARTS = (0, 256, 640, 1024)
LIVE = 1408
F32 = jnp.float32
BF16 = jnp.bfloat16
VMEM_LIMIT = 60 * 1024 * 1024


def dot(a, b):
    return jnp.dot(a, b, preferred_element_type=F32)


def dot_nt(a, b):
    return lax.dot_general(a, b, (((1,), (1,)), ((), ())), preferred_element_type=F32)


def dot_tn(a, b):
    return lax.dot_general(a, b, (((0,), (0,)), ((), ())), preferred_element_type=F32)


def norm_parts(rows):
    centred = rows - jnp.mean(rows, axis=-1, keepdims=True)
    rstd = lax.rsqrt(jnp.mean(centred * centred, axis=-1, keepdims=True) + 1e-05)
    return centred * rstd, rstd


def norm_back(grad, hat, rstd, gain):
    scaled = grad * gain
    return rstd * (
        scaled
        - jnp.mean(scaled, axis=-1, keepdims=True)
        - hat * jnp.mean(scaled * hat, axis=-1, keepdims=True)
    )


def diagonal_pair(ref, top):
    ref[0:64, 0:128] = top[0:64]
    ref[64:128, 128:256] = top[64:128]


MESH = pl.DeviceIdType.MESH
EVERY = slice(None)


class Place:
    def __init__(self):
        self.dp = lax.axis_index("dp")
        self.core = lax.axis_index("outer")
        self.z, self.y, self.x = self.dp // 4, (self.dp // 2) % 2, self.dp % 2

    def sibling(self):
        return (self.dp, 1 - self.core)

    def along_x(self):
        return (self.dp + 1 - 2 * self.x, self.core)

    def along_y(self):
        return (self.dp + 2 - 4 * self.y, self.core)

    def other_z(self, shift):
        return lax.rem(self.z + shift, 4)

    def along_z(self, shift):
        return (self.dp + 4 * (self.other_z(shift) - self.z), self.core)

    def greet(self):
        barrier = pltpu.get_barrier_semaphore()
        everyone = [self.sibling(), self.along_x(), self.along_y()] + [self.along_z(shift) for shift in (1, 2, 3)]
        for device in everyone:
            pl.semaphore_signal(barrier, inc=1, device_id=device, device_id_type=MESH)
        pl.semaphore_wait(barrier, len(everyone))


class Travel:
    def __init__(self, place, send, recv):
        self.place, self.send, self.recv = place, send, recv

    def copy(self, stage, src, dst, device):
        return pltpu.make_async_remote_copy(
            src_ref=src, dst_ref=dst, send_sem=self.send.at[stage], recv_sem=self.recv.at[stage], device_id=device,
            device_id_type=MESH,
        )

    def go(self, stage, src, dst, device):
        self.copy(stage, src, dst, device).start()

    def arrived(self, stage, dst):
        self.copy(stage, dst, dst, self.place.sibling()).wait_recv()

    def left(self, stage, src):
        self.copy(stage, src, src, self.place.sibling()).wait_send()


class Gather(Travel):
    def __init__(self, place, view, own, lane, send, recv, local):
        super().__init__(place, send, recv)
        self.view, self.own, self.lane, self.local = view, own, lane, local
        self.unit = 2 * place.core + lane

    def mine(self):
        at = self.place
        return self.view(self.unit, at.z, at.y, at.x)

    def stage_z(self):
        at = self.place
        pltpu.make_async_copy(self.own(self.unit), self.mine(), self.local).start()
        for shift in (1, 2, 3):
            self.go(shift - 1, self.own(self.unit), self.mine(), at.along_z(shift))

    def wait_z(self):
        at = self.place
        pltpu.make_async_copy(self.own(self.unit), self.mine(), self.local).wait()
        for shift in (1, 2, 3):
            self.arrived(shift - 1, self.view(self.unit, at.other_z(4 - shift), at.y, at.x))

    def column(self, far):
        at = self.place
        if self.lane:
            return self.view(self.unit, EVERY, 1 - at.y if far else at.y, at.x)
        return self.view(self.unit, EVERY, at.y, 1 - at.x if far else at.x)

    def half(self, unit, far):
        at = self.place
        if self.lane:
            return self.view(unit, EVERY, EVERY, 1 - at.x if far else at.x)
        return self.view(unit, EVERY, 1 - at.y if far else at.y, EVERY)

    def stage_first(self):
        part = self.column(False)
        self.go(3, part, part, self.place.along_y() if self.lane else self.place.along_x())

    def wait_first(self):
        self.arrived(3, self.column(True))

    def stage_second(self):
        part = self.half(self.unit, False)
        self.go(4, part, part, self.place.along_x() if self.lane else self.place.along_y())
        self.go(5, part, part, self.place.sibling())

    def wait_second(self):
        self.arrived(4, self.half(self.unit, True))

    def stage_share(self):
        part = self.half(self.unit, True)
        self.go(6, part, part, self.place.sibling())

    def wait_share(self):
        other = 2 * (1 - self.place.core) + self.lane
        self.arrived(5, self.half(other, False))
        self.arrived(6, self.half(other, True))

    def finish(self):
        for stage in range(3):
            self.left(stage, self.own(self.unit))
        self.left(3, self.column(False))
        self.left(4, self.half(self.unit, False))
        self.left(5, self.half(self.unit, False))
        self.left(6, self.half(self.unit, True))


class FirstGather(Travel):
    SHIFTS = (0, 3, 1, 2)

    def __init__(self, place, view, own, lane, send, recv, local):
        super().__init__(place, send, recv)
        self.view, self.own, self.lane, self.local = view, own, lane, local
        self.unit = 2 * place.core + lane

    def part(self, unit, z, far_first, far_second):
        at = self.place
        far_x, far_y = (far_second, far_first) if self.lane else (far_first, far_second)
        return self.view(unit, z, 1 - at.y if far_y else at.y, 1 - at.x if far_x else at.x)

    def block(self, shift, far_first, far_second):
        return self.part(self.unit, self.place.other_z(4 - shift), far_first, far_second)

    def first_partner(self):
        return self.place.along_y() if self.lane else self.place.along_x()

    def second_partner(self):
        return self.place.along_x() if self.lane else self.place.along_y()

    def keep(self):
        return pltpu.make_async_copy(self.own(self.unit), self.block(0, False, False), self.local)

    def begin(self):
        mine = self.own(self.unit)
        there = self.block(0, False, False)
        for shift in (3, 1, 2):
            self.go(shift - 1, mine, there, self.place.along_z(shift))
        self.go(4, mine, there, self.first_partner())
        self.go(8, mine, there, self.second_partner())
        self.keep().start()

    def column_block(self, shift):
        here = self.block(shift, False, False)
        self.arrived(shift - 1, here)
        self.go(4 + shift, here, here, self.first_partner())
        self.go(8 + shift, here, here, self.second_partner())

    def column_done(self):
        self.keep().wait()
        self.share(0, False, False)

    def share(self, index, far_first, far_second):
        part = self.part(self.unit, EVERY, far_first, far_second)
        self.go(16 + index, part, part, self.place.sibling())

    def far_block(self, shift):
        here = self.block(shift, True, False)
        self.arrived(4 + shift, here)
        self.go(12 + shift, here, here, self.second_partner())

    def far_done(self):
        self.share(1, True, False)
        for shift in self.SHIFTS:
            self.arrived(8 + shift, self.block(shift, False, True))
        self.share(2, False, True)

    def rest(self):
        for shift in self.SHIFTS:
            self.arrived(12 + shift, self.block(shift, True, True))
        self.share(3, True, True)

    def done(self):
        other = 2 * (1 - self.place.core) + self.lane
        for index, (far_first, far_second) in enumerate(((False, False), (True, False), (False, True), (True, True))):
            self.arrived(16 + index, self.part(other, EVERY, far_first, far_second))

    def finish(self):
        for stage in range(3):
            self.left(stage, self.own(self.unit))
        for leg in (4, 8):
            self.left(leg, self.own(self.unit))
            for shift in (1, 2, 3):
                self.left(leg + shift, self.block(shift, False, False))
        for shift in range(4):
            self.left(12 + shift, self.block(shift, True, False))
        for index, (far_first, far_second) in enumerate(((False, False), (True, False), (False, True), (True, True))):
            self.left(16 + index, self.part(self.unit, EVERY, far_first, far_second))


class GatherSmall(Travel):
    def __init__(self, place, ref, own, send, recv):
        super().__init__(place, send, recv)
        self.ref, self.own = ref, own

    def stage_z(self):
        at = self.place
        self.ref[at.z, at.y, at.x] = self.own[...]
        for shift in (1, 2, 3):
            self.go(shift - 1, self.own, self.ref.at[at.z, at.y, at.x], at.along_z(shift))

    def wait_z(self):
        at = self.place
        for shift in (1, 2, 3):
            self.arrived(shift - 1, self.ref.at[at.other_z(4 - shift), at.y, at.x])

    def stage_first(self):
        at = self.place
        part = self.ref.at[:, at.y, at.x]
        self.go(3, part, part, at.along_x())

    def wait_first(self):
        at = self.place
        self.arrived(3, self.ref.at[:, at.y, 1 - at.x])

    def stage_second(self):
        at = self.place
        part = self.ref.at[:, at.y]
        self.go(4, part, part, at.along_y())

    def wait_second(self):
        at = self.place
        self.arrived(4, self.ref.at[:, 1 - at.y])

    def finish(self):
        at = self.place
        for stage in range(3):
            self.left(stage, self.own)
        self.left(3, self.ref.at[:, at.y, at.x])
        self.left(4, self.ref.at[:, at.y])


def unit_first(ref):
    return lambda u, z, y, x: ref.at[u, z, y, x]


def unit_last(ref):
    return lambda u, z, y, x: ref.at[z, y, x, u]


class Reduce(Travel):
    def __init__(self, place, own, other, lane, acc, wide, mid, narrow, final, final_other, send, recv, local):
        super().__init__(place, send, recv)
        self.own, self.other, self.lane, self.local = own, other, lane, local
        self.acc, self.wide, self.mid, self.narrow = acc, wide, mid, narrow
        self.final, self.final_other = final, final_other

    def stage_share(self):
        self.go(0, self.other, self.wide, self.place.sibling())
        pltpu.make_async_copy(self.own, self.acc, self.local).start()

    def wait_share(self):
        pltpu.make_async_copy(self.own, self.acc, self.local).wait()
        self.arrived(0, self.wide)

        def add(z, carry):
            self.acc[z] = self.acc[z] + self.wide[z]
            return carry

        lax.fori_loop(0, 4, add, 0)

    def half(self, far):
        at = self.place
        if self.lane:
            return self.acc.at[:, :, 1 - at.x if far else at.x]
        return self.acc.at[:, 1 - at.y if far else at.y]

    def stage_first(self):
        at = self.place
        self.go(1, self.half(True), self.mid, at.along_x() if self.lane else at.along_y())

    def wait_first(self):
        at = self.place
        self.arrived(1, self.mid)

        def add(z, carry):
            for i in range(2):
                part = self.acc.at[z, i, at.x] if self.lane else self.acc.at[z, at.y, i]
                part[...] = part[...] + self.mid[z, i]
            return carry

        lax.fori_loop(0, 4, add, 0)

    def quarter(self):
        at = self.place
        if self.lane:
            return self.acc.at[:, 1 - at.y, at.x]
        return self.acc.at[:, at.y, 1 - at.x]

    def stage_second(self):
        self.go(2, self.quarter(), self.narrow.at[0:4], self.place.along_y() if self.lane else self.place.along_x())

    def wait_second(self):
        at = self.place
        self.arrived(2, self.narrow.at[0:4])
        part = self.acc.at[:, at.y, at.x]
        part[...] = part[...] + self.narrow[0:4]

    def block(self, shift):
        at = self.place
        return self.acc.at[at.other_z(shift), at.y, at.x]

    def stage_z(self):
        for shift in (1, 2, 3):
            self.go(2 + shift, self.block(shift), self.narrow.at[3 + shift], self.place.along_z(shift))

    def wait_z(self):
        total = self.block(0)[...].astype(F32)
        for shift in (1, 2, 3):
            self.arrived(2 + shift, self.narrow.at[3 + shift])
            total = total + self.narrow[3 + shift].astype(F32)
        self.final[...] = total

    def stage_final(self):
        self.go(6, self.final, self.final, self.place.sibling())

    def wait_final(self):
        self.arrived(6, self.final_other)
        self.left(0, self.other)
        self.left(1, self.half(True))
        self.left(2, self.quarter())
        for shift in (1, 2, 3):
            self.left(2 + shift, self.block(shift))
        self.left(6, self.final)


class ReduceSmall(Travel):
    def __init__(self, place, own, acc, wide, mid, narrow, final, send, recv):
        super().__init__(place, send, recv)
        self.own, self.acc, self.wide, self.mid, self.narrow, self.final = own, acc, wide, mid, narrow, final

    def stage_share(self):
        self.go(0, self.own, self.wide, self.place.sibling())

    def wait_share(self):
        self.arrived(0, self.wide)
        self.acc[...] = self.own[...] + self.wide[...]

    def stage_first(self):
        at = self.place
        self.go(1, self.acc.at[:, 1 - at.y], self.mid, at.along_y())

    def wait_first(self):
        at = self.place
        self.arrived(1, self.mid)
        half = self.acc.at[:, at.y]
        half[...] = half[...] + self.mid[...]

    def stage_second(self):
        at = self.place
        self.go(2, self.acc.at[:, at.y, 1 - at.x], self.narrow.at[0:4], at.along_x())

    def wait_second(self):
        at = self.place
        self.arrived(2, self.narrow.at[0:4])
        part = self.acc.at[:, at.y, at.x]
        part[...] = part[...] + self.narrow[0:4]

    def block(self, shift):
        at = self.place
        return self.acc.at[at.other_z(shift), at.y, at.x]

    def stage_z(self):
        for shift in (1, 2, 3):
            self.go(2 + shift, self.block(shift), self.narrow.at[3 + shift], self.place.along_z(shift))

    def wait_z(self):
        at = self.place
        total = self.block(0)[...]
        for shift in (1, 2, 3):
            self.arrived(2 + shift, self.narrow.at[3 + shift])
            total = total + self.narrow[3 + shift]
        self.final[...] = total
        self.left(0, self.own)
        self.left(1, self.acc.at[:, 1 - at.y])
        self.left(2, self.acc.at[:, at.y, 1 - at.x])
        for shift in (1, 2, 3):
            self.left(2 + shift, self.block(shift))


def reduce_scratch(count, rows, d):
    return [
        pltpu.VMEM((count, 4, 2, 2, rows, d), BF16), pltpu.VMEM((count, 4, 2, 2, rows, d), BF16),
        pltpu.VMEM((count, 4, 2, rows, d), BF16), pltpu.VMEM((count, 7, rows, d), BF16),
        pltpu.SemaphoreType.DMA((count, 7)), pltpu.SemaphoreType.DMA((count, 7)), pltpu.SemaphoreType.DMA((count,)),
    ]


def reduce_unit(place, grad, scratch, index, lane, final, unit, other, columns=None):
    acc, wide, mid, narrow, send, recv, local = scratch
    own, theirs = grad(unit, EVERY, EVERY, EVERY), grad(other, EVERY, EVERY, EVERY)
    final_own, final_other = final.at[unit], final.at[other]
    if columns is not None:
        own, theirs = own.at[:, :, :, :, columns], theirs.at[:, :, :, :, columns]
        final_own, final_other = final_own.at[:, columns], final_other.at[:, columns]
    return Reduce(
        place, own, theirs, lane, acc.at[index], wide.at[index], mid.at[index], narrow.at[index], final_own, final_other,
        send.at[index], recv.at[index], local.at[index],
    )


def reduce_round(place, grad, scratch, index, final, columns=None):
    return [
        reduce_unit(
            place, grad, scratch, index + l, l, final, 2 * place.core + l, 2 * (1 - place.core) + l, columns
        )
        for l in range(2)
    ]


def both(lanes, *names):
    for name in names:
        for lane in lanes:
            getattr(lane, name)()


REDUCE_STEPS = (
    ("stage_share",), ("wait_share", "stage_first"), ("wait_first", "stage_second"), ("wait_second", "stage_z"),
    ("wait_z", "stage_final"), ("wait_final",),
)
GATHER_STEPS = (
    ("stage_z",), ("wait_z", "stage_first"), ("wait_first", "stage_second"), ("wait_second", "stage_share"), ("wait_share",),
)


def job(lanes, steps):
    return [lambda names=names: both(lanes, *names) for names in steps]


def plan(jobs, places):
    found, late = {}, []
    for number, (steps, start, spans, *latest) in enumerate(jobs):
        time = start
        allowed = places[:places.index(latest[0]) + 1] if latest else places
        for i, step in enumerate(steps):
            fitting = [place for place in allowed if place[1] >= time] or allowed[-1:] * len(latest)
            if fitting:
                name, time = fitting[0]
                found.setdefault(name, []).append(step)
            else:
                late.append((time, number, step))
            time = time + (spans[i] if i < len(spans) else 0.0)
    return found, [step for _, _, step in sorted(late, key=lambda entry: entry[:2])]


def hook_in(found, name, condition):
    if name in found:

        @pl.when(condition)
        def _():
            for step in found[name]:
                step()


GATHER_PACE = 9.5
GATHER_SPANS = (6.0, 7.0, 10.0, 4.0)
PASS_TIME, PASS_TIMES = 8.5, (1.5, 3.0, 4.5, 6.0, 7.5, 8.5)
FFN_TIME = 5.0
FFN_BACK_TIME = 6.0
REDUCE_SPANS = (4.0, 8.0, 6.0, 8.0, 3.0)
SLIM_SPANS = (3.0, 6.0, 5.0, 6.0, 3.0)
HALVES = (slice(0, 256), slice(256, 512))
HEADS_TIME, HEADS_TIMES = 8.0, (0.0, 1.7, 3.4, 5.1, 6.8)
LAST_TIME = 2.0
FFN_REDUCE_PACE = 4.5
WRITER_SPANS = (8.0, 6.0, 8.0, 3.0)
WRITER_PACE = 3.0


def matrix(block):
    return block.reshape(-1, block.shape[-1])


def forward_kernel(ring, count, *refs):
    refs = list(refs)

    def take(number):
        out = refs[:number]
        del refs[:number]
        return out

    tok_ref, mem_ref, doc_ref, keep_ref = take(4)
    if ring:
        shards = take(7)
        narrow_refs = take(3)
    else:
        attn_ref, w1_ref, w2_ref, vec_in_ref, b1_in_ref = take(5)
    n1_ref, qt_ref, k_ref, v_ref, e_ref, linv_ref, ot_ref, h1_ref, out_ref, res_ref, act_ref, slope_ref, vec_ref = take(13)
    if ring:
        attn_ref, w1_ref, w2_ref, wr_ref, gate_ref = take(5)
    bias_ref, vt_ref, hidden_ref, b1_ref, attn_v, w1_v, w2_v, wsem = take(8)
    seg = tok_ref.shape[1]
    slots = mem_ref.shape[1]
    step = pl.program_id(0)
    load_attn = lambda: pltpu.make_async_copy(attn_ref, attn_v, wsem.at[0])
    load_w1 = lambda: pltpu.make_async_copy(w1_ref, w1_v, wsem.at[1])
    load_w2 = lambda: pltpu.make_async_copy(w2_ref, w2_v, wsem.at[2])
    if ring:
        units, psem, sown_ref, sall_ref, send, recv, local, ssend, srecv, fsend, frecv = take(11)
        place = Place()
        views = [unit_first(attn_ref), unit_first(w1_ref), unit_last(w2_ref), unit_first(wr_ref), unit_last(gate_ref)]
        rounds = []
        for r, view in enumerate(views):
            own = (lambda u: shards[6].at[u]) if r == 4 else (lambda u, r=r: units.at[4 * r + u])
            if r == 0:
                lanes = [
                    FirstGather(place, unit_first(attn_v), own, l, fsend.at[l], frecv.at[l], local.at[r, l]) for l in range(2)
                ]
            else:
                lanes = [Gather(place, view, own, l, send.at[r, l], recv.at[r, l], local.at[r, l]) for l in range(2)]
            rounds.append(lanes)
        small = GatherSmall(place, sall_ref, sown_ref, ssend, srecv)
        packs = [(shards[0], units.at[0:3]), (shards[1], units.at[3])]
        packs += [(shards[2].at[:, j * 512:(j + 1) * 512], units.at[4 + j]) for j in range(4)]
        packs += [(shards[3], units.at[8:12]), (shards[4], units.at[12:15]), (shards[5], units.at[15])]

        def pack(i):
            return pltpu.make_async_copy(packs[i][0], packs[i][1], psem.at[i])

        passes = [((s, i), PASS_TIME * s + PASS_TIMES[i]) for s in range(count) for i in range(len(PASS_TIMES))]
        jobs = []
        for r in range(1, 5):
            steps = job(rounds[r], GATHER_STEPS)
            if r in (1, 2):
                share = steps[-1]
                load = load_w1 if r == 1 else load_w2
                steps[-1] = lambda share=share, load=load: (share(), load().start())
            latest = (passes[-1],) if r in (1, 2) else ()
            if r == 1:
                jobs.append((steps[1:], 0.0, GATHER_SPANS[1:]) + latest)
            else:
                jobs.append((steps, GATHER_PACE * (r - 1) - GATHER_SPANS[0], GATHER_SPANS) + latest)
        places = list(passes)
        at_load = PASS_TIME * count
        places += [((count + s, i), at_load + FFN_TIME * (s + i / 4)) for s in range(count) for i in range(4)]
        found, rest = plan(jobs, places)

    def hook(name, extra=True):
        if ring:
            hook_in(found, name, (step == name[0]) & extra)

    @pl.when(step < count)
    def _():
        if ring:

            @pl.when(step == 0)
            def _():
                for i in range(len(packs)):
                    pack(i).start()
                bias, gbias, gains = (ref[...].astype(F32) for ref in narrow_refs)
                narrow = jnp.concatenate([gbias, gains], 0)
                lane = lax.broadcasted_iota(jnp.int32, (4, 128), 1) // narrow.shape[1]
                narrow = jnp.where(lane == lax.rem(place.dp, 4), jnp.concatenate([narrow] * 4, 1), 0.0)
                sown_ref[...] = jnp.concatenate([bias, narrow, jnp.zeros((3, 128), F32)], 0)
                place.greet()
                small.stage_z()
                pack(0).wait()
                pack(1).wait()
                both(rounds[0], "begin")
                for i in range(2, len(packs)):
                    pack(i).wait()
        else:

            @pl.when(step == 0)
            def _():
                load_attn().start()
                load_w1().start()
                load_w2().start()
                vec_ref[...] = vec_in_ref[...]
                b1_ref[...] = b1_in_ref[...]
                load_attn().wait()

        keep = keep_ref[0][:, 0:1]
        docs = doc_ref[0].astype(F32)
        key_docs = jnp.broadcast_to(docs, (128, seg)).T
        slot_docs = jnp.broadcast_to(keep - 1.0, (slots, 128))
        key_docs = jnp.concatenate([slot_docs, jnp.full((128 - slots, 128), -1.0, F32), key_docs], 0)
        for block, (first, last_row) in enumerate(SPANS):
            length = last_row - first
            position = lax.broadcasted_iota(jnp.int32, (length, BLOCK), 0) + (first - 128 - block * BLOCK)
            position = position <= lax.broadcasted_iota(jnp.int32, (length, BLOCK), 1)
            same = key_docs[first:last_row] == docs[:, block * BLOCK:(block + 1) * BLOCK]
            bias_ref[STARTS[block]:STARTS[block] + length, :] = jnp.where(same & position, 0.0, -1e30)
        if ring:

            @pl.when(step == 0)
            def _():
                small.wait_z()
                small.stage_first()
                for shift in FirstGather.SHIFTS[1:]:
                    for lane in rounds[0]:
                        lane.column_block(shift)
                both(rounds[0], "column_done")
                small.wait_first()
                small.stage_second()
                for shift in FirstGather.SHIFTS:
                    for lane in rounds[0]:
                        lane.far_block(shift)
                both(rounds[1], "stage_z")
                both(rounds[0], "far_done")
                small.wait_second()
                for m in range(4):
                    total = sall_ref[m, 0, 0] + sall_ref[m, 0, 1] + sall_ref[m, 1, 0] + sall_ref[m, 1, 1]
                    vec_ref[:, m * 128:(m + 1) * 128] = jnp.concatenate([total[1:8], total[0:1]], 0)
                    for i in range(4):
                        b1_ref[m, :, i * 128:(i + 1) * 128] = sall_ref[m, i // 2, i % 2, 0:1, :]
                both(rounds[0], "rest")
                both(rounds[0], "done")
                pltpu.make_async_copy(attn_v, attn_ref, wsem.at[0]).start()

        x = tok_ref[0].astype(F32)
        gain_one = vec_ref[1:2, :]
        hat, _ = norm_parts(x)
        n1t = (hat * gain_one).astype(BF16)
        hat, _ = norm_parts(mem_ref[0] * keep)
        n1_ref[0, 0:slots, :] = (hat * gain_one).astype(BF16)
        n1_ref[0, slots:128, :] = jnp.zeros((128 - slots, x.shape[1]), BF16)
        n1_ref[0, 128:, :] = n1t
        qt_ref[0] = (dot_nt(matrix(attn_v[0]).T, n1t) * 0.125).astype(BF16)
        n1 = n1_ref[0]
        keys = dot(n1, matrix(attn_v[1])).astype(BF16)
        v = dot(n1, matrix(attn_v[2])).astype(BF16)
        for pair in range(4):
            k_ref[0, pair] = keys[:, pair * 128:(pair + 1) * 128]
            v_ref[0, pair] = v[:, pair * 128:(pair + 1) * 128]
        vt_ref[...] = v.T
        for s in range(count):
            hook((s, 0))

        def one_pair(pair, carry):
            lanes = pl.ds(pl.multiple_of(pair * 128, 128), 128)
            for block, (first, last_row) in enumerate(SPANS):
                start = STARTS[block] - first
                columns = pl.ds(block * BLOCK, BLOCK)
                query = qt_ref[0, lanes, columns]
                zero = jnp.zeros((64, BLOCK), BF16)
                query = jnp.concatenate(
                    [jnp.concatenate([query[0:64], zero], 1), jnp.concatenate([zero, query[64:128]], 1)], 0
                )
                scores, largest = [], None
                for row in range(first, last_row, 128):
                    bias = bias_ref[start + row:start + row + 128, :]
                    part = dot(k_ref[0, pair, row:row + 128, :], query) + jnp.concatenate([bias, bias], 1)
                    scores.append(part)
                    part = jnp.max(part.reshape(16, 8, 256), axis=0)
                    largest = part if largest is None else jnp.maximum(largest, part)
                largest = jnp.max(largest, axis=0, keepdims=True)
                es, total = [], None
                for i, row in enumerate(range(first, last_row, 128)):
                    e = jnp.exp(scores[i] - largest)
                    part = jnp.sum(e.reshape(16, 8, 256), axis=0)
                    total = part if total is None else total + part
                    es.append(e.astype(BF16))
                    e_ref[0, pair, start + row:start + row + 128, :] = es[-1]
                linv = 1.0 / jnp.sum(total, axis=0, keepdims=True)
                linv_ref[0, pair, block, :, :] = linv
                e = jnp.concatenate(es, 0)
                values = vt_ref[lanes, first:last_row]
                mixed = [
                    dot(values[i * 64:(i + 1) * 64], e[:, i * 128:(i + 1) * 128]) * linv[:, i * 128:(i + 1) * 128]
                    for i in range(2)
                ]
                ot_ref[0, lanes, columns] = jnp.concatenate(mixed, 0).astype(BF16)
            for s in range(count):
                for i in range(4):
                    hook((s, 1 + i), pair == i)
            return carry

        lax.fori_loop(0, 4, one_pair, 0)
        h1 = x + dot(ot_ref[0].T, matrix(attn_v[3]))
        h1_ref[0] = h1
        hidden_ref[step] = h1
        for s in range(count):
            hook((s, 5))

    @pl.when(step >= count)
    def _():
        @pl.when(step == count)
        def _():
            load_w1().wait()
            load_w2().wait()

        h1 = hidden_ref[step - count]
        hat, _ = norm_parts(h1)
        n2 = (hat * vec_ref[2:3, :]).astype(BF16)
        tall = seg // 2
        for block in range(2):
            rows = slice(block * tall, (block + 1) * tall)
            result = h1[rows]
            for part in range(8):
                columns = slice((part % 2) * 256, (part % 2) * 256 + 256)
                before = dot(n2[rows], matrix(w1_v[part // 2])[:, columns]) + b1_ref[part // 2][:, columns]
                cdf = 0.5 + 0.5 * lax.erf(before * 0.7071067811865476)
                active = (before * cdf).astype(BF16)
                act_ref[0, part // 2, rows, columns] = active
                slope = cdf + before * jnp.exp(before * before * -0.5) * 0.3989422804014327
                slope_ref[0, part // 2, rows, columns] = slope.astype(BF16)
                result = result + dot(active, matrix(w2_v[part // 2])[columns, :])
                if part in (3, 7):
                    for s in range(count, 2 * count):
                        hook((s, 2 * block + (part == 7)))
            out_ref[0, rows, :] = result.astype(BF16)
        res_ref[0] = result
        if ring:

            @pl.when(step == 2 * count - 1)
            def _():
                pltpu.make_async_copy(attn_v, attn_ref, wsem.at[0]).wait()
                for step_left in rest:
                    step_left()
                for lanes in rounds:
                    both(lanes, "finish")
                small.finish()


ANY = pl.BlockSpec(memory_space=pl.ANY)


def full_spec(shape):
    return pl.BlockSpec(shape, lambda i: (0,) * len(shape), pipeline_mode=pl.Buffered(1))


def phase_spec(shape, first, count):
    return pl.BlockSpec((1,) + shape, lambda i: (jnp.clip(i - first, 0, count - 1),) + (0,) * len(shape))


def call_forward(ring, tokens, memory, docs, keep, weights):
    n, seg, d = tokens.shape
    slots = memory.shape[1]
    early = [
        ((seg + 128, d), BF16), ((d, seg), BF16), ((4, seg + 128, 128), BF16), ((4, seg + 128, 128), BF16), ((4, LIVE, 256), BF16),
        ((4, 4, 1, 256), F32), ((d, seg), BF16), ((seg, d), F32),
    ]
    late = [((seg, d), BF16), ((seg // 2, d), F32), ((4, seg, 512), BF16), ((4, seg, 512), BF16)]
    units = (4, 4, 2, 2, 32, d)
    unit_shapes = [units, units, (4, 2, 2, 4, 32, d), units, (4, 2, 2, 4, 16, d)]
    out_shape = [jax.ShapeDtypeStruct((n,) + shape, kind) for shape, kind in early + late]
    out_shape += [jax.ShapeDtypeStruct((8, d), F32)]
    out_specs = [phase_spec(shape, 0, n) for shape, _ in early] + [phase_spec(shape, n, n) for shape, _ in late]
    out_specs += [full_spec((8, d))]
    in_specs = [phase_spec((seg, d), 0, n), phase_spec((slots, d), 0, n), phase_spec((1, seg), 0, n), phase_spec((1, 128), 0, n)]
    scratch = [
        pltpu.VMEM((LIVE, 128), F32), pltpu.VMEM((d, seg + 128), BF16), pltpu.VMEM((n, seg, d), F32), pltpu.VMEM((4, 1, d), F32), pltpu.VMEM(unit_shapes[0], BF16),
        pltpu.VMEM(unit_shapes[1], BF16), pltpu.VMEM(unit_shapes[2], BF16), pltpu.SemaphoreType.DMA((3,)),
    ]
    params = dict(vmem_limit_bytes=VMEM_LIMIT)
    if ring:
        in_specs += [ANY] * 7 + [full_spec(array.shape) for array in weights[7:]]
        out_shape += [jax.ShapeDtypeStruct(shape, BF16) for shape in unit_shapes]
        out_specs += [ANY] * 5
        scratch += [
            pltpu.VMEM((16, 32, d), BF16), pltpu.SemaphoreType.DMA((9,)), pltpu.VMEM((8, 128), F32),
            pltpu.VMEM((4, 2, 2, 8, 128), F32), pltpu.SemaphoreType.DMA((5, 2, 7)), pltpu.SemaphoreType.DMA((5, 2, 7)),
            pltpu.SemaphoreType.DMA((5, 2)), pltpu.SemaphoreType.DMA((5,)), pltpu.SemaphoreType.DMA((5,)),
            pltpu.SemaphoreType.DMA((2, 20)), pltpu.SemaphoreType.DMA((2, 20)),
        ]
        params.update(collective_id=0, has_side_effects=True)
    else:
        in_specs += [ANY] * 3 + [full_spec((8, d)), full_spec((4, 1, d))]
    return pl.pallas_call(
        functools.partial(forward_kernel, ring, n),
        grid=(2 * n,),
        out_shape=out_shape,
        in_specs=in_specs,
        out_specs=out_specs,
        scratch_shapes=scratch,
        compiler_params=pltpu.CompilerParams(**params),
        name="gather_forward" if ring else "forward_rows",
    )(tokens, memory, docs, keep, *weights)


def writer_all(
    gate_done, read_done, res_ref, mem_ref, memgrad_ref, doc_ref, keep_ref, wr_ref, gate_ref, vec_ref,
    newmem_ref, dres_ref, dkept_ref, gwr_ref, ggate_ref, ggb_ref,
    n3_ref, ns_ref, kept_ref, sq_ref, tk_ref, tv_ref, p_ref, wt_ref, dsq_ref, dlog_ref, dw_ref,
):
    n, half, d = res_ref.shape
    slots = mem_ref.shape[1]
    gain = vec_ref[3:4, :]

    biases = []
    for i in range(n):
        rows, small = slice(i * half, (i + 1) * half), slice(i * slots, (i + 1) * slots)
        hat, _ = norm_parts(res_ref[i])
        n3_ref[rows, :] = (hat * gain).astype(BF16)
        kept = mem_ref[i] * keep_ref[i][:, 0:1]
        kept_ref[small, :] = kept
        hat, _ = norm_parts(kept)
        ns_ref[small, :] = (hat * gain).astype(BF16)
        docs = doc_ref[i].astype(F32)
        bias = jnp.where(docs == jnp.max(docs), 0.0, -1e30)[:, docs.shape[1] - half:]
        biases.append(jnp.broadcast_to(bias, (128, half)).T)
    tk_ref[...] = dot(n3_ref[...], wr_ref[1]).astype(BF16)
    tv_ref[...] = dot(n3_ref[...], wr_ref[2]).astype(BF16)
    sq_ref[...] = (dot(ns_ref[...], wr_ref[0]) * 0.125).astype(BF16)
    low_half = lax.broadcasted_iota(jnp.int32, (1, 128), 1) < 64

    def halves(rows):
        zero = jnp.zeros_like(rows)
        return jnp.concatenate([jnp.where(low_half, rows, zero), jnp.where(low_half, zero, rows)], 0)

    for i in range(n):
        rows, small = slice(i * half, (i + 1) * half), slice(i * slots, (i + 1) * slots)
        for pair in range(4):
            lanes = slice(pair * 128, pair * 128 + 128)
            scores = dot_nt(tk_ref[rows, lanes], halves(sq_ref[small, lanes])) + biases[i]
            e = jnp.exp(scores - jnp.max(scores, axis=0, keepdims=True))
            p = e * (1.0 / jnp.sum(e, axis=0, keepdims=True))
            p_ref[i, pair] = p
            mixed = dot_tn(p.astype(BF16), tv_ref[rows, lanes])
            wt_ref[small, lanes] = jnp.where(low_half, mixed[:slots], mixed[slots:]).astype(BF16)

    def put(ref, index, value):
        ref[index] = value.astype(BF16).reshape(ref.shape[1:])

    write = dot(wt_ref[...], wr_ref[3])
    kept = kept_ref[...]
    write_low = write.astype(BF16)
    kept_low = kept.astype(BF16)
    logit = dot(kept_low, gate_ref[0]) + dot(write_low, gate_ref[1]) + vec_ref[0:1, :]
    gate = jax.nn.sigmoid(logit)
    new = gate * kept + (1.0 - gate) * write
    memgrad = memgrad_ref[...].reshape(n * slots, d)
    newmem_ref[...] = new.reshape(n, slots, d)
    dlogit = memgrad * (kept - write) * gate * (1.0 - gate)
    dlog_ref[...] = dlogit.astype(BF16)
    dlow = dlog_ref[...]
    ggb_ref[...] = jnp.sum(dlow.astype(F32), axis=0, keepdims=True)
    ggate_ref[0:2] = dot_tn(kept_low, dlow).astype(BF16).reshape((2,) + ggate_ref.shape[1:])
    ggate_ref[2:4] = dot_tn(write_low, dlow).astype(BF16).reshape((2,) + ggate_ref.shape[1:])
    gate_done()
    dkept = memgrad * gate + dot_nt(dlow, gate_ref[0])
    dwrite = memgrad * (1.0 - gate) + dot_nt(dlow, gate_ref[1])
    dkept_ref[...] = dkept.reshape(n, slots, d)
    dw_low = dwrite.astype(BF16)
    put(gwr_ref, 3, dot_tn(wt_ref[...], dw_low))
    dw_ref[...] = dot_nt(dw_low, wr_ref[3]).astype(BF16)

    for i in range(n):
        rows, small = slice(i * half, (i + 1) * half), slice(i * slots, (i + 1) * slots)
        for pair in range(4):
            lanes = slice(pair * 128, pair * 128 + 128)
            p = p_ref[i, pair]
            grads = halves(dw_ref[small, lanes])
            keys, values = tk_ref[rows, lanes], tv_ref[rows, lanes]
            dp = dot_nt(values, grads)
            ds = (p * (dp - jnp.sum(dp * p, axis=0, keepdims=True))).astype(BF16)
            dq = dot_tn(ds, keys) * 0.125
            dsq_ref[small, lanes] = jnp.where(low_half, dq[:slots], dq[slots:]).astype(BF16)
            tk_ref[rows, lanes] = dot(ds, halves(sq_ref[small, lanes])).astype(BF16)
            tv_ref[rows, lanes] = dot(p.astype(BF16), grads).astype(BF16)
    read_done()
    put(gwr_ref, 0, dot_tn(ns_ref[...], dsq_ref[...]))
    put(gwr_ref, 1, dot_tn(n3_ref[...], tk_ref[...]))
    put(gwr_ref, 2, dot_tn(n3_ref[...], tv_ref[...]))
    grad = dot_nt(dsq_ref[...], wr_ref[0])
    hat, rstd = norm_parts(kept_ref[...])
    dkept_ref[...] += norm_back(grad, hat, rstd, gain).reshape(n, slots, d)

    for i in range(n):
        rows = slice(i * half, (i + 1) * half)
        grad = dot_nt(tk_ref[rows, :], wr_ref[1]) + dot_nt(tv_ref[rows, :], wr_ref[2])
        hat, rstd = norm_parts(res_ref[i])
        dres_ref[i] = norm_back(grad, hat, rstd, gain)


def ffn_back_kernel(ring, count, *refs):
    refs = list(refs)

    def take(number):
        out = refs[:number]
        del refs[:number]
        return out

    writer_in = take(8)
    vec_ref = writer_in[7]
    og_ref, h1_ref, act_ref, slope_ref, ot_ref, linv_ref, w1_ref, w2_ref, attn_ref = take(9)
    newmem_ref, dkept_ref, ggb_ref, gb_ref, gw1_ref, gw2_ref, gwo_ref, dh_ref, dot_ref, gwr_out, ggate_out = take(11)
    writer_scratch = take(11)
    dres_ref, acc1_ref, acc2_ref, acco_ref, w1_v, w2_v, wo_v, wsem = take(8)
    step = pl.program_id(0)
    seg = og_ref.shape[1]
    loads = lambda: [
        pltpu.make_async_copy(w1_ref, w1_v, wsem.at[0]), pltpu.make_async_copy(w2_ref, w2_v, wsem.at[1]),
        pltpu.make_async_copy(attn_ref.at[3], wo_v, wsem.at[2]),
    ]
    if ring:
        gwr_ref, ggate_ref, fwr_ref, fgate_ref = take(4)
        wide_scratch, slim_scratch = take(7), take(7)
        place = Place()
        writer_rounds = [
            reduce_round(place, unit_first(gwr_ref), wide_scratch, 2 * i, fwr_ref, half) for i, half in enumerate(HALVES)
        ]
        gate_round = reduce_round(place, unit_last(ggate_ref), slim_scratch, 0, fgate_ref)
        jobs = [
            (job(gate_round, REDUCE_STEPS)[2:], 0.0, WRITER_SPANS[1:]),
            (job(writer_rounds[0], REDUCE_STEPS)[1:], 1.5, WRITER_SPANS),
            (job(writer_rounds[1], REDUCE_STEPS)[1:], 1.5 + WRITER_PACE, WRITER_SPANS),
        ]
        places = [((1 + s, i), FFN_BACK_TIME * (s + i / 4)) for s in range(count) for i in range(4)]
        found, rest = plan(jobs, places)
    else:
        gwr_ref, ggate_ref = gwr_out, ggate_out

    @pl.when(step == 0)
    def _():
        for load in loads():
            load.start()
        if ring:
            place.greet()
        acc1_ref[...] = jnp.zeros_like(acc1_ref)
        acc2_ref[...] = jnp.zeros_like(acc2_ref)
        acco_ref[...] = jnp.zeros_like(acco_ref)
        gb_ref[...] = jnp.zeros_like(gb_ref)
        gate_done = (lambda: both(gate_round, "stage_share")) if ring else (lambda: None)
        read_done = (lambda: both(gate_round, "wait_share", "stage_first")) if ring else (lambda: None)
        writer_all(
            gate_done, read_done, *writer_in, newmem_ref, dres_ref, dkept_ref, gwr_ref, ggate_ref, ggb_ref, *writer_scratch
        )
        if ring:
            both(writer_rounds[0] + writer_rounds[1], "stage_share")
        for load in loads():
            load.wait()

    @pl.when(step > 0)
    def _():
        top = og_ref[0, 0:seg // 2, :].astype(F32)
        bottom = og_ref[0, seg // 2:, :].astype(F32) + dres_ref[step - 1]
        dresult = jnp.concatenate([top, bottom], 0)
        low = dresult.astype(BF16)
        h1 = h1_ref[0]
        hat, rstd = norm_parts(h1)
        gain = vec_ref[2:3, :]
        n2t = (hat * gain).astype(BF16).T
        lowt = low.T
        grad = jnp.zeros_like(dresult)
        for part in range(4):
            if ring:
                for s in range(1, 1 + count):
                    hook_in(found, (s, part), step == s)
            acc2_ref[part] += dot(lowt, act_ref[0, part])
            dbefore = (dot_nt(low, w2_v[part]) * slope_ref[0, part].astype(F32)).astype(BF16)
            gb_ref[part] += jnp.sum(dbefore.astype(F32), axis=0, keepdims=True)
            acc1_ref[part] += dot(n2t, dbefore)
            grad = grad + dot_nt(dbefore, w1_v[part])
        dh = dresult + norm_back(grad, hat, rstd, gain)
        dh_ref[0] = dh
        dlow = dh.astype(BF16)
        mixed_grad = dot_nt(wo_v[...], dlow)
        for pair in range(4):
            for block in range(seg // BLOCK):
                columns = slice(block * BLOCK, (block + 1) * BLOCK)
                for i in range(2):
                    features = slice(pair * 128 + i * 64, pair * 128 + i * 64 + 64)
                    scale = linv_ref[0, pair, block, :, i * 128:(i + 1) * 128]
                    dot_ref[0, features, columns] = (mixed_grad[features, columns] * scale).astype(BF16)
        acco_ref[...] += dot(ot_ref[0], dlow)

        @pl.when(step == count)
        def _():
            stores = [
                pltpu.make_async_copy(w1_v, gw1_ref, wsem.at[0]), pltpu.make_async_copy(w2_v, gw2_ref, wsem.at[1]),
                pltpu.make_async_copy(wo_v, gwo_ref, wsem.at[2]),
            ]
            w1_v[...] = acc1_ref[...].astype(BF16)
            stores[0].start()
            for part in range(4):
                w2_v[part] = acc2_ref[part].T.astype(BF16)
            stores[1].start()
            wo_v[...] = acco_ref[...].astype(BF16)
            stores[2].start()
            if ring:
                for step_left in rest:
                    step_left()
                gwr_out[...] = fwr_ref[...]
                ggate_out[...] = fgate_ref[...]
            for store in stores:
                store.wait()


def call_ffn_back(ring, res, memory, memory_grad, docs, keep, wr, gate, vec, out_grad, h1, act, slope, ot, linv, w1, w2, attn):
    n, half, d = res.shape
    seg = 2 * half
    slots = memory.shape[1]
    rows, small = n * half, n * slots
    writer_args = (res, memory, memory_grad, docs, keep, wr, gate, vec)
    units = (4, 4, 2, 2, 32, d)
    gate_units = (4, 2, 2, 4, 16, d)
    if ring:
        grads = [((4, 32, d), F32), ((4, 16, d), F32)]
    else:
        grads = [(units, BF16), (gate_units, BF16)]
    whole = [((n, slots, d), F32), ((n, slots, d), F32), ((1, d), F32), ((4, 1, d), F32)]
    stored = [((4, d, d), BF16), ((4, d, d), BF16), ((d, d), BF16)]
    scratch = [
        pltpu.VMEM((rows, d), BF16), pltpu.VMEM((small, d), BF16), pltpu.VMEM((small, d), F32), pltpu.VMEM((small, d), BF16),
        pltpu.VMEM((rows, d), BF16), pltpu.VMEM((rows, d), BF16), pltpu.VMEM((n, 4, half, 2 * slots), F32),
        pltpu.VMEM((small, d), BF16), pltpu.VMEM((small, d), BF16), pltpu.VMEM((small, d), BF16), pltpu.VMEM((small, d), BF16),
        pltpu.VMEM((n, half, d), F32), pltpu.VMEM((4, d, d), F32), pltpu.VMEM((4, d, d), F32), pltpu.VMEM((d, d), F32),
        pltpu.VMEM((4, d, d), BF16), pltpu.VMEM((4, d, d), BF16), pltpu.VMEM((d, d), BF16), pltpu.SemaphoreType.DMA((3,)),
    ]
    params = dict(vmem_limit_bytes=VMEM_LIMIT)
    if ring:
        scratch += [pltpu.VMEM(units, BF16), pltpu.VMEM(gate_units, BF16)]
        scratch += [pltpu.VMEM((4, 32, d), F32), pltpu.VMEM((4, 16, d), F32)]
        scratch += reduce_scratch(4, 32, d // 2) + reduce_scratch(2, 16, d)
        params.update(collective_id=1, has_side_effects=True)
    return pl.pallas_call(
        functools.partial(ffn_back_kernel, ring, n),
        grid=(n + 1,),
        out_shape=[jax.ShapeDtypeStruct(shape, kind) for shape, kind in whole + stored]
        + [jax.ShapeDtypeStruct((n, seg, d), F32), jax.ShapeDtypeStruct((n, d, seg), BF16)]
        + [jax.ShapeDtypeStruct(shape, kind) for shape, kind in grads],
        in_specs=[full_spec(array.shape) for array in writer_args] + [
            phase_spec((seg, d), 1, n), phase_spec((seg, d), 1, n), phase_spec((4, seg, 512), 1, n),
            phase_spec((4, seg, 512), 1, n), phase_spec((d, seg), 1, n), phase_spec((4, 4, 1, 256), 1, n), ANY, ANY, ANY,
        ],
        out_specs=[full_spec(shape) for shape, _ in whole] + [ANY] * 3 + [phase_spec((seg, d), 1, n), phase_spec((d, seg), 1, n)]
        + [full_spec(shape) for shape, _ in grads],
        scratch_shapes=scratch,
        compiler_params=pltpu.CompilerParams(**params),
        name="ffn_back",
    )(*writer_args, out_grad, h1, act, slope, ot, linv, w1, w2, attn)


def attn_back_kernel(ring, count, *refs):
    refs = list(refs)

    def take(number):
        out = refs[:number]
        del refs[:number]
        return out

    qt_ref, k_ref, v_ref, e_ref, ot_ref, dot_ref = take(6)
    tok_ref, mem_ref, keep_ref, dkept_ref, dh_ref = take(5)
    n1_from, attn_from, vec_ref = take(3)
    if ring:
        ggb_ref, gb_ref, gw1_ref, gw2_ref, gwo_ref = take(5)
    gtok_ref, gmem_ref = take(2)
    if ring:
        fqkv_ref, fo_ref, fw1_ref, fw2_ref, fsmall_ref = take(5)
    else:
        (gqkv_ref,) = take(1)
    dqt_ref, dkl_ref, dvl_ref, dk_ref, dv_ref, qp_ref, dp_ref, n1_ref, attn_ref, wsem = take(10)
    load_n1 = lambda: pltpu.make_async_copy(n1_from, n1_ref, wsem.at[0])
    load_attn = lambda: pltpu.make_async_copy(attn_from.at[0:3], attn_ref, wsem.at[1])
    step = pl.program_id(0)
    seg = tok_ref.shape[1]
    d = tok_ref.shape[2]
    slots = mem_ref.shape[1]
    if ring:
        gqkv_ref, ffn_final, out_final, heads_final = take(4)
        wide_scratch, out_scratch, heads_scratch = take(7), take(7), take(7)
        sown, sacc, swide, smid, snarrow, ssend, srecv = take(7)
        place = Place()
        ffn_rounds = [
            reduce_round(place, grad, wide_scratch, 4 * j + 2 * i, ffn_final.at[j], half)
            for j, grad in ((1, unit_last(gw2_ref)), (0, unit_first(gw1_ref))) for i, half in enumerate(HALVES)
        ]
        out_unit = reduce_unit(place, unit_last(gwo_ref), out_scratch, 0, 0, out_final, place.core, 1 - place.core)
        heads = [
            reduce_unit(
                place, unit_first(gqkv_ref.at[p]), heads_scratch, p, p % 2, heads_final.at[p], place.core, 1 - place.core
            )
            for p in range(4)
        ]
        small = ReduceSmall(place, sown, sacc, swide, smid, snarrow, fsmall_ref, ssend, srecv)
        jobs = [(job(ffn_rounds[i], REDUCE_STEPS), FFN_REDUCE_PACE * i, REDUCE_SPANS) for i in range(4)]
        jobs.append((job([out_unit], REDUCE_STEPS), FFN_REDUCE_PACE * 4, SLIM_SPANS))
        jobs.append((job([small], REDUCE_STEPS[:4] + (("wait_z",),)), FFN_REDUCE_PACE * 4 + 1.0, SLIM_SPANS))
        for p in range(4):
            jobs.append((job([heads[p]], REDUCE_STEPS)[1:], HEADS_TIME * (p + 1) + SLIM_SPANS[0], SLIM_SPANS[1:]))
        places = [((p, i), HEADS_TIME * p + HEADS_TIMES[i]) for p in range(4) for i in range(5)]
        places += [((4 + s, 0), 4 * HEADS_TIME + LAST_TIME * (s + 1)) for s in range(count)]
        found, rest = plan(jobs, places)

    def hook(name, extra=True):
        if ring:
            hook_in(found, name, (step == name[0]) & extra)

    @pl.when(step < 4)
    def _():
        @pl.when(step == 0)
        def _():
            load_n1().start()
            load_attn().start()
            if ring:
                place.greet()
                for m in range(4):
                    for i in range(4):
                        lanes = slice(i * 128, (i + 1) * 128)
                        sown[m, i // 2, i % 2] = jnp.concatenate(
                            [gb_ref[m, :, lanes], ggb_ref[:, m * 128:(m + 1) * 128], jnp.zeros((6, 128), F32)], 0
                        )
            qp_ref[...] = jnp.zeros_like(qp_ref)
            dp_ref[...] = jnp.zeros_like(dp_ref)

        features = pl.ds(pl.multiple_of(step * 128, 128), 128)

        def one_segment(s, carry):
            for p in range(4):
                for i in range(4):
                    hook((p, i), s == min(i, count - 1))
            dk_ref[...] = jnp.zeros_like(dk_ref)
            dv_ref[...] = jnp.zeros_like(dv_ref)
            for block, (first, last) in enumerate(SPANS):
                start = STARTS[block]
                columns = slice(block * BLOCK, (block + 1) * BLOCK)
                mixed_grad = dot_ref[s, :, columns]
                delta = mixed_grad.astype(F32) * ot_ref[s, :, columns].astype(F32)
                delta = jnp.concatenate(
                    [jnp.sum(delta[0:64], axis=0, keepdims=True), jnp.sum(delta[64:128], axis=0, keepdims=True)], 1
                )
                held = dp_ref.at[block]
                diagonal_pair(held, mixed_grad)
                query = qp_ref.at[block]
                diagonal_pair(query, qt_ref[s, :, columns])
                e = e_ref[s, 0, start:start + last - first, :]
                dp = dot(v_ref[s, 0, first:last, :], held[...])
                ds = (e.astype(F32) * (dp - delta)).astype(BF16)
                dv_ref[first:last, :] += dot_nt(e, held[...])
                dk_ref[first:last, :] += dot_nt(ds, query[...])
                dq = dot_tn(k_ref[s, 0, first:last, :], ds) * 0.125
                dqt_ref[s, features, columns] = jnp.concatenate([dq[0:64, 0:128], dq[64:128, 128:256]], 0).astype(BF16)
            dkl_ref[s, step] = dk_ref[...].astype(BF16)
            dvl_ref[s, step] = dv_ref[...].astype(BF16)
            return carry

        lax.fori_loop(0, count, one_segment, 0)
        for p in range(4):
            hook((p, 4))

        @pl.when(step == 0)
        def _():
            load_n1().wait()
            load_attn().wait()

        gq = dot(dqt_ref[0, features, :], n1_ref[0, 128:, :])
        gkv = dot_tn(n1_ref[0], jnp.concatenate([dkl_ref[0, step], dvl_ref[0, step]], 1))
        for s in range(1, count):
            gq = gq + dot(dqt_ref[s, features, :], n1_ref[s, 128:, :])
            gkv = gkv + dot_tn(n1_ref[s], jnp.concatenate([dkl_ref[s, step], dvl_ref[s, step]], 1))
        both_cores = (2, 16, 16, 128)
        parts = [part.astype(BF16).reshape(16, 2, 16, 128) for part in (gq.T, gkv[:, 0:128], gkv[:, 128:256])]
        for i, part in enumerate(parts):
            for core in range(2):
                gqkv_ref[step, core, :, :, :, i * 16:(i + 1) * 16, :] = part[:, core].reshape(4, 2, 2, 16, 128)
        if ring:
            for p in range(4):

                @pl.when(step == p)
                def _(p=p):
                    both([heads[p]], "stage_share")

    @pl.when(step >= 4)
    def _():
        here = step - 4
        gain = vec_ref[1:2, :]
        dk = jnp.concatenate([dkl_ref[here, p] for p in range(4)], 1)
        dv = jnp.concatenate([dvl_ref[here, p] for p in range(4)], 1)
        grad = dot_nt(dk, attn_ref[1]) + dot_nt(dv, attn_ref[2])
        slot_grad = grad[0:slots]
        kept = mem_ref[0] * keep_ref[0][:, 0:1]
        hat, rstd = norm_parts(kept)
        gmem_ref[0] = (dkept_ref[0] + norm_back(slot_grad, hat, rstd, gain)) * keep_ref[0][:, 0:1]
        grad = grad[128:] + dot_nt(dqt_ref[here].T, attn_ref[0])
        hat, rstd = norm_parts(tok_ref[0].astype(F32))
        gtok_ref[0] = dh_ref[0] + norm_back(grad, hat, rstd, gain)
        for s in range(count):
            hook((4 + s, 0))

        if ring:

            @pl.when(step == 3 + count)
            def _():
                for step_left in rest:
                    step_left()
                fqkv_ref[...] = heads_final[...]
                fo_ref[...] = out_final[...]
                fw1_ref[...] = ffn_final[0]
                fw2_ref[...] = ffn_final[1]


def call_attn_back(
    ring, dh, tokens, memory, keep, n1, qt, k, v, e, ot, mixed_grad, dkept, attn, vec, extra
):
    n, seg, d = tokens.shape
    slots = memory.shape[1]
    shapes = [((n, seg, d), F32), ((n, slots, d), F32)]
    out_specs = [phase_spec((seg, d), 4, n), phase_spec((slots, d), 4, n)]

    def pair_spec(shape, axis):
        return pl.BlockSpec(shape, lambda i: tuple(jnp.minimum(i, 3) if j == axis else 0 for j in range(len(shape))))

    in_specs = [
        pair_spec((n, 128, seg), 1), pair_spec((n, 1, seg + 128, 128), 1), pair_spec((n, 1, seg + 128, 128), 1),
        pair_spec((n, 1, LIVE, 256), 1), pair_spec((n, 128, seg), 1), pair_spec((n, 128, seg), 1),
        phase_spec((seg, d), 4, n), phase_spec((slots, d), 4, n), phase_spec((1, 128), 4, n), phase_spec((slots, d), 4, n),
        phase_spec((seg, d), 4, n),
        ANY, ANY, full_spec(vec.shape),
    ]
    heads = (4, 2, 4, 2, 2, 48, 128)
    scratch = [
        pltpu.VMEM((n, d, seg), BF16), pltpu.VMEM((n, 4, seg + 128, 128), BF16), pltpu.VMEM((n, 4, seg + 128, 128), BF16),
        pltpu.VMEM((seg + 128, 128), F32), pltpu.VMEM((seg + 128, 128), F32), pltpu.VMEM((4, 128, 256), BF16),
        pltpu.VMEM((4, 128, 256), BF16), pltpu.VMEM(n1.shape, BF16), pltpu.VMEM((3, d, d), BF16), pltpu.SemaphoreType.DMA((2,)),
    ]
    params = dict(vmem_limit_bytes=VMEM_LIMIT)
    if ring:
        in_specs += [full_spec(extra[0].shape), full_spec(extra[1].shape), ANY, ANY, ANY]
        more = [((4, 2, 48, 128), F32), ((2, 16, d), F32), ((4, 32, d), F32), ((4, 32, d), F32), ((8, 128), F32)]
        scratch += [
            pltpu.VMEM(heads, BF16), pltpu.VMEM((2, 4, 32, d), F32), pltpu.VMEM((2, 16, d), F32),
            pltpu.VMEM((4, 2, 48, 128), F32),
        ]
        scratch += reduce_scratch(8, 32, d // 2) + reduce_scratch(1, 16, d) + reduce_scratch(4, 48, 128)
        scratch += [pltpu.VMEM((4, 2, 2, 8, 128), F32)] * 3 + [
            pltpu.VMEM((4, 2, 8, 128), F32), pltpu.VMEM((7, 8, 128), F32),
            pltpu.SemaphoreType.DMA((6,)), pltpu.SemaphoreType.DMA((6,)),
        ]
        params.update(collective_id=2, has_side_effects=True)
    else:
        more = [(heads, BF16)]
    return pl.pallas_call(
        functools.partial(attn_back_kernel, ring, n),
        grid=(4 + n,),
        out_shape=[jax.ShapeDtypeStruct(shape, kind) for shape, kind in shapes + more],
        in_specs=in_specs,
        out_specs=out_specs + [full_spec(shape) for shape, _ in more],
        scratch_shapes=scratch,
        compiler_params=pltpu.CompilerParams(**params),
        name="attn_back",
    )(qt, k, v, e, ot, mixed_grad, tokens, memory, keep, dkept, dh, n1, attn, vec, *extra)


def hand_out_kernel(
    fqkv_ref, fo_ref, fw1_ref, fw2_ref, fwr_ref, fgate_ref, small_ref, qkv_ref, in_ref, wqkv_ref, gain_ref,
    gqkv_ref, gout_ref, gin_ref, gffn_ref, gwqkv_ref, gwout_ref, ggate_ref, gb_ref, ggb_ref, ggain_ref,
):
    for pair in range(4):
        for core in range(2):
            rows = slice(core * 16, core * 16 + 16)
            for i in range(3):
                gqkv_ref[i, rows, pair * 128:(pair + 1) * 128] = fqkv_ref[pair, core, i * 16:(i + 1) * 16, :]
    for core in range(2):
        gout_ref[core * 16:core * 16 + 16, :] = fo_ref[core]
    for j in range(4):
        gin_ref[:, j * 512:(j + 1) * 512] = fw1_ref[j]
    gffn_ref[...] = fw2_ref[...]
    gwqkv_ref[...] = fwr_ref[0:3]
    gwout_ref[...] = fwr_ref[3]
    ggate_ref[...] = fgate_ref[...]
    gb_ref[...] = small_ref[0:1, :]
    rows = ggb_ref.shape[1]
    place = lax.rem(lax.axis_index("dp"), 4)
    narrow = jnp.zeros((1, rows), F32)
    for i in range(4):
        narrow = narrow + small_ref[1:2, i * rows:(i + 1) * rows] * (place == i).astype(F32)
    ggb_ref[...] = narrow
    sums = [
        jnp.sum(jnp.sum(qkv_ref[...].astype(F32) * gqkv_ref[...], axis=0), axis=-1, keepdims=True),
        jnp.sum(in_ref[...].astype(F32) * gin_ref[...], axis=-1, keepdims=True),
        jnp.sum(jnp.sum(wqkv_ref[...].astype(F32) * gwqkv_ref[...], axis=0), axis=-1, keepdims=True),
    ]
    for i in range(3):
        across = jnp.broadcast_to(sums[i], (rows, 128)).T[0:1, :]
        ggain_ref[i:i + 1, :] = across / gain_ref[i:i + 1, :].astype(F32)


def call_hand_out(*args):
    rows, d = args[2].shape[1:]
    vmem = pl.BlockSpec(memory_space=pltpu.VMEM)
    shapes = [
        (3, rows, d), (rows, d), (rows, 4 * d), (4, rows, d), (3, rows, d), (rows, d), (4, rows // 2, d), (1, 128), (1, rows),
        (3, rows),
    ]
    return pl.pallas_call(
        hand_out_kernel,
        out_shape=[jax.ShapeDtypeStruct(shape, F32) for shape in shapes],
        in_specs=[vmem] * 11,
        out_specs=[vmem] * 10,
        name="hand_out",
    )(*args)


def plain_weights(attn_qkv, attn_out, ffn_in, ffn_out, writer_qkv, writer_out, gate_weight, ffn_bias, gate_bias, gains):
    rows, d = attn_out.shape
    packed = jnp.concatenate(
        [
            attn_qkv, attn_out[None], ffn_in.reshape(rows, 4, d).transpose(1, 0, 2), ffn_out.reshape(4, rows, d),
            writer_qkv, writer_out[None], gate_weight.reshape(2, rows, d),
        ],
        0,
    )
    packed = lax.all_gather(packed, "dp", axis=0)
    n = packed.shape[0]

    def by_rows(first, last):
        return packed[:, first:last].transpose(1, 0, 2, 3).reshape(last - first, n * rows, d)

    small = jnp.concatenate([ffn_bias.reshape(4, rows), gate_bias[None], gains], 0).astype(F32)
    small = lax.all_gather(small, "dp", axis=0)
    b1 = small[:, 0:4].reshape(4, 1, d)
    vec = small.transpose(1, 0, 2).reshape(8, d)
    vec = jnp.concatenate([vec[4:8], jnp.zeros((4, d), F32)], 0)
    w2 = packed[:, 8:12].reshape(4, d, d)
    return by_rows(0, 4), by_rows(4, 8), w2, by_rows(12, 16), packed[:, 16:18].reshape(2, d, d), vec, b1


def plain_grads(rows, attn_qkv, ffn_in, writer_qkv, gains, gattn, gw1, gw2, gwr, ggate, gb, ggb):
    d = gattn.shape[-1]
    n = d // rows

    def by_rows(grad):
        return grad.reshape(-1, n, rows, d).transpose(1, 0, 2, 3)

    packed = jnp.concatenate(
        [by_rows(gattn), by_rows(gw1), gw2.reshape(n, 4, rows, d), by_rows(gwr), ggate.reshape(n, 2, rows, d)], 1
    )
    owned = lax.psum_scatter(packed.astype(F32), "dp", scatter_dimension=0, tiled=False)
    owned = lax.psum(owned.astype(BF16), "outer").astype(F32)
    small = jnp.concatenate([gb.reshape(n, 4 * rows), ggb.reshape(n, rows)], 1)
    small = lax.psum(lax.psum_scatter(small, "dp", scatter_dimension=0, tiled=False), "outer")
    gin = owned[4:8].transpose(1, 0, 2).reshape(rows, 4 * d)
    ggains = jnp.stack(
        [
            jnp.sum(attn_qkv.astype(F32) * owned[0:3], (0, 2)), jnp.sum(ffn_in.astype(F32) * gin, 1),
            jnp.sum(writer_qkv.astype(F32) * owned[12:15], (0, 2)),
        ]
    )
    return (
        owned[0:3], owned[3], gin, owned[8:12].reshape(4 * rows, d), owned[12:15], owned[15], owned[16:18].reshape(2 * rows, d),
        small[0:4 * rows], small[4 * rows:], ggains / gains.astype(F32),
    )


def body(
    tokens, memory, doc_ids, resets, out_grad, memory_grad,
    attn_qkv, attn_out, ffn_in, ffn_bias, ffn_out, writer_qkv, writer_out, gate_weight, gate_bias, gains,
):
    micro, segs, seg, d = tokens.shape
    slots = memory.shape[2]
    rows = attn_out.shape[0]
    n = micro * segs
    ring = lax.axis_size("dp") == 16 and lax.axis_size("outer") == 2 and rows == 32
    tokens, out_grad = tokens.reshape(n, seg, d), out_grad.reshape(n, seg, d)
    memory, memory_grad = memory.reshape(n, slots, d), memory_grad.reshape(n, slots, d)
    docs = doc_ids.reshape(n, 1, seg)
    keep = jnp.broadcast_to((1 - resets).astype(F32).reshape(n, 1, 1), (n, 1, 128))
    if ring:
        weights = (
            attn_qkv, attn_out, ffn_in, ffn_out.reshape(4, rows, d), writer_qkv, writer_out,
            gate_weight.reshape(4, rows // 2, d), ffn_bias.reshape(1, 4 * rows), gate_bias.reshape(1, rows), gains,
        )
    else:
        attn, w1, w2, wr, gate, vec, b1 = plain_weights(
            attn_qkv, attn_out, ffn_in, ffn_out, writer_qkv, writer_out, gate_weight, ffn_bias, gate_bias, gains
        )
        units = (4, 4, 2, 2, 32, d)
        weights = (attn.reshape(units), w1.reshape(units), w2.reshape(4, 2, 2, 4, 32, d), vec, b1)
    n1, qt, k, v, e, linv, ot, h1, out, res, act, slope, vec, *whole = call_forward(ring, tokens, memory, docs, keep, weights)
    if ring:
        attn, w1, w2, wr = (array.reshape(4, d, d) for array in whole[:4])
        gate = whole[4].reshape(2, d, d)
    new_memory, dkept, ggb, gb, gw1, gw2, gwo, dh, mixed_grad, gwr, ggate = call_ffn_back(
        ring, res, memory, memory_grad, docs, keep, wr, gate, vec, out_grad, h1, act, slope, ot, linv, w1, w2, attn
    )
    extra = ()
    if ring:
        extra = (ggb, gb, gw1.reshape(4, 4, 2, 2, 32, d), gw2.reshape(4, 2, 2, 4, 32, d), gwo.reshape(4, 2, 2, 2, 16, d))
    grad_tokens, grad_memory, *rest = call_attn_back(
        ring, dh, tokens, memory, keep, n1, qt, k, v, e, ot, mixed_grad, dkept, attn, vec, extra
    )
    if ring:
        grads = call_hand_out(*rest[:4], gwr, ggate, rest[4], attn_qkv, ffn_in, writer_qkv, gains)
    else:
        (heads,) = rest
        gattn = heads.reshape(4, 2, 16, 3, 16, 128).transpose(3, 2, 1, 4, 0, 5).reshape(3, d, d)
        gattn = jnp.concatenate([gattn, gwo[None]], 0)
        grads = plain_grads(rows, attn_qkv, ffn_in, writer_qkv, gains, gattn, gw1, gw2, gwr, ggate, gb, ggb)
    gqkv, gout, gin, gffn, gwqkv, gwout, ggw, gb, ggb, ggains = grads
    return (
        out.reshape(micro, segs, seg, d), new_memory.reshape(micro, segs, slots, d),
        grad_tokens.reshape(micro, segs, seg, d), grad_memory.reshape(micro, segs, slots, d),
        gqkv, gout, gin, gb.reshape(4 * rows), gffn.reshape(4 * rows, d), gwqkv, gwout, ggw.reshape(2 * rows, d),
        ggb.reshape(rows), ggains,
    )


def solution(mesh):
    split = ("dp", "outer")
    whole = P(None, split, None, None)
    weights = (
        P(None, "dp", None), P("dp", None), P("dp", None), P("dp"), P("dp", None), P(None, "dp", None),
        P("dp", None), P("dp", None), P("dp"), P(None, "dp"),
    )
    return jax.shard_map(
        body,
        mesh=mesh,
        in_specs=(whole, whole, P(None, split, None), P(None, split), whole, whole) + weights,
        out_specs=(whole, whole, whole, whole) + weights,
        check_vma=False,
    )
```
